256 devices in a mesh: tower: 2 (over x_lo), blk: 128 (over y, x_hi, z, core).
Axes of the slice: x: 4 (x_hi: 2, x_lo: 2; x = x_hi * 2 + x_lo), y: 4, z: 8, core: 2. Of those that a mesh axis runs over, the one named last changes fastest.
Arguments:
- embeddings: bfloat16 [2, 16384, 896], P('tower', 'blk'), may hold values from -0.25 to 0.25
- pair: int32 [16384], P('blk'), may hold values from 0 to 16383, as said below
- logit_scale: float32 [], replicated, may hold values from 16 to 32
Outputs:
- emb_grad: bfloat16 [2, 16384, 896], P('tower', 'blk')
- loss: float32 [2], P('tower')
- scale_grad: float32 [2], P('tower')
The draws below stay inside these ranges and needn't reach their ends.
Inputs may be any that keep to these rules, and one draw needn't show every extreme that they name: pair is a permutation: every text index appears once.
All inputs are finite; a program needn't handle non-finite values.
Results may differ from the reference program's by a relative error of at most 0.0054.
Values may be sent and summed in bfloat16 or wider, within the bound.
A program may use at most 128 MiB of HBM per device.

```python
import math
import jax
import jax.numpy as jnp
from jax import lax

D = 896
TOK_DEV = 128
TOKENS = 16384


def shared_pair(key):
    return jax.random.permutation(jax.random.fold_in(key, 11), TOKENS).astype(jnp.int32)


def draw_pair(key, part):
    return shared_pair(key)


def draw_embeddings(key, part):
    matching = shared_pair(key)
    key = jax.random.fold_in(key, 5)
    key_image, key_noise, key_copy, key_flag, key_source = jax.random.split(key, 5)
    position = jnp.arange(TOKENS, dtype=jnp.float32) / (TOKENS - 1)
    image = jax.random.normal(key_image, (TOKENS, D), jnp.float32)
    noise = jax.random.normal(key_noise, (TOKENS, D), jnp.float32)
    copy_noise = jax.random.normal(key_copy, (TOKENS, D), jnp.float32)
    strength = 0.8 * position
    inverse = jnp.zeros((TOKENS,), jnp.int32).at[matching].set(jnp.arange(TOKENS, dtype=jnp.int32))
    shared = strength[inverse]
    base_text = shared[:, None] * image[inverse] + jnp.sqrt(1.0 - shared * shared)[:, None] * noise
    flags = jax.random.randint(key_flag, (TOKENS,), 0, 20) == 0
    source_image = jax.random.randint(key_source, (TOKENS,), TOKENS - TOKENS // 4, TOKENS)
    source_text = matching[source_image]
    similar = 0.97 * base_text[source_text] + 0.2431 * copy_noise
    text = jnp.where(flags[:, None], similar, base_text)
    both = jnp.stack([image, text]) * 0.03125
    return jnp.clip(both, -0.25, 0.25).astype(jnp.bfloat16)


def setup_inputs(seed: int = 0) -> dict:
    streams_of = jax.random.split(jax.random.key(seed), 4)
    embeddings = draw_embeddings(jax.random.fold_in(streams_of[3], 71), 0)
    pair = draw_pair(jax.random.fold_in(streams_of[3], 71), 0)
    logit_scale = jnp.clip(jnp.exp(jax.random.uniform(streams_of[2], (), jnp.float32, math.log(16.0), math.log(32.0))), 16.0, 32.0)
    return {"embeddings": embeddings, "pair": pair, "logit_scale": logit_scale}


eps = 1e-06

def normalize(embedded):
    widened = embedded.astype(jnp.float32)
    lengths = jnp.sqrt(lax.optimization_barrier(jnp.sum(widened * widened, axis=1)) + eps)
    return (widened / lengths[:, None], lengths)

def first_pass(own_unit, other_unit, targets, scale_value):
    block_rows = TOK_DEV * 8
    block_total = TOKENS // block_rows
    column_ids = jnp.arange(TOKENS, dtype=jnp.int32)

    def per_block(inputs_pair):
        unit_rows, row_targets = inputs_pair
        scores = scale_value * jnp.dot(unit_rows, other_unit.T, preferred_element_type=jnp.float32)
        exponent = jnp.exp(scores - scale_value)
        positive = column_ids[None, :] == row_targets[:, None]
        return (lax.optimization_barrier(jnp.sum(exponent, axis=1)), lax.optimization_barrier(jnp.sum(exponent * scores, axis=1)), lax.optimization_barrier(jnp.sum(jnp.where(positive, scores, 0.0), axis=1)))
    denom, expected, matched = lax.map(per_block, (own_unit.reshape(block_total, block_rows, -1), targets.reshape(block_total, block_rows)))
    return (denom.reshape(-1), expected.reshape(-1), matched.reshape(-1))

def second_pass(own_unit, other_unit, targets, scale_value, own_denom, other_denom):
    block_rows = TOK_DEV * 8
    block_total = TOKENS // block_rows
    column_ids = jnp.arange(TOKENS, dtype=jnp.int32)

    def per_block(inputs_pair):
        unit_rows, row_targets, row_denom = inputs_pair
        scores = scale_value * jnp.dot(unit_rows, other_unit.T, preferred_element_type=jnp.float32)
        exponent = jnp.exp(scores - scale_value)
        positive = column_ids[None, :] == row_targets[:, None]
        weights = 0.5 * (exponent / row_denom[:, None] + exponent / other_denom[None, :]) - jnp.where(positive, 1.0, 0.0)
        return jnp.dot(weights.astype(jnp.bfloat16), other_unit, preferred_element_type=jnp.float32)
    grads = lax.map(per_block, (own_unit.reshape(block_total, block_rows, -1), targets.reshape(block_total, block_rows), own_denom.reshape(block_total, block_rows)))
    return grads.reshape(TOKENS, -1) * scale_value

def backward_norm(grads, unit32, lengths):
    inner = lax.optimization_barrier(jnp.sum(unit32 * grads, axis=1))
    return (grads - unit32 * inner[:, None]) / lengths[:, None]

def reference(embeddings, pair, logit_scale):
    scale_value = logit_scale.astype(jnp.float32)
    image32, image_len = normalize(embeddings[0])
    text32, text_len = normalize(embeddings[1])
    image_unit = image32.astype(jnp.bfloat16)
    text_unit = text32.astype(jnp.bfloat16)
    indices = jnp.arange(TOKENS, dtype=jnp.int32)
    inverse = jnp.zeros((TOKENS,), jnp.int32).at[pair].set(indices)
    z_image, e_image, p_image = first_pass(image_unit, text_unit, pair, scale_value)
    z_text, e_text, p_text = first_pass(text_unit, image_unit, inverse, scale_value)
    loss = jnp.stack([jnp.sum(scale_value + jnp.log(z_image) - p_image), jnp.sum(scale_value + jnp.log(z_text) - p_text)]) / (2 * TOKENS)
    scale_grad = jnp.stack([jnp.sum(e_image / z_image - p_image), jnp.sum(e_text / z_text - p_text)]) / scale_value / (2 * TOKENS)
    grad_image = second_pass(image_unit, text_unit, pair, scale_value, z_image, z_text)
    grad_text = second_pass(text_unit, image_unit, inverse, scale_value, z_text, z_image)
    emb_grad = jnp.stack([backward_norm(grad_image, image32, image_len), backward_norm(grad_text, text32, text_len)]).astype(jnp.bfloat16)
    return (emb_grad, loss, scale_grad)
```

```python
import jax
import jax.numpy as jnp
from jax import lax
from jax.experimental import pallas as pl
from jax.experimental.pallas import tpu as pltpu
from jax.sharding import PartitionSpec as P

eps = 1e-06
TOK = 128
D = 896
TOKENS = 16384
NY, NXH, NZ, NC = 4, 2, 8, 2
f32 = jnp.float32
bf16 = jnp.bfloat16
MESH = pl.DeviceIdType.MESH


def device(t, y, xh, z, c):
    return (t, ((y * NXH + xh) * NZ + z) * NC + c)


def kernel(
    scale_ref, emb_ref, pair_ref,
    out_ref, loss_ref, sgrad_ref,
    own, images, texts, texts_t, pairs, exps, weights,
    text_part, text_send, text_recv, image_part, image_send, image_sib, image_recv,
    stat_send, z_img_all, z_txt_all, e_img, scal_send, scal_z, scal_p, fin_send, fin_recv,
    s_txt, r_txt, s_img, r_img, s_sib, r_sib, s_pair, r_pair, s_x, r_x,
    s_zi, r_zi, s_zt, r_zt, s_sz, r_sz, s_sp, r_sp,
    s_rt, r_rt, s_ri, r_ri, s_rs, r_rs, s_fin, r_fin,
):
    t = lax.axis_index("tower")
    b = lax.axis_index("blk")
    c = b % 2
    z = (b // 2) % 8
    xh = (b // 16) % 2
    y = b // 32
    is_text = t == 1
    is_root = c == t
    line_rank = z * 2 + c
    plane_rank = (t * 4 + y) * 2 + xh
    text_index = y * 2 + xh
    scale = scale_ref[0]

    line_peers = [
        device(t, y, xh, (z + dz) % 8, (c + dc) % 2)
        for dz in (4, 3, 5, 2, 6, 1, 7, 0) for dc in (0, 1) if dz or dc
    ]
    plane_peers = [
        device((t + dt) % 2, (y + dy) % 4, (xh + dx) % 2, z, c)
        for dy in (2, 1, 3, 0) for dx in (1, 0) for dt in (0, 1) if dy or dx or dt
    ]
    sibling = device(t, y, xh, z, 1 - c)
    ring_peers = [device(t, y, xh, (z + dz) % 8, c) for dz in (4, 3, 5, 2, 6, 1, 7)]

    def send(src, dst, ssem, rsem, target):
        pltpu.make_async_remote_copy(
            src_ref=src, dst_ref=dst, send_sem=ssem, recv_sem=rsem,
            device_id=target, device_id_type=MESH,
        ).start()

    def landed(dst, rsem):
        pltpu.make_async_copy(dst, dst, rsem).wait()

    barrier = pltpu.get_barrier_semaphore()
    for peer in line_peers + plane_peers:
        pl.semaphore_signal(barrier, inc=1, device_id=peer, device_id_type=MESH)

    wide = emb_ref[0].astype(f32)
    lengths = jnp.sqrt(jnp.sum(wide * wide, axis=1, keepdims=True) + eps)
    unit = (wide / lengths).astype(bf16)
    own[...] = unit

    @pl.when(is_text)
    def _():
        texts[text_index] = unit

    @pl.when(jnp.logical_and(t == 0, c == 0))
    def _():
        images[z] = unit

    @pl.when(is_root)
    def _():
        pairs[z] = pair_ref[...]

    pl.semaphore_wait(barrier, 30)

    @pl.when(jnp.logical_and(t == 0, c == 1))
    def _():
        send(own, images.at[z], s_x.at[0], r_x.at[0], device(1, y, xh, z, c))

    @pl.when(is_root)
    def _():
        for k, peer in enumerate(line_peers):
            send(pair_ref, pairs.at[z], s_pair.at[k], r_pair.at[z], peer)

    @pl.when(is_text)
    def _():
        for k, peer in enumerate(plane_peers):
            send(own, texts.at[text_index], s_txt.at[k], r_txt.at[text_index], peer)

    @pl.when(jnp.logical_and(t == 1, c == 1))
    def _():
        landed(images.at[z], r_x.at[0])

    @pl.when(is_root)
    def _():
        for k, peer in enumerate(ring_peers):
            send(images.at[z], images.at[z], s_img.at[k], r_img.at[z], peer)
        send(images.at[z], images.at[z], s_sib.at[0], r_sib.at[z], sibling)
        for k, dz in enumerate((1, 7, 2, 6, 3, 5, 4)):
            other = (z + dz) % 8
            landed(images.at[other], r_img.at[other])
            send(images.at[other], images.at[other], s_sib.at[1 + k], r_sib.at[other], sibling)
            landed(pairs.at[other], r_pair.at[other])

    @pl.when(jnp.logical_not(is_root))
    def _():
        for dz in (0, 1, 7, 2, 6, 3, 5, 4):
            other = (z + dz) % 8
            landed(images.at[other], r_sib.at[other])
            landed(pairs.at[other], r_pair.at[other])

    def text_landed(dy, dx):
        other = ((y + dy) % 4) * 2 + (xh + dx) % 2
        landed(texts.at[other], r_txt.at[other])

    for dy in range(4):
        for dx in range(2):
            if dy == 0 and dx == 0:
                @pl.when(jnp.logical_not(is_text))
                def _():
                    text_landed(0, 0)
            else:
                text_landed(dy, dx)

    pair_row = jnp.concatenate([pairs[k][0:1] for k in range(8)], axis=1)
    sub_ids = lax.broadcasted_iota(jnp.int32, (TOK, 1), 0)

    def first_id(block):
        return ((block * 8 + z) * 2 + c) * TOK

    all_images = images[...].reshape(8 * TOK, D)

    def stats(block, carry):
        zi, ei, pi = carry
        rows = texts[block]
        dots = lax.dot_general(rows, all_images, (((1,), (1,)), ((), ())), preferred_element_type=f32)
        scores = scale * dots
        ex = jnp.exp(scores - scale)
        exps[block] = ex
        es = ex * scores
        match = pair_row == first_id(block) + sub_ids
        zi = zi + jnp.sum(ex, axis=0, keepdims=True)
        ei = ei + jnp.sum(es, axis=0, keepdims=True)
        pi = pi + jnp.sum(jnp.where(match, scores, 0.0), axis=0, keepdims=True)
        zr = ex[:, 0:TOK]
        er = es[:, 0:TOK]
        for k in range(1, 8):
            zr = zr + ex[:, k * TOK:(k + 1) * TOK]
            er = er + es[:, k * TOK:(k + 1) * TOK]
        stat_send[1, pl.ds(block, 1), :] = jnp.sum(zr.T, axis=0, keepdims=True)
        e_img[1, pl.ds(block, 1), :] = jnp.sum(er.T, axis=0, keepdims=True)
        texts_t[block] = rows.astype(f32).T.astype(bf16)
        return zi, ei, pi

    zero = jnp.zeros((1, 8 * TOK), f32)
    zi, ei, pi = lax.fori_loop(0, 8, stats, (zero, zero, zero))
    for k in range(8):
        stat_send[0, k:k + 1, :] = zi[:, k * TOK:(k + 1) * TOK]
        e_img[0, k:k + 1, :] = ei[:, k * TOK:(k + 1) * TOK]

    for k, peer in enumerate(line_peers):
        send(stat_send.at[0], z_img_all.at[line_rank], s_zi.at[k], r_zi.at[line_rank], peer)
    for k, peer in enumerate(plane_peers):
        send(stat_send.at[1], z_txt_all.at[plane_rank], s_zt.at[k], r_zt.at[plane_rank], peer)
    z_img_all[line_rank] = stat_send[0]
    z_txt_all[plane_rank] = stat_send[1]

    def line_others():
        return [((z + dz) % 8) * 2 + (c + dc) % 2 for dz in range(8) for dc in range(2) if dz or dc]

    def plane_others():
        return [
            (((t + dt) % 2) * 4 + (y + dy) % 4) * 2 + (xh + dx) % 2
            for dy in range(4) for dx in range(2) for dt in range(2) if dy or dx or dt
        ]

    for other in line_others():
        landed(z_img_all.at[other], r_zi.at[other])
    for other in plane_others():
        landed(z_txt_all.at[other], r_zt.at[other])
    z_img = jnp.sum(z_img_all[...], axis=0)
    z_txt = jnp.sum(z_txt_all[...], axis=0)

    half_img = 0.5 / z_img
    half_txt = 0.5 / z_txt
    stat_send[2] = half_txt
    img_row = jnp.concatenate([half_img[k:k + 1] for k in range(8)], axis=1)

    def weigh(block, _):
        column = jnp.broadcast_to(stat_send[2, pl.ds(block, 1), :], (TOK, TOK)).T
        ids = first_id(block) + sub_ids
        for k in range(8):
            lanes = slice(k * TOK, (k + 1) * TOK)
            match = pair_row[:, lanes] == ids
            value = exps[block, :, lanes] * (img_row[:, lanes] + column)
            weights[block, :, lanes] = (value - jnp.where(match, 1.0, 0.0)).astype(bf16)
        return 0

    lax.fori_loop(0, 8, weigh, 0)

    lane = lax.broadcasted_iota(jnp.int32, (8, TOK), 1)

    def total(x):
        return jnp.sum(jnp.sum(x, axis=0, keepdims=True), axis=1, keepdims=True)

    log_img = total(jnp.log(z_img))
    log_txt = total(jnp.log(z_txt))
    t_img = total(e_img[0] / z_img)
    t_txt = total(e_img[1] / z_txt)
    matched = jnp.sum(pi, axis=1, keepdims=True)
    scal_send[0] = jnp.where(
        lane == 0, log_txt,
        jnp.where(lane == 1, t_img, jnp.where(lane == 2, t_txt, jnp.where(lane == 3, matched, 0.0))),
    )
    for k, peer in enumerate(line_peers):
        send(scal_send.at[0], scal_z.at[line_rank], s_sz.at[k], r_sz.at[line_rank], peer)
    scal_z[line_rank] = scal_send[0]

    def text_block(step, _):
        block = (text_index + 4 + step) % 8
        part = jnp.dot(weights[block], all_images, preferred_element_type=f32)
        text_part[block] = part
        text_send[block] = part.astype(bf16)

        @pl.when(jnp.logical_or(block != text_index, t == 0))
        def _():
            send(
                text_send.at[block], text_recv.at[plane_rank], s_rt.at[block], r_rt.at[plane_rank],
                device(1, block // 2, block % 2, z, c),
            )
        return 0

    lax.fori_loop(0, 8, text_block, 0)

    def image_pair(p, _):
        acc = jnp.zeros((D, 2 * TOK), f32)
        lanes = pl.ds(pl.multiple_of(p * 2 * TOK, 2 * TOK), 2 * TOK)
        for k in range(8):
            acc = acc + jnp.dot(texts_t[k], weights[k, :, lanes], preferred_element_type=f32)
        for h in range(2):
            image_part[2 * p + h] = acc[:, h * TOK:(h + 1) * TOK]

        @pl.when(jnp.logical_not(is_root))
        def _():
            for h in range(2):
                image_send[2 * p + h] = acc[:, h * TOK:(h + 1) * TOK].astype(bf16)
                send(
                    image_send.at[2 * p + h], image_sib.at[2 * p + h], s_rs.at[2 * p + h], r_rs.at[2 * p + h],
                    sibling,
                )
        return 0

    lax.fori_loop(0, 4, image_pair, 0)

    @pl.when(is_root)
    def _():
        def forward(step, _):
            block = (z + 4 + step) % 8
            landed(image_sib.at[block], r_rs.at[block])
            both = image_part[block] + image_sib[block].astype(f32)
            image_part[block] = both
            image_send[block] = both.astype(bf16)

            @pl.when(block != z)
            def _():
                send(
                    image_send.at[block], image_recv.at[z], s_ri.at[block], r_ri.at[z],
                    device(t, y, xh, block, c),
                )
            return 0
        lax.fori_loop(0, 8, forward, 0)

    for other in line_others():
        landed(scal_z.at[other], r_sz.at[other])
    line_sum = jnp.sum(scal_z[...], axis=0)
    scal_send[1] = jnp.where(lane == 4, log_img, line_sum)
    for k, peer in enumerate(plane_peers):
        send(scal_send.at[1], scal_p.at[plane_rank], s_sp.at[k], r_sp.at[plane_rank], peer)
    scal_p[plane_rank] = scal_send[1]

    def finish(grads):
        unit32 = wide / lengths
        grads = scale * grads
        inner = jnp.sum(unit32 * grads, axis=1, keepdims=True)
        out_ref[0] = ((grads - unit32 * inner) / lengths).astype(bf16)

    @pl.when(is_text)
    def _():
        acc = text_part[text_index]
        for other in plane_others():
            landed(text_recv.at[other], r_rt.at[other])
            acc = acc + text_recv[other].astype(f32)
        finish(acc)

    @pl.when(is_root)
    def _():
        acc = image_part[z]
        for dz in range(1, 8):
            other = (z + dz) % 8
            landed(image_recv.at[other], r_ri.at[other])
            acc = acc + image_recv[other].astype(f32)

        @pl.when(is_text)
        def _():
            fin_send[...] = acc.astype(bf16)
            send(fin_send, fin_recv, s_fin.at[0], r_fin.at[0], device(0, y, xh, z, c))

        @pl.when(jnp.logical_not(is_text))
        def _():
            finish(acc.T)

    @pl.when(jnp.logical_and(t == 0, c == 1))
    def _():
        landed(fin_recv, r_fin.at[0])
        finish(fin_recv[...].astype(f32).T)

    for other in plane_others():
        landed(scal_p.at[other], r_sp.at[other])
    all_sum = jnp.sum(scal_p[...], axis=0)

    def pick(k):
        return jnp.sum(jnp.where(lane[0:1] == k, all_sum[0:1], 0.0))

    log_txt_all = jnp.sum(jnp.where(lane[0:1] == 0, line_sum[0:1], 0.0))
    log_all = jnp.where(is_text, log_txt_all, pick(4))
    t_all = jnp.where(is_text, pick(2), pick(1))
    p_all = pick(3)
    loss_ref[0] = (scale * TOKENS + log_all - p_all) * (1.0 / (2 * TOKENS))
    sgrad_ref[0] = (t_all - p_all) / scale * (1.0 / (2 * TOKENS))

    def left(src, sem):
        pltpu.make_async_copy(src, src, sem).wait()

    for k in range(15):
        left(stat_send.at[0], s_zi.at[k])
        left(stat_send.at[1], s_zt.at[k])
        left(scal_send.at[0], s_sz.at[k])
        left(scal_send.at[1], s_sp.at[k])

    @pl.when(is_text)
    def _():
        for k in range(15):
            left(own, s_txt.at[k])

    @pl.when(jnp.logical_and(t == 0, c == 1))
    def _():
        left(own, s_x.at[0])

    @pl.when(jnp.logical_and(t == 1, c == 1))
    def _():
        left(fin_send, s_fin.at[0])

    @pl.when(is_root)
    def _():
        for k in range(15):
            left(pair_ref, s_pair.at[k])
        for k in range(7):
            left(own, s_img.at[k])
        for k in range(8):
            left(own, s_sib.at[k])
        for dz in range(1, 8):
            block = (z + dz) % 8
            left(image_send.at[block], s_ri.at[block])

    @pl.when(jnp.logical_not(is_root))
    def _():
        for k in range(8):
            left(image_send.at[k], s_rs.at[k])

    for k in range(8):
        @pl.when(jnp.logical_or(k != text_index, t == 0))
        def _():
            left(text_send.at[k], s_rt.at[k])


def body(embeddings, pair, logit_scale):
    vmem = pl.BlockSpec(memory_space=pltpu.VMEM)
    smem = pl.BlockSpec(memory_space=pltpu.SMEM)
    dma = pltpu.SemaphoreType.DMA
    sems = [15, 8, 7, 8, 8, 8, 15, 8, 1, 1, 15, 16, 15, 16, 15, 16, 15, 16, 8, 16, 8, 8, 8, 8, 1, 1]
    emb_grad, loss, scale_grad = pl.pallas_call(
        kernel,
        out_shape=(
            jax.ShapeDtypeStruct((1, TOK, D), bf16),
            jax.ShapeDtypeStruct((1,), f32),
            jax.ShapeDtypeStruct((1,), f32),
        ),
        in_specs=[smem, vmem, vmem],
        out_specs=(vmem, smem, smem),
        scratch_shapes=[
            pltpu.VMEM((TOK, D), bf16),
            pltpu.VMEM((8, TOK, D), bf16),
            pltpu.VMEM((8, TOK, D), bf16),
            pltpu.VMEM((8, D, TOK), bf16),
            pltpu.VMEM((8, 8, TOK), jnp.int32),
            pltpu.VMEM((8, TOK, 8 * TOK), f32),
            pltpu.VMEM((8, TOK, 8 * TOK), bf16),
            pltpu.VMEM((8, TOK, D), f32),
            pltpu.VMEM((8, TOK, D), bf16),
            pltpu.VMEM((16, TOK, D), bf16),
            pltpu.VMEM((8, D, TOK), f32),
            pltpu.VMEM((8, D, TOK), bf16),
            pltpu.VMEM((8, D, TOK), bf16),
            pltpu.VMEM((8, D, TOK), bf16),
            pltpu.VMEM((3, 8, TOK), f32),
            pltpu.VMEM((16, 8, TOK), f32),
            pltpu.VMEM((16, 8, TOK), f32),
            pltpu.VMEM((2, 8, TOK), f32),
            pltpu.VMEM((2, 8, TOK), f32),
            pltpu.VMEM((16, 8, TOK), f32),
            pltpu.VMEM((16, 8, TOK), f32),
            pltpu.VMEM((D, TOK), bf16),
            pltpu.VMEM((D, TOK), bf16),
        ] + [dma((n,)) for n in sems],
        compiler_params=pltpu.CompilerParams(
            collective_id=0, has_side_effects=True, vmem_limit_bytes=56 * 2 ** 20
        ),
        cost_estimate=pl.CostEstimate(flops=6 * 1024 * 1024 * D, bytes_accessed=2 ** 20, transcendentals=2 ** 20),
        name="contrastive",
    )(
        logit_scale.astype(f32).reshape(1),
        embeddings,
        jnp.broadcast_to(pair[None, :], (8, TOK)),
    )
    return emb_grad, loss, scale_grad


def solution(mesh):
    placed = (P("tower", "blk", None), P("blk"), P())
    return jax.shard_map(
        body,
        mesh=mesh,
        in_specs=placed,
        out_specs=(P("tower", "blk", None), P("tower"), P("tower")),
        check_vma=False,
    )
```

```python
import jax
import jax.numpy as jnp
from jax import lax
from jax.experimental import pallas as pl
from jax.experimental.pallas import tpu as pltpu
from jax.sharding import PartitionSpec as P

eps = 1e-06
TOK = 128
D = 896
TOKENS = 16384
NY, NXH, NZ, NC = 4, 2, 8, 2
HALF, QUART = TOK // 2, TOK // 4
WIDE = 8 * TOK
f32 = jnp.float32
bf16 = jnp.bfloat16
MESH = pl.DeviceIdType.MESH
STEPS = 9
SENDS = 256


def device(t, y, xh, z, c):
    return (t, ((y * NXH + xh) * NZ + z) * NC + c)


def kernel(
    scale_ref, emb_ref, pair_ref,
    out_ref, loss_ref, sgrad_ref,
    own, images, texts, texts_t, pairs, exps, weights,
    text_part, text_send, ra_one, ra_two, ra_x, ra_fin, rb_odd, rb_even, rb_one, rb_two,
    image_part, image_send, image_sib, image_right, image_left,
    stat_send, z_img_all, z_txt_all, e_sums, scal_send, scal_z, scal_p, fin_send, fin_recv,
    s_all, r_txt, r_img, r_sib, r_pair, r_x, r_zi, r_zt, r_sz, r_sp,
    r_a1, r_a2, r_ax, r_af, r_bo, r_be, r_b1, r_b2, r_is, r_ir, r_il, r_fin,
):
    t = lax.axis_index("tower")
    b = lax.axis_index("blk")
    c = b % 2
    z = (b // 2) % 8
    xh = (b // 16) % 2
    y = b // 32
    odd = t == 1
    even = t == 0
    root = c == t
    line_rank = z * 2 + c
    plane_rank = (t * 4 + y) * 2 + xh
    me = y * 2 + xh
    scale = scale_ref[0]
    y_up, y_dn, y_far = (y + 1) % 4, (y + 3) % 4, (y + 2) % 4
    xo = 1 - xh

    conds = {
        "all": None, "odd": odd, "even": even, "root": root, "leaf": jnp.logical_not(root),
        "giver": jnp.logical_and(t == 0, c == 1), "taker": jnp.logical_and(t == 1, c == 1),
        "first": jnp.logical_and(t == 0, c == 0),
    }
    pending = {name: [] for name in conds}
    count = [0]

    def when(name):
        if name == "all":
            return lambda fn: fn()
        return pl.when(conds[name])

    def send(name, src, dst, rsem, target):
        slot = count[0]
        count[0] += 1
        ssem = s_all.at[slot]
        pltpu.make_async_remote_copy(
            src_ref=src, dst_ref=dst, send_sem=ssem, recv_sem=rsem,
            device_id=target, device_id_type=MESH,
        ).start()
        pending[name].append((slot, src.shape))

    def landed(dst, rsem):
        pltpu.make_async_copy(dst, dst, rsem).wait()

    up = device(t, y_up, xh, z, c)
    dn = device(t, y_dn, xh, z, c)
    zp = device(t, y, xh, (z + 1) % 8, c)
    zm = device(t, y, xh, (z + 7) % 8, c)
    sibling = device(t, y, xh, z, 1 - c)
    across = [device(1 - t, y, 0, z, c), device(1 - t, y, 1, z, c)]
    line_peers = [
        device(t, y, xh, (z + dz) % 8, (c + dc) % 2)
        for dz in (4, 3, 5, 2, 6, 1, 7, 0) for dc in (0, 1) if dz or dc
    ]
    plane_peers = [
        device((t + dt) % 2, (y + dy) % 4, (xh + dx) % 2, z, c)
        for dy in (2, 1, 3, 0) for dx in (1, 0) for dt in (0, 1) if dy or dx or dt
    ]
    line_others = [((z + dz) % 8) * 2 + (c + dc) % 2 for dz in range(8) for dc in range(2) if dz or dc]
    plane_others = [
        (((t + dt) % 2) * 4 + (y + dy) % 4) * 2 + (xh + dx) % 2
        for dy in range(4) for dx in range(2) for dt in range(2) if dy or dx or dt
    ]

    barrier = pltpu.get_barrier_semaphore()
    for peer in line_peers + plane_peers:
        pl.semaphore_signal(barrier, inc=1, device_id=peer, device_id_type=MESH)

    wide = emb_ref[0].astype(f32)
    lengths = jnp.sqrt(jnp.sum(wide * wide, axis=1, keepdims=True) + eps)
    unit = (wide / lengths).astype(bf16)

    @when("odd")
    def _():
        texts[me] = unit

    @when("giver")
    def _():
        own[...] = unit

    @when("first")
    def _():
        images[z] = unit

    @when("root")
    def _():
        pairs[z] = pair_ref[...]

    pl.semaphore_wait(barrier, 30)

    def rows(index, quarter, quarters):
        return texts.at[index, pl.ds(quarter * QUART, quarters * QUART)]

    def tsend(name, index, quarter, quarters, target):
        send(name, rows(index, quarter, quarters), rows(index, quarter, quarters), r_txt.at[index, quarter], target)

    def twait(index, quarter, quarters):
        landed(rows(index, quarter, quarters), r_txt.at[index, quarter])

    def ihalf(slot, h):
        return images.at[slot, pl.ds(h * HALF, HALF)]

    def isend(slot, h, target):
        send("root", ihalf(slot, h), ihalf(slot, h), r_img.at[slot, h], target)

    def iwait(slot, h):
        landed(ihalf(slot, h), r_img.at[slot, h])

    def to_sibling(slot):
        send("root", images.at[slot], images.at[slot], r_sib.at[slot], sibling)

    def image_hop(k):
        @when("root")
        def _():
            left, right = (z + 8 - k) % 8, (z + k) % 8
            for h in ((0, 1)):
                iwait(left, h)
                if k < 3 or h == 0:
                    isend(left, h, zp)
                iwait(right, h)
                if k < 3 or h == 1:
                    isend(right, h, zm)
            to_sibling(left)
            to_sibling(right)

    if STEPS > 1:
        @when("giver")
        def _():
            for h in range(2):
                part = own.at[pl.ds(h * HALF, HALF)]
                send("giver", part, ihalf(z, h), r_x.at[h], device(1, y, xh, z, c))

        @when("odd")
        def _():
            for e in range(2):
                tsend("odd", me, 0, 2, across[e])
            for peer in (up, dn):
                tsend("odd", me, 2, 2, peer)
            for e in range(2):
                tsend("odd", me, 2, 2, across[e])
            for peer in (up, dn):
                tsend("odd", me, 0, 2, peer)

        @when("root")
        def _():
            for h in range(2):
                @when("odd")
                def _():
                    landed(ihalf(z, h), r_x.at[h])
                isend(z, h, zp)
                isend(z, h, zm)
            to_sibling(z)
            for peer in line_peers:
                send("root", pair_ref, pairs.at[z], r_pair.at[z], peer)

        image_hop(1)

        @when("even")
        def _():
            for q in range(2):
                index = y * 2 + q
                twait(index, 0, 2)
                tsend("even", index, 0, 2, up)
                tsend("even", index, 0, 2, dn)
                tsend("even", index, xh, 1, across[1 - q])
            for q in range(2):
                index = y * 2 + q
                twait(index, 2, 2)
                tsend("even", index, 2 + xh, 1, across[1 - q])

        @when("odd")
        def _():
            index = y_dn * 2 + xh
            twait(index, 2, 2)
            tsend("odd", index, 2, 1, up)
            for e in range(2):
                tsend("odd", index, 2, 2, across[e])
            index = y_up * 2 + xh
            twait(index, 2, 2)
            tsend("odd", index, 3, 1, dn)
            for e in range(2):
                tsend("odd", index, 2, 2, across[e])

        image_hop(2)

        @when("odd")
        def _():
            for k in range(2):
                index = y * 2 + xo
                twait(index, k, 1)
                tsend("odd", index, k, 1, up)
                tsend("odd", index, k, 1, dn)
            for k in range(2):
                index = y_far * 2 + xh
                twait(index, 2 + k, 1)
                for e in range(2):
                    tsend("odd", index, 2 + k, 1, across[e])

        @when("even")
        def _():
            for ya in (y_dn, y_up):
                for q in range(2):
                    index = ya * 2 + q
                    twait(index, 2, 2)
                    tsend("even", index, 2 + xh, 1, across[1 - q])
            for q in range(2):
                index = y_dn * 2 + q
                twait(index, 0, 2)
                tsend("even", index, 0, 1, up)
                index = y_up * 2 + q
                twait(index, 0, 2)
                tsend("even", index, 1, 1, dn)

        image_hop(3)

        @when("odd")
        def _():
            index = y_dn * 2 + xh
            twait(index, 0, 2)
            tsend("odd", index, 0, 1, up)
            index = y_up * 2 + xh
            twait(index, 0, 2)
            tsend("odd", index, 1, 1, dn)
            index = y_dn * 2 + xo
            twait(index, 0, 1)
            tsend("odd", index, 0, 1, up)
            twait(index, 1, 1)
            index = y_up * 2 + xo
            twait(index, 1, 1)
            tsend("odd", index, 1, 1, dn)
            twait(index, 0, 1)
            for k in range(2):
                for q in range(2):
                    twait(y_far * 2 + q, k, 1)
            for ya in (y, y_dn, y_up, y_far):
                for k in range(2):
                    twait(ya * 2 + xo, 2 + k, 1)

        @when("even")
        def _():
            for q in range(2):
                index = y_far * 2 + q
                for k in range(2):
                    twait(index, 2 + k, 1)
                tsend("even", index, 2 + xh, 1, across[1 - q])
            for q in range(2):
                for k in range(2):
                    twait(y_far * 2 + q, k, 1)

        @when("root")
        def _():
            far = (z + 4) % 8
            for h in range(2):
                iwait(far, h)
            to_sibling(far)
            for dz in range(1, 8):
                landed(pairs.at[(z + dz) % 8], r_pair.at[(z + dz) % 8])

        @when("leaf")
        def _():
            for slot in range(8):
                landed(images.at[slot], r_sib.at[slot])
                landed(pairs.at[slot], r_pair.at[slot])

    def first_id(index):
        return ((index * 8 + z) * 2 + c) * TOK

    def pair_lanes():
        return jnp.concatenate([pairs[k][0:1] for k in range(8)], axis=1)

    sub_ids = lax.broadcasted_iota(jnp.int32, (TOK, 1), 0)

    def total(x):
        return jnp.sum(jnp.sum(x, axis=0, keepdims=True), axis=1, keepdims=True)

    if STEPS > 2:
        pair_row = pair_lanes()
        all_images = images[...].reshape(WIDE, D)

        def stats(p, carry):
            zi, ei, pi = carry
            two = texts[pl.ds(2 * p, 2)].reshape(2 * TOK, D)
            dots = lax.dot_general(two, all_images, (((1,), (1,)), ((), ())), preferred_element_type=f32)
            scores = scale * dots
            ex = jnp.exp(scores - scale)
            exps[pl.ds(2 * p, 2)] = ex.reshape(2, TOK, WIDE)
            es = ex * scores
            ids = jnp.concatenate([first_id(2 * p) + sub_ids, first_id(2 * p + 1) + sub_ids], axis=0)
            match = pair_row == ids
            zi = zi + jnp.sum(ex, axis=0, keepdims=True)
            ei = ei + jnp.sum(es, axis=0, keepdims=True)
            pi = pi + jnp.sum(jnp.where(match, scores, 0.0), axis=0, keepdims=True)
            zr = ex[:, 0:TOK]
            er = es[:, 0:TOK]
            for k in range(1, 8):
                zr = zr + ex[:, k * TOK:(k + 1) * TOK]
                er = er + es[:, k * TOK:(k + 1) * TOK]
            for h in range(2):
                part = slice(h * TOK, (h + 1) * TOK)
                stat_send[1, pl.ds(2 * p + h, 1), :] = jnp.sum(zr[part].T, axis=0, keepdims=True)
                e_sums[1, pl.ds(2 * p + h, 1), :] = jnp.sum(er[part].T, axis=0, keepdims=True)
            return zi, ei, pi

        zero = jnp.zeros((1, WIDE), f32)
        zi, ei, pi = lax.fori_loop(0, 4, stats, (zero, zero, zero))
        for k in range(8):
            stat_send[0, k:k + 1, :] = zi[:, k * TOK:(k + 1) * TOK]
            e_sums[0, k:k + 1, :] = ei[:, k * TOK:(k + 1) * TOK]

    if STEPS > 3:
        for peer in line_peers:
            send("all", stat_send.at[0], z_img_all.at[line_rank], r_zi.at[line_rank], peer)
        for peer in plane_peers:
            send("all", stat_send.at[1], z_txt_all.at[plane_rank], r_zt.at[plane_rank], peer)
        z_img_all[line_rank] = stat_send[0]
        z_txt_all[plane_rank] = stat_send[1]
        for k in range(8):
            texts_t[:, k * TOK:(k + 1) * TOK] = texts[k].astype(f32).T.astype(bf16)
        for other in line_others:
            landed(z_img_all.at[other], r_zi.at[other])
        for other in plane_others:
            landed(z_txt_all.at[other], r_zt.at[other])
        z_img = jnp.sum(z_img_all[...], axis=0)
        z_txt = jnp.sum(z_txt_all[...], axis=0)

    if STEPS > 4:
        half_img = 0.5 / z_img
        stat_send[2] = 0.5 / z_txt
        img_row = jnp.concatenate([half_img[k:k + 1] for k in range(8)], axis=1)

        def weigh(index, _):
            column = jnp.broadcast_to(stat_send[2, pl.ds(index, 1), :], (TOK, TOK)).T
            ids = first_id(index) + sub_ids
            for k in range(8):
                lanes = slice(k * TOK, (k + 1) * TOK)
                match = pair_row[:, lanes] == ids
                value = exps[index, :, lanes] * (img_row[:, lanes] + column)
                weights[index, :, lanes] = (value - jnp.where(match, 1.0, 0.0)).astype(bf16)
            return 0

        lax.fori_loop(0, 8, weigh, 0)

    def text_block(ya):
        pair_of = pl.ds(2 * ya, 2)
        two = weights[pair_of].reshape(2 * TOK, WIDE)
        part = jnp.dot(two, all_images, preferred_element_type=f32)
        text_part[pair_of] = part.reshape(2, TOK, D)

    def quart(ref, index, k):
        return ref.at[index, pl.ds(k * QUART, QUART)]

    def give_b(slot, ya):
        index = ya * 2 + xo
        text_send[index, HALF:TOK] = text_part[index, HALF:TOK].astype(bf16)
        for k in range(2):
            send("odd", quart(text_send, index, 2 + k), rb_even.at[slot, xh], r_be.at[slot, xh], across[k])

    def pass_b(slot, ya):
        for q in range(2):
            index = ya * 2 + q
            landed(rb_even.at[slot, 1 - q], r_be.at[slot, 1 - q])
            spot = pl.ds((2 + xh) * QUART, QUART)
            text_part[index, spot] = text_part[index, spot] + rb_even[slot, 1 - q].astype(f32)
            text_send[index, HALF:TOK] = text_part[index, HALF:TOK].astype(bf16)
            send("even", text_send.at[index, HALF:TOK], rb_odd.at[slot, xh], r_bo.at[slot, xh], across[q])

    def take_b(slot, ya):
        index = ya * 2 + xh
        for e in range(2):
            landed(rb_odd.at[slot, e], r_bo.at[slot, e])
        text_part[index, HALF:TOK] = (
            text_part[index, HALF:TOK] + rb_odd[slot, 0].astype(f32) + rb_odd[slot, 1].astype(f32)
        )

    def image_block(p):
        lanes = pl.ds(pl.multiple_of(p * 2 * TOK, 2 * TOK), 2 * TOK)
        part = jnp.dot(texts_t[...], weights[:, :, lanes].reshape(WIDE, 2 * TOK), preferred_element_type=f32)
        for h in range(2):
            image_part[2 * p + h] = part[:, h * TOK:(h + 1) * TOK]

        @when("leaf")
        def _():
            for h in range(2):
                image_send[2 * p + h] = part[:, h * TOK:(h + 1) * TOK].astype(bf16)
            both = pl.ds(2 * p, 2)
            send("leaf", image_send.at[both], image_sib.at[both], r_is.at[p], sibling)

    def add_sibling(p):
        both = pl.ds(2 * p, 2)
        landed(image_sib.at[both], r_is.at[p])
        for h in range(2):
            image_part[2 * p + h] = image_part[2 * p + h] + image_sib[2 * p + h].astype(f32)

    def dhalf(h):
        return pl.ds(h * (D // 2), D // 2)

    def ring_send(m, h, right):
        hops = 4 - m
        slot = (z + hops) % 8 if right else (z + 8 - hops) % 8
        into = image_right if right else image_left
        sem = r_ir if right else r_il
        spot = dhalf(h)
        value = image_part[slot, spot]
        if m > 1 or (m == 1 and h == (0 if right else 1)):
            landed(into.at[m - 1, spot], sem.at[m - 1, h])
            value = value + into[m - 1, spot].astype(f32)
        image_send[slot, spot] = value.astype(bf16)
        send("root", image_send.at[slot, spot], into.at[m, spot], sem.at[m, h], zp if right else zm)

    if STEPS > 5:
        text_block(y_far)
        for q in range(2):
            index = y_far * 2 + q
            text_send[index, 0:HALF] = text_part[index, 0:HALF].astype(bf16)
        far_two = pl.ds(2 * y_far, 2)
        send("all", text_send.at[far_two, 0:QUART], ra_one.at[0], r_a1.at[0], up)
        send("all", text_send.at[far_two, QUART:HALF], ra_one.at[1], r_a1.at[1], dn)
        orders = (y_far, y_dn, y_up, y)

        @when("odd")
        def _():
            give_b(0, y_far)

        for slot in (1, 2, 3):
            text_block(orders[slot])

            @when("odd")
            def _():
                give_b(slot, orders[slot])

        lane = lax.broadcasted_iota(jnp.int32, (8, TOK), 1)
        log_img = total(jnp.log(z_img))
        log_txt = total(jnp.log(z_txt))
        t_img = total(e_sums[0] / z_img)
        t_txt = total(e_sums[1] / z_txt)
        matched = jnp.sum(pi, axis=1, keepdims=True)
        scal_send[0] = jnp.where(
            lane == 0, log_txt,
            jnp.where(lane == 1, t_img, jnp.where(lane == 2, t_txt, jnp.where(lane == 3, matched, 0.0))),
        )
        for peer in line_peers:
            send("all", scal_send.at[0], scal_z.at[line_rank], r_sz.at[line_rank], peer)
        scal_z[line_rank] = scal_send[0]

        half_z = z // 2
        p_order = [(half_z + k) % 4 for k in (2, 1, 3, 0)]
        image_block(p_order[0])
        image_block(p_order[1])

        @when("even")
        def _():
            pass_b(0, y_far)

        def hop_a(way, ya, quarter, target):
            landed(ra_one.at[way], r_a1.at[way])
            for q in range(2):
                index = ya * 2 + q
                spot = slice(quarter * QUART, (quarter + 1) * QUART)
                text_part[index, spot] = text_part[index, spot] + ra_one[way, q].astype(f32)
                text_send[index, 0:HALF] = text_part[index, 0:HALF].astype(bf16)
            send("all", text_send.at[pl.ds(2 * ya, 2), 0:HALF], ra_two.at[way], r_a2.at[way], target)

        hop_a(0, y_up, 0, up)
        hop_a(1, y_dn, 1, dn)

        image_block(p_order[2])

        @when("even")
        def _():
            pass_b(1, y_dn)

        image_block(p_order[3])

        @when("root")
        def _():
            for p in p_order:
                add_sibling(p)
            ring_send(0, 0, True)
            ring_send(0, 1, False)
            ring_send(1, 1, True)
            ring_send(1, 0, False)

        @when("even")
        def _():
            pass_b(2, y_up)
            pass_b(3, y)

        @when("root")
        def _():
            ring_send(1, 0, True)
            ring_send(1, 1, False)

        @when("odd")
        def _():
            take_b(0, y_far)
            index = y_far * 2 + xh
            text_send[index, HALF:TOK] = text_part[index, HALF:TOK].astype(bf16)
            send("odd", quart(text_send, index, 2), rb_one.at[0], r_b1.at[0], up)
            send("odd", quart(text_send, index, 3), rb_one.at[1], r_b1.at[1], dn)

        @when("root")
        def _():
            for h in (1, 0):
                ring_send(2, h, True)
                ring_send(2, 1 - h, False)

        for way in range(2):
            landed(ra_two.at[way], r_a2.at[way])
        for q in range(2):
            index = y * 2 + q
            text_part[index, 0:HALF] = (
                text_part[index, 0:HALF] + ra_two[0, q].astype(f32) + ra_two[1, q].astype(f32)
            )

        @when("odd")
        def _():
            index = y * 2 + xo
            text_send[index, 0:HALF] = text_part[index, 0:HALF].astype(bf16)
            for k in range(2):
                send("odd", quart(text_send, index, k), ra_x.at[xh], r_ax.at[xh], across[k])

            take_b(1, y_dn)
            take_b(2, y_up)
            for way, ya, quarter, target in ((0, y_up, 2, up), (1, y_dn, 3, dn)):
                index = ya * 2 + xh
                landed(rb_one.at[way], r_b1.at[way])
                spot = slice(quarter * QUART, (quarter + 1) * QUART)
                text_part[index, spot] = text_part[index, spot] + rb_one[way].astype(f32)
                text_send[index, HALF:TOK] = text_part[index, HALF:TOK].astype(bf16)
                send("odd", text_send.at[index, HALF:TOK], rb_two.at[way], r_b2.at[way], target)

        @when("even")
        def _():
            for q in range(2):
                index = y * 2 + q
                landed(ra_x.at[1 - q], r_ax.at[1 - q])
                spot = pl.ds(xh * QUART, QUART)
                text_part[index, spot] = text_part[index, spot] + ra_x[1 - q].astype(f32)
                text_send[index, 0:HALF] = text_part[index, 0:HALF].astype(bf16)
                send("even", text_send.at[index, 0:HALF], ra_fin.at[xh], r_af.at[xh], across[q])

        @when("root")
        def _():
            for h in (1, 0):
                ring_send(3, h, True)
                ring_send(3, 1 - h, False)

        for other in line_others:
            landed(scal_z.at[other], r_sz.at[other])
        line_sum = jnp.sum(scal_z[...], axis=0)
        scal_send[1] = jnp.where(lane == 4, log_img, line_sum)
        for peer in plane_peers:
            send("all", scal_send.at[1], scal_p.at[plane_rank], r_sp.at[plane_rank], peer)
        scal_p[plane_rank] = scal_send[1]

        def finish(grads):
            unit32 = wide / lengths
            grads = scale * grads
            inner = jnp.sum(unit32 * grads, axis=1, keepdims=True)
            out_ref[0] = ((grads - unit32 * inner) / lengths).astype(bf16)

        @when("root")
        def _():
            for h in range(2):
                landed(image_right.at[3, dhalf(h)], r_ir.at[3, h])
                landed(image_left.at[3, dhalf(h)], r_il.at[3, h])
            acc = image_part[z] + image_right[3].astype(f32) + image_left[3].astype(f32)

            @when("odd")
            def _():
                fin_send[...] = acc.astype(bf16)
                send("taker", fin_send, fin_recv, r_fin.at[0], device(0, y, xh, z, c))

            @when("even")
            def _():
                finish(acc.T)

        @when("odd")
        def _():
            take_b(3, y)
            for way in range(2):
                landed(rb_two.at[way], r_b2.at[way])
            text_part[me, HALF:TOK] = (
                text_part[me, HALF:TOK] + rb_two[0].astype(f32) + rb_two[1].astype(f32)
            )
            for e in range(2):
                landed(ra_fin.at[e], r_af.at[e])
            text_part[me, 0:HALF] = (
                text_part[me, 0:HALF] + ra_fin[0].astype(f32) + ra_fin[1].astype(f32)
            )
            finish(text_part[me])

        @when("giver")
        def _():
            landed(fin_recv, r_fin.at[0])
            finish(fin_recv[...].astype(f32).T)

        for other in plane_others:
            landed(scal_p.at[other], r_sp.at[other])
        all_sum = jnp.sum(scal_p[...], axis=0)

        def pick(x, k):
            return jnp.sum(jnp.where(lane[0:1] == k, x[0:1], 0.0))

        log_all = jnp.where(odd, pick(line_sum, 0), pick(all_sum, 4))
        t_all = jnp.where(odd, pick(all_sum, 2), pick(all_sum, 1))
        p_all = pick(all_sum, 3)
        loss_ref[0] = (scale * TOKENS + log_all - p_all) * (1.0 / (2 * TOKENS))
        sgrad_ref[0] = (t_all - p_all) / scale * (1.0 / (2 * TOKENS))

    sizes = {
        (QUART, D): texts.at[0, 0:QUART], (HALF, D): texts.at[0, 0:HALF], (TOK, D): texts.at[0],
        (2, QUART, D): texts.at[0:2, 0:QUART], (2, HALF, D): texts.at[0:2, 0:HALF],
        (8, TOK): stat_send.at[0], (2, D, TOK): image_send.at[0:2],
        (D // 2, TOK): image_send.at[0, 0:D // 2], (D, TOK): fin_send,
    }
    for name, copies in pending.items():
        if copies:
            @when(name)
            def _():
                for slot, shape in copies:
                    pltpu.make_async_copy(sizes[shape], sizes[shape], s_all.at[slot]).wait()


def body(embeddings, pair, logit_scale):
    vmem = pl.BlockSpec(memory_space=pltpu.VMEM)
    smem = pl.BlockSpec(memory_space=pltpu.SMEM)
    dma = pltpu.SemaphoreType.DMA
    scratch = [
        ((TOK, D), bf16),
        ((8, TOK, D), bf16),
        ((8, TOK, D), bf16),
        ((D, WIDE), bf16),
        ((8, 8, TOK), jnp.int32),
        ((8, TOK, WIDE), f32),
        ((8, TOK, WIDE), bf16),
        ((8, TOK, D), f32),
        ((8, TOK, D), bf16),
        ((2, 2, QUART, D), bf16),
        ((2, 2, HALF, D), bf16),
        ((2, QUART, D), bf16),
        ((2, HALF, D), bf16),
        ((4, 2, HALF, D), bf16),
        ((4, 2, QUART, D), bf16),
        ((2, QUART, D), bf16),
        ((2, HALF, D), bf16),
        ((8, D, TOK), f32),
        ((8, D, TOK), bf16),
        ((8, D, TOK), bf16),
        ((4, D, TOK), bf16),
        ((4, D, TOK), bf16),
        ((3, 8, TOK), f32),
        ((16, 8, TOK), f32),
        ((16, 8, TOK), f32),
        ((2, 8, TOK), f32),
        ((2, 8, TOK), f32),
        ((16, 8, TOK), f32),
        ((16, 8, TOK), f32),
        ((D, TOK), bf16),
        ((D, TOK), bf16),
    ]
    sems = [
        (SENDS,), (8, 4), (8, 2), (8,), (8,), (2,), (16,), (16,), (16,), (16,),
        (2,), (2,), (2,), (2,), (4, 2), (4, 2), (2,), (2,), (4,), (4, 2), (4, 2), (1,),
    ]
    return pl.pallas_call(
        kernel,
        out_shape=(
            jax.ShapeDtypeStruct((1, TOK, D), bf16),
            jax.ShapeDtypeStruct((1,), f32),
            jax.ShapeDtypeStruct((1,), f32),
        ),
        in_specs=[smem, vmem, vmem],
        out_specs=(vmem, smem, smem),
        scratch_shapes=[pltpu.VMEM(shape, dtype) for shape, dtype in scratch] + [dma(shape) for shape in sems],
        compiler_params=pltpu.CompilerParams(
            collective_id=0, has_side_effects=True, vmem_limit_bytes=56 * 2 ** 20
        ),
        cost_estimate=pl.CostEstimate(flops=6 * WIDE * WIDE * D, bytes_accessed=2 ** 20, transcendentals=2 ** 20),
        name="contrastive",
    )(
        logit_scale.astype(f32).reshape(1),
        embeddings,
        jnp.broadcast_to(pair[None, :], (8, TOK)),
    )


def solution(mesh):
    placed = (P("tower", "blk", None), P("blk"), P())
    return jax.shard_map(
        body,
        mesh=mesh,
        in_specs=placed,
        out_specs=(P("tower", "blk", None), P("tower"), P("tower")),
        check_vma=False,
    )
```

```python
import jax
import jax.numpy as jnp
from jax import lax
from jax.experimental import pallas as pl
from jax.experimental.pallas import tpu as pltpu
from jax.sharding import PartitionSpec as P

eps = 1e-06
TOK = 128
D = 896
TOKENS = 16384
NY, NXH, NZ, NC = 4, 2, 8, 2
HALF, QUART = TOK // 2, TOK // 4
WIDE = 8 * TOK
f32 = jnp.float32
bf16 = jnp.bfloat16
MESH = pl.DeviceIdType.MESH
STEPS = 9
SENDS = 320


def device(t, y, xh, z, c):
    return (t, ((y * NXH + xh) * NZ + z) * NC + c)


def kernel(
    scale_ref, emb_hbm, pair_ref,
    out_ref, loss_ref, sgrad_ref,
    emb_ref, own, images, texts, pairs, exps, weights,
    text_part, text_send, ra_one, ra_two, ra_x, ra_fin, rb_odd, rb_even, rb_one, rb_two,
    image_part, image_send, image_sib, image_right, image_left,
    stat_send, z_img_all, z_txt_all, e_sums, scal_send, scal_z, scal_p, fin_send, fin_recv,
    s_in, s_all, r_txt, r_img, r_sib, r_pair, r_x, r_zi, r_zt, r_sz, r_sp,
    r_a1, r_a2, r_ax, r_af, r_bo, r_be, r_b1, r_b2, r_is, r_ir, r_il, r_fin,
):
    t = lax.axis_index("tower")
    b = lax.axis_index("blk")
    c = b % 2
    z = (b // 2) % 8
    xh = (b // 16) % 2
    y = b // 32
    odd = t == 1
    even = t == 0
    line_rank = z * 2 + c
    plane_rank = (t * 4 + y) * 2 + xh
    me = y * 2 + xh
    scale = scale_ref[0]
    y_up, y_dn, y_far = (y + 1) % 4, (y + 3) % 4, (y + 2) % 4
    xo = 1 - xh

    conds = {"all": None, "odd": odd, "even": even}
    pending = {name: [] for name in conds}
    count = [0]

    def when(name):
        if name == "all":
            return lambda fn: fn()
        return pl.when(conds[name])

    def send(name, src, dst, rsem, target):
        slot = count[0]
        count[0] += 1
        pltpu.make_async_remote_copy(
            src_ref=src, dst_ref=dst, send_sem=s_all.at[slot], recv_sem=rsem,
            device_id=target, device_id_type=MESH,
        ).start()
        pending[name].append((slot, src.shape))

    def landed(dst, rsem):
        pltpu.make_async_copy(dst, dst, rsem).wait()

    up = device(t, y_up, xh, z, c)
    dn = device(t, y_dn, xh, z, c)
    zp = device(t, y, xh, (z + 1) % 8, c)
    zm = device(t, y, xh, (z + 7) % 8, c)
    sibling = device(t, y, xh, z, 1 - c)
    across = [device(1 - t, y, 0, z, c), device(1 - t, y, 1, z, c)]
    partner = device(1 - t, y, xh, z, c)
    line_peers = [
        device(t, y, xh, (z + dz) % 8, (c + dc) % 2)
        for dz in (4, 3, 5, 2, 6, 1, 7, 0) for dc in (0, 1) if dz or dc
    ]
    plane_peers = [
        device((t + dt) % 2, (y + dy) % 4, (xh + dx) % 2, z, c)
        for dy in (2, 1, 3, 0) for dx in (1, 0) for dt in (0, 1) if dy or dx or dt
    ]
    line_others = [((z + dz) % 8) * 2 + (c + dc) % 2 for dz in range(8) for dc in range(2) if dz or dc]
    plane_others = [
        (((t + dt) % 2) * 4 + (y + dy) % 4) * 2 + (xh + dx) % 2
        for dy in range(4) for dx in range(2) for dt in range(2) if dy or dx or dt
    ]

    fetch = pltpu.make_async_copy(emb_hbm.at[0], emb_ref, s_in.at[0])
    fetch.start()
    barrier = pltpu.get_barrier_semaphore()
    for peer in (up, dn, zp, zm, sibling, across[0], across[1]):
        pl.semaphore_signal(barrier, inc=1, device_id=peer, device_id_type=MESH)
    fetch.wait()

    def normal(part):
        wide = emb_ref[part].astype(f32)
        lengths = jnp.sqrt(jnp.sum(wide * wide, axis=1, keepdims=True) + eps)
        return wide / lengths, lengths

    lower, upper = slice(0, HALF), slice(HALF, TOK)
    unit_low = normal(lower)[0].astype(bf16)
    unit_high = normal(upper)[0].astype(bf16)

    @when("odd")
    def _():
        texts[me, lower] = unit_low
        texts[me, upper] = unit_high

    @when("even")
    def _():
        images[z, c] = unit_low
        own[...] = unit_high

    pairs[z, c] = jnp.broadcast_to(pair_ref[...], (8, TOK))
    pl.semaphore_wait(barrier, 7)

    def rows(index, quarter, quarters):
        return texts.at[index, pl.ds(quarter * QUART, quarters * QUART)]

    def tsend(name, index, quarter, quarters, target):
        send(name, rows(index, quarter, quarters), rows(index, quarter, quarters), r_txt.at[index, quarter], target)

    def twait(index, quarter, quarters):
        landed(rows(index, quarter, quarters), r_txt.at[index, quarter])

    def piece(slot, h):
        return images.at[slot, c, pl.ds(h * QUART, QUART)]

    def isend(name, slot, h, target):
        send(name, piece(slot, h), piece(slot, h), r_img.at[slot, h], target)

    def iwait(slot, h):
        landed(piece(slot, h), r_img.at[slot, h])

    def to_sibling(name, slot):
        send(name, images.at[slot, c], images.at[slot, c], r_sib.at[slot], sibling)

    def image_hop(name, k, h):
        left, right = (z + 8 - k) % 8, (z + k) % 8
        iwait(left, h)
        if k < 3 or h == 0:
            isend(name, left, h, zp)
        iwait(right, h)
        if k < 3 or h == 1:
            isend(name, right, h, zm)
        if h == 1:
            to_sibling(name, left)
            to_sibling(name, right)

    def image_last(name):
        far = (z + 4) % 8
        for h in range(2):
            iwait(far, h)
        to_sibling(name, far)
        for slot in range(8):
            landed(images.at[slot, 1 - c], r_sib.at[slot])

    if STEPS > 1:
        @when("even")
        def _():
            n = "even"
            for h in range(2):
                isend(n, z, h, zp)
                isend(n, z, h, zm)
                send(n, own.at[pl.ds(h * QUART, QUART)], piece(z, h), r_x.at[h], partner)
            to_sibling(n, z)
            image_hop(n, 1, 0)
            for q in range(2):
                index = y * 2 + q
                twait(index, 0, 2)
                tsend(n, index, xh, 1, across[1 - q])
                tsend(n, index, 0, 2, up)
                tsend(n, index, 0, 2, dn)
            image_hop(n, 1, 1)
            for q in range(2):
                index = y * 2 + q
                twait(index, 2 + xh, 1)
                tsend(n, index, 2 + xh, 1, across[1 - q])
            image_hop(n, 2, 0)
            for q in range(2):
                index = y_dn * 2 + q
                twait(index, 2 + xh, 1)
                tsend(n, index, 2 + xh, 1, across[1 - q])
            image_hop(n, 2, 1)
            for q in range(2):
                index = y_up * 2 + q
                twait(index, 2 + xh, 1)
                tsend(n, index, 2 + xh, 1, across[1 - q])
            for q in range(2):
                index = y_dn * 2 + q
                twait(index, 0, 2)
                tsend(n, index, 0, 1, up)
                index = y_up * 2 + q
                twait(index, 0, 2)
                tsend(n, index, 1, 1, dn)
                if q == 0:
                    image_hop(n, 3, 0)
            image_hop(n, 3, 1)
            for q in range(2):
                index = y_far * 2 + q
                twait(index, 2 + xh, 1)
                tsend(n, index, 2 + xh, 1, across[1 - q])
            image_last(n)
            for ya in (y, y_dn, y_up, y_far):
                for q in range(2):
                    twait(ya * 2 + q, 2 + xo, 1)
            for q in range(2):
                for k in range(2):
                    twait(y_far * 2 + q, k, 1)

        @when("odd")
        def _():
            n = "odd"
            mine, below, above, far = me, y_dn * 2 + xh, y_up * 2 + xh, y_far * 2 + xh
            for e in range(2):
                tsend(n, mine, 0, 2, across[e])
            for peer in (up, dn):
                tsend(n, mine, 2, 2, peer)
            for e in range(2):
                tsend(n, mine, 2 + e, 1, across[e])
            for peer in (up, dn):
                tsend(n, mine, 0, 2, peer)
            for h in range(2):
                landed(piece(z, h), r_x.at[h])
                isend(n, z, h, zp)
                isend(n, z, h, zm)
            to_sibling(n, z)
            twait(below, 2, 2)
            tsend(n, below, 2, 1, up)
            for e in range(2):
                tsend(n, below, 2 + e, 1, across[e])
            twait(above, 2, 2)
            tsend(n, above, 3, 1, dn)
            for e in range(2):
                tsend(n, above, 2 + e, 1, across[e])
            image_hop(n, 1, 0)
            twait(below, 0, 2)
            tsend(n, below, 0, 1, up)
            twait(above, 0, 2)
            tsend(n, above, 1, 1, dn)
            image_hop(n, 1, 1)
            for k in range(2):
                index = y * 2 + xo
                twait(index, k, 1)
                tsend(n, index, k, 1, up)
                tsend(n, index, k, 1, dn)
            for k in range(2):
                twait(far, 2 + k, 1)
                tsend(n, far, 2 + k, 1, across[k])
            for e in range(2):
                tsend(n, mine, 3 - e, 1, across[e])
                tsend(n, below, 3 - e, 1, across[e])
            image_hop(n, 2, 0)
            for e in range(2):
                tsend(n, above, 3 - e, 1, across[e])
                tsend(n, far, 3 - e, 1, across[e])
            image_hop(n, 2, 1)
            index = y_dn * 2 + xo
            twait(index, 0, 1)
            tsend(n, index, 0, 1, up)
            index = y_up * 2 + xo
            twait(index, 1, 1)
            tsend(n, index, 1, 1, dn)
            image_hop(n, 3, 0)
            image_hop(n, 3, 1)
            image_last(n)
            twait(y_dn * 2 + xo, 1, 1)
            twait(y_up * 2 + xo, 0, 1)
            for k in range(2):
                for q in range(2):
                    twait(y_far * 2 + q, k, 1)
            for ya in (y, y_dn, y_up, y_far):
                for k in range(2):
                    twait(ya * 2 + xo, 2 + k, 1)

        for peer in line_peers:
            send("all", pairs.at[z, c], pairs.at[z, c], r_pair.at[line_rank], peer)

    def first_id(index):
        return ((index * 8 + z) * 2 + c) * TOK

    sub_ids = lax.broadcasted_iota(jnp.int32, (TOK, 1), 0)

    def total(x):
        return jnp.sum(jnp.sum(x, axis=0, keepdims=True), axis=1, keepdims=True)

    if STEPS > 2:
        all_images = images[...].reshape(WIDE, D)

        def stats(p, carry):
            zi, ei = carry
            two = texts[pl.ds(2 * p, 2)].reshape(2 * TOK, D)
            dots = lax.dot_general(two, all_images, (((1,), (1,)), ((), ())), preferred_element_type=f32)
            scores = scale * dots
            ex = jnp.exp(scores - scale)
            exps[pl.ds(2 * p, 2)] = ex.reshape(2, TOK, WIDE)
            es = ex * scores
            zi = zi + jnp.sum(ex, axis=0, keepdims=True)
            ei = ei + jnp.sum(es, axis=0, keepdims=True)
            zr = ex[:, 0:TOK]
            er = es[:, 0:TOK]
            for k in range(1, 8):
                zr = zr + ex[:, k * TOK:(k + 1) * TOK]
                er = er + es[:, k * TOK:(k + 1) * TOK]
            for h in range(2):
                part = slice(h * TOK, (h + 1) * TOK)
                stat_send[1, pl.ds(2 * p + h, 1), :] = jnp.sum(zr[part].T, axis=0, keepdims=True)
                e_sums[1, pl.ds(2 * p + h, 1), :] = jnp.sum(er[part].T, axis=0, keepdims=True)
            return zi, ei

        zero = jnp.zeros((1, WIDE), f32)
        zi, ei = lax.fori_loop(0, 4, stats, (zero, zero))
        for k in range(8):
            stat_send[0, k:k + 1, :] = zi[:, k * TOK:(k + 1) * TOK]
            e_sums[0, k:k + 1, :] = ei[:, k * TOK:(k + 1) * TOK]

    if STEPS > 3:
        for peer in line_peers:
            send("all", stat_send.at[0], z_img_all.at[line_rank], r_zi.at[line_rank], peer)
        for peer in plane_peers:
            send("all", stat_send.at[1], z_txt_all.at[plane_rank], r_zt.at[plane_rank], peer)
        z_img_all[line_rank] = stat_send[0]
        z_txt_all[plane_rank] = stat_send[1]
        for dz in range(8):
            for dc in range(2):
                if dz or dc:
                    zo, co = (z + dz) % 8, (c + dc) % 2
                    landed(pairs.at[zo, co], r_pair.at[zo * 2 + co])

        def own_half(k, core):
            line = pairs[k, core, 0:1]
            return jnp.where(odd, line[:, HALF:TOK], line[:, 0:HALF])

        pair_row = jnp.concatenate([own_half(k, core) for k in range(8) for core in range(2)], axis=1)
        for other in line_others:
            landed(z_img_all.at[other], r_zi.at[other])
        for other in plane_others:
            landed(z_txt_all.at[other], r_zt.at[other])
        z_img = jnp.sum(z_img_all[...], axis=0)
        z_txt = jnp.sum(z_txt_all[...], axis=0)

    if STEPS > 4:
        half_img = 0.5 / z_img
        stat_send[2] = 0.5 / z_txt
        img_row = jnp.concatenate([half_img[k:k + 1] for k in range(8)], axis=1)

        def weigh(index, carry):
            column = jnp.broadcast_to(stat_send[2, pl.ds(index, 1), :], (TOK, TOK)).T
            ids = first_id(index) + sub_ids
            hits = []
            for k in range(8):
                lanes = slice(k * TOK, (k + 1) * TOK)
                match = pair_row[:, lanes] == ids
                ex = exps[index, :, lanes]
                value = ex * (img_row[:, lanes] + column)
                weights[index, :, lanes] = (value - jnp.where(match, 1.0, 0.0)).astype(bf16)
                hits.append(jnp.sum(jnp.where(match, ex, 0.0), axis=0, keepdims=True))
            return carry + jnp.concatenate(hits, axis=1)

        hit = lax.fori_loop(0, 8, weigh, jnp.zeros((1, WIDE), f32))

    def text_block(ya):
        pair_of = pl.ds(2 * ya, 2)
        two = weights[pair_of].reshape(2 * TOK, WIDE)
        part = jnp.dot(two, all_images, preferred_element_type=f32)
        text_part[pair_of] = part.reshape(2, TOK, D)

    def quart(k):
        return pl.ds(k * QUART, QUART)

    def stage(index, k):
        text_send[index, quart(k)] = text_part[index, quart(k)].astype(bf16)
        return text_send.at[index, quart(k)]

    def stage_two(ya, k):
        for q in range(2):
            stage(ya * 2 + q, k)
        return text_send.at[pl.ds(2 * ya, 2), quart(k)]

    def add(index, k, value):
        text_part[index, quart(k)] = text_part[index, quart(k)] + value.astype(f32)

    def give_b(slot, ya):
        for k in range(2):
            send("odd", stage(ya * 2 + xo, 2 + k), rb_even.at[slot, xh], r_be.at[slot, xh], across[k])

    def free_b(slot, ya):
        for q in range(2):
            send("even", stage(ya * 2 + q, 2 + xo), rb_odd.at[slot, xh, 0], r_bo.at[slot, xh, 0], across[q])

    def pass_b(slot, ya):
        for q in range(2):
            index = ya * 2 + q
            landed(rb_even.at[slot, 1 - q], r_be.at[slot, 1 - q])
            add(index, 2 + xh, rb_even[slot, 1 - q])
            send("even", stage(index, 2 + xh), rb_odd.at[slot, xh, 1], r_bo.at[slot, xh, 1], across[q])

    def take_b(slot, ya):
        index = ya * 2 + xh
        for part in range(2):
            for e in range(2):
                landed(rb_odd.at[slot, e, part], r_bo.at[slot, e, part])
                add(index, 2 + (e if part else 1 - e), rb_odd[slot, e, part])

    def image_block(p):
        lanes = pl.ds(pl.multiple_of(p * 2 * TOK, 2 * TOK), 2 * TOK)
        part = lax.dot_general(
            weights[:, :, lanes].reshape(WIDE, 2 * TOK), texts[...].reshape(WIDE, D),
            (((0,), (0,)), ((), ())), preferred_element_type=f32,
        )
        both = pl.ds(2 * p, 2)
        image_part[both] = part.reshape(2, 2, HALF, D)
        image_send[both, 1 - c] = image_part[both, 1 - c].astype(bf16)
        send("all", image_send.at[both, 1 - c], image_sib.at[both], r_is.at[p], sibling)

    def add_sibling(p):
        both = pl.ds(2 * p, 2)
        landed(image_sib.at[both], r_is.at[p])
        image_part[both, c] = image_part[both, c] + image_sib[both].astype(f32)

    def ring_send(m, h, right):
        hops = 4 - m
        slot = (z + hops) % 8 if right else (z + 8 - hops) % 8
        into = image_right if right else image_left
        sem = r_ir if right else r_il
        value = image_part[slot, c, quart(h)]
        if m > 1 or (m == 1 and h == (0 if right else 1)):
            landed(into.at[m - 1, quart(h)], sem.at[m - 1, h])
            value = value + into[m - 1, quart(h)].astype(f32)
        image_send[slot, c, quart(h)] = value.astype(bf16)
        send(
            "all", image_send.at[slot, c, quart(h)], into.at[m, quart(h)], sem.at[m, h], zp if right else zm
        )

    if STEPS > 5:
        half_z = z // 2
        p_far, p_up, p_dn, p_own = [(half_z + k) % 4 for k in (2, 1, 3, 0)]

        image_block(p_far)
        text_block(y_far)
        send("all", stage_two(y_far, 0), ra_one.at[0], r_a1.at[0], up)
        send("all", stage_two(y_far, 1), ra_one.at[1], r_a1.at[1], dn)

        def spread(slot, ya):
            @when("odd")
            def _():
                give_b(slot, ya)

            @when("even")
            def _():
                free_b(slot, ya)

        spread(0, y_far)
        text_block(y_dn)
        send("all", stage_two(y_dn, 0), ra_two.at[1, 0], r_a2.at[1, 0], dn)
        spread(1, y_dn)
        add_sibling(p_far)
        ring_send(0, 0, True)
        ring_send(0, 1, False)
        text_block(y_up)
        send("all", stage_two(y_up, 1), ra_two.at[0, 0], r_a2.at[0, 0], up)
        spread(2, y_up)
        image_block(p_up)

        @when("even")
        def _():
            pass_b(0, y_far)

        image_block(p_dn)
        add_sibling(p_up)

        def hop_a(way, ya, target):
            landed(ra_one.at[way], r_a1.at[way])
            for q in range(2):
                add(ya * 2 + q, way, ra_one[way, q])
            send("all", stage_two(ya, way), ra_two.at[way, 1], r_a2.at[way, 1], target)

        hop_a(0, y_up, up)
        hop_a(1, y_dn, dn)
        add_sibling(p_dn)
        ring_send(1, 1, True)
        ring_send(1, 0, False)
        text_block(y)
        spread(3, y)

        @when("even")
        def _():
            pass_b(1, y_dn)

        ring_send(1, 0, True)
        ring_send(1, 1, False)
        image_block(p_own)

        @when("even")
        def _():
            pass_b(2, y_up)
            pass_b(3, y)

        lane = lax.broadcasted_iota(jnp.int32, (8, TOK), 1)
        log_img = total(jnp.log(z_img))
        log_txt = total(jnp.log(z_txt))
        t_img = total(e_sums[0] / z_img)
        t_txt = total(e_sums[1] / z_txt)
        found = hit > 0.0
        matched = jnp.sum(
            jnp.where(found, jnp.log(jnp.where(found, hit, 1.0)) + scale, 0.0), axis=1, keepdims=True
        )
        scal_send[0] = jnp.where(
            lane == 0, log_txt,
            jnp.where(lane == 1, t_img, jnp.where(lane == 2, t_txt, jnp.where(lane == 3, matched, 0.0))),
        )
        for peer in line_peers:
            send("all", scal_send.at[0], scal_z.at[line_rank], r_sz.at[line_rank], peer)
        scal_z[line_rank] = scal_send[0]
        add_sibling(p_own)

        @when("odd")
        def _():
            take_b(0, y_far)
            send("odd", stage(y_far * 2 + xh, 2), rb_one.at[0], r_b1.at[0], up)
            send("odd", stage(y_far * 2 + xh, 3), rb_one.at[1], r_b1.at[1], dn)

        for h in (1, 0):
            ring_send(2, h, True)
            ring_send(2, 1 - h, False)

        for part in range(2):
            for way in range(2):
                landed(ra_two.at[way, part], r_a2.at[way, part])
                for q in range(2):
                    add(y * 2 + q, way if part else 1 - way, ra_two[way, part, q])

        @when("odd")
        def _():
            for k in range(2):
                send("odd", stage(y * 2 + xo, k), ra_x.at[xh], r_ax.at[xh], across[k])
            take_b(1, y_dn)
            take_b(2, y_up)
            send("odd", stage(y_up * 2 + xh, 3), rb_two.at[0, 0], r_b2.at[0, 0], up)
            send("odd", stage(y_dn * 2 + xh, 2), rb_two.at[1, 0], r_b2.at[1, 0], dn)
            for way, ya, target in ((0, y_up, up), (1, y_dn, dn)):
                landed(rb_one.at[way], r_b1.at[way])
                add(ya * 2 + xh, 2 + way, rb_one[way])
                send("odd", stage(ya * 2 + xh, 2 + way), rb_two.at[way, 1], r_b2.at[way, 1], target)

        @when("even")
        def _():
            for q in range(2):
                send("even", stage(y * 2 + q, xo), ra_fin.at[xh, 0], r_af.at[xh, 0], across[q])

        for h in (1, 0):
            ring_send(3, h, True)
            ring_send(3, 1 - h, False)

        @when("even")
        def _():
            for q in range(2):
                landed(ra_x.at[1 - q], r_ax.at[1 - q])
                add(y * 2 + q, xh, ra_x[1 - q])
                send("even", stage(y * 2 + q, xh), ra_fin.at[xh, 1], r_af.at[xh, 1], across[q])

        for other in line_others:
            landed(scal_z.at[other], r_sz.at[other])
        line_sum = jnp.sum(scal_z[...], axis=0)
        scal_send[1] = jnp.where(lane == 4, log_img, line_sum)
        for peer in plane_peers:
            send("all", scal_send.at[1], scal_p.at[plane_rank], r_sp.at[plane_rank], peer)
        scal_p[plane_rank] = scal_send[1]

        def finish(part, grads):
            unit32, lengths = normal(part)
            grads = scale * grads
            inner = jnp.sum(unit32 * grads, axis=1, keepdims=True)
            out_ref[0, part] = ((grads - unit32 * inner) / lengths).astype(bf16)

        @when("odd")
        def _():
            take_b(3, y)

        for h in range(2):
            landed(image_right.at[3, quart(h)], r_ir.at[3, h])
            landed(image_left.at[3, quart(h)], r_il.at[3, h])
        acc = image_part[z, c] + image_right[3].astype(f32) + image_left[3].astype(f32)

        @when("odd")
        def _():
            fin_send[...] = acc.astype(bf16)
            send("odd", fin_send, fin_recv, r_fin.at[0], partner)
            for part in range(2):
                for way in range(2):
                    landed(rb_two.at[way, part], r_b2.at[way, part])
                    add(me, 2 + (way if part else 1 - way), rb_two[way, part])
            finish(upper, text_part[me, upper])
            for part in range(2):
                for e in range(2):
                    landed(ra_fin.at[e, part], r_af.at[e, part])
                    add(me, e if part else 1 - e, ra_fin[e, part])
            finish(lower, text_part[me, lower])

        @when("even")
        def _():
            finish(lower, acc)
            landed(fin_recv, r_fin.at[0])
            finish(upper, fin_recv[...].astype(f32))

        for other in plane_others:
            landed(scal_p.at[other], r_sp.at[other])
        all_sum = jnp.sum(scal_p[...], axis=0)

        def pick(x, k):
            return jnp.sum(jnp.where(lane[0:1] == k, x[0:1], 0.0))

        log_all = jnp.where(odd, pick(line_sum, 0), pick(all_sum, 4))
        t_all = jnp.where(odd, pick(all_sum, 2), pick(all_sum, 1))
        p_all = pick(all_sum, 3)
        loss_ref[0] = (scale * TOKENS + log_all - p_all) * (1.0 / (2 * TOKENS))
        sgrad_ref[0] = (t_all - p_all) / scale * (1.0 / (2 * TOKENS))

    sizes = {
        (QUART, D): texts.at[0, 0:QUART], (HALF, D): texts.at[0, 0:HALF],
        (2, QUART, D): texts.at[0:2, 0:QUART], (2, HALF, D): texts.at[0:2, 0:HALF],
        (8, TOK): stat_send.at[0],
    }
    for name, copies in pending.items():
        if copies:
            @when(name)
            def _():
                for slot, shape in copies:
                    pltpu.make_async_copy(sizes[shape], sizes[shape], s_all.at[slot]).wait()


def body(embeddings, pair, logit_scale):
    vmem = pl.BlockSpec(memory_space=pltpu.VMEM)
    smem = pl.BlockSpec(memory_space=pltpu.SMEM)
    dma = pltpu.SemaphoreType.DMA
    scratch = [
        ((TOK, D), bf16),
        ((HALF, D), bf16),
        ((8, 2, HALF, D), bf16),
        ((8, TOK, D), bf16),
        ((8, 2, 8, TOK), jnp.int32),
        ((8, TOK, WIDE), f32),
        ((8, TOK, WIDE), bf16),
        ((8, TOK, D), f32),
        ((8, TOK, D), bf16),
        ((2, 2, QUART, D), bf16),
        ((2, 2, 2, QUART, D), bf16),
        ((2, QUART, D), bf16),
        ((2, 2, QUART, D), bf16),
        ((4, 2, 2, QUART, D), bf16),
        ((4, 2, QUART, D), bf16),
        ((2, QUART, D), bf16),
        ((2, 2, QUART, D), bf16),
        ((8, 2, HALF, D), f32),
        ((8, 2, HALF, D), bf16),
        ((8, HALF, D), bf16),
        ((4, HALF, D), bf16),
        ((4, HALF, D), bf16),
        ((3, 8, TOK), f32),
        ((16, 8, TOK), f32),
        ((16, 8, TOK), f32),
        ((2, 8, TOK), f32),
        ((2, 8, TOK), f32),
        ((16, 8, TOK), f32),
        ((16, 8, TOK), f32),
        ((HALF, D), bf16),
        ((HALF, D), bf16),
    ]
    sems = [
        (1,), (SENDS,), (8, 4), (8, 2), (8,), (16,), (2,), (16,), (16,), (16,), (16,),
        (2,), (2, 2), (2,), (2, 2), (4, 2, 2), (4, 2), (2,), (2, 2), (4,), (4, 2), (4, 2), (1,),
    ]
    return pl.pallas_call(
        kernel,
        out_shape=(
            jax.ShapeDtypeStruct((1, TOK, D), bf16),
            jax.ShapeDtypeStruct((1,), f32),
            jax.ShapeDtypeStruct((1,), f32),
        ),
        in_specs=[smem, pl.BlockSpec(memory_space=pl.ANY), vmem],
        out_specs=(vmem, smem, smem),
        scratch_shapes=[pltpu.VMEM(shape, dtype) for shape, dtype in scratch] + [dma(shape) for shape in sems],
        compiler_params=pltpu.CompilerParams(
            collective_id=0, has_side_effects=True, vmem_limit_bytes=56 * 2 ** 20
        ),
        cost_estimate=pl.CostEstimate(flops=6 * WIDE * WIDE * D, bytes_accessed=2 ** 20, transcendentals=2 ** 20),
        name="contrastive",
    )(
        logit_scale.astype(f32).reshape(1),
        embeddings,
        pair.reshape(1, TOK),
    )


def solution(mesh):
    placed = (P("tower", "blk", None), P("blk"), P())
    return jax.shard_map(
        body,
        mesh=mesh,
        in_specs=placed,
        out_specs=(P("tower", "blk", None), P("tower"), P("tower")),
        check_vma=False,
    )
```

```python
import jax
import jax.numpy as jnp
from jax import lax
from jax.experimental import pallas as pl
from jax.experimental.pallas import tpu as pltpu
from jax.sharding import PartitionSpec as P

eps = 1e-06
TOK = 128
D = 896
TOKENS = 16384
NY, NXH, NZ, NC = 4, 2, 8, 2
HALF, QUART = TOK // 2, TOK // 4
WIDE = 8 * TOK
f32 = jnp.float32
bf16 = jnp.bfloat16
MESH = pl.DeviceIdType.MESH
STEPS = 9
WAVES = 2
DIRECT = 0
DRAINS = 0
ORDER = 1
SCAL = 0
SCAL2 = 1
SENDS = 48


def device(t, y, xh, z, c):
    return (t, ((y * NXH + xh) * NZ + z) * NC + c)


def kernel(
    scale_ref, emb_hbm, pair_ref,
    out_ref, loss_ref, sgrad_ref,
    emb_ref, own, images, texts, pairs, exps, weights,
    text_part, text_send, ra_one, ra_two, ra_x, ra_fin, rb_odd, rb_even, rb_one, rb_two,
    image_part, image_send, image_sib, image_right, image_left, image_first,
    z_row, e_row, columns, pair_rows, hits, stat_send, z_img_all, z_txt_all, e_sums, scal_send, scal_z, scal_p, fin_send, fin_recv,
    s_in, s_all, r_txt, r_img, r_sib, r_pair, r_x, r_zi, r_zt, r_sz, r_sp,
    r_a1, r_a2, r_ax, r_af, r_bo, r_be, r_b1, r_b2, r_is, r_ir, r_il, r_fin, r_far, r_i0,
):
    t = lax.axis_index("tower")
    b = lax.axis_index("blk")
    c = b % 2
    z = (b // 2) % 8
    xh = (b // 16) % 2
    y = b // 32
    odd = t == 1
    even = t == 0
    line_rank = z * 2 + c
    plane_rank = (t * 4 + y) * 2 + xh
    me = y * 2 + xh
    scale = scale_ref[0]
    y_up, y_dn, y_far = (y + 1) % 4, (y + 3) % 4, (y + 2) % 4
    xo = 1 - xh

    conds = {"all": None, "odd": odd, "even": even}
    pending = {name: {} for name in conds}
    count = [0]

    def when(name):
        if name == "all":
            return lambda fn: fn()
        return pl.when(conds[name])

    def send(name, src, dst, rsem, target, batch=""):
        groups = pending[name].setdefault((src.shape, batch), [])
        if not groups or groups[-1][1] == (4 if len(src.shape) == 3 else 15 if src.shape[0] == 8 else 8):
            groups.append([count[0], 0])
            count[0] += 1
        groups[-1][1] += 1
        pltpu.make_async_remote_copy(
            src_ref=src, dst_ref=dst, send_sem=s_all.at[groups[-1][0]], recv_sem=rsem,
            device_id=target, device_id_type=MESH,
        ).start()

    def drain(name, batch=None):
        for key in [k for k in pending[name] if batch is None or k[1] == batch]:
            shape = key[0]
            for slot, copies in pending[name].pop(key):
                if len(shape) == 3:
                    like = texts.at[0:2 * copies, 0:shape[1]]
                elif shape[0] == 8:
                    like = z_img_all.at[0:copies]
                else:
                    like = texts.at[0:copies, 0:shape[0]]
                pltpu.make_async_copy(like, like, s_all.at[slot]).wait()

    def landed(dst, rsem):
        pltpu.make_async_copy(dst, dst, rsem).wait()

    up = device(t, y_up, xh, z, c)
    dn = device(t, y_dn, xh, z, c)
    zp = device(t, y, xh, (z + 1) % 8, c)
    zm = device(t, y, xh, (z + 7) % 8, c)
    sibling = device(t, y, xh, z, 1 - c)
    zp_sibling = device(t, y, xh, (z + 1) % 8, 1 - c)
    zm_sibling = device(t, y, xh, (z + 7) % 8, 1 - c)
    across = [device(1 - t, y, 0, z, c), device(1 - t, y, 1, z, c)]
    partner = device(1 - t, y, xh, z, c)
    partner_zp = device(1 - t, y, xh, (z + 1) % 8, c)
    partner_zm = device(1 - t, y, xh, (z + 7) % 8, c)
    line_peers = [
        device(t, y, xh, (z + dz) % 8, (c + dc) % 2)
        for dz in (4, 3, 5, 2, 6, 1, 7, 0) for dc in (0, 1) if dz or dc
    ]
    plane_peers = [
        device((t + dt) % 2, (y + dy) % 4, (xh + dx) % 2, z, c)
        for dy in (2, 1, 3, 0) for dx in (1, 0) for dt in (0, 1) if dy or dx or dt
    ]

    fetch = pltpu.make_async_copy(emb_hbm.at[0], emb_ref, s_in.at[0])
    fetch.start()
    barrier = pltpu.get_barrier_semaphore()
    for peer in (up, dn, zp, zm, sibling, across[0], across[1], partner_zp, partner_zm):
        pl.semaphore_signal(barrier, inc=1, device_id=peer, device_id_type=MESH)
    fetch.wait()

    def normal(part):
        wide = emb_ref[part].astype(f32)
        lengths = jnp.sqrt(jnp.sum(wide * wide, axis=1, keepdims=True) + eps)
        return wide / lengths, lengths

    lower, upper = slice(0, HALF), slice(HALF, TOK)
    unit_low = normal(lower)[0].astype(bf16)
    unit_high = normal(upper)[0].astype(bf16)

    @when("odd")
    def _():
        texts[me, lower] = unit_low
        texts[me, upper] = unit_high

    @when("even")
    def _():
        images[z, c] = unit_low
        own[...] = unit_high

    pairs[line_rank] = jnp.broadcast_to(pair_ref[...], (8, TOK))
    pl.semaphore_wait(barrier, 9)

    def rows(index, quarter):
        return texts.at[index, pl.ds(quarter * QUART, QUART)]

    def tsend(name, index, quarter, target, batch=""):
        send(name, rows(index, quarter), rows(index, quarter), r_txt.at[index, quarter], target, batch)

    def twait(index, quarter):
        landed(rows(index, quarter), r_txt.at[index, quarter])

    size = HALF // WAVES

    def piece(slot, w):
        return images.at[slot, c, pl.ds(w * size, size)]

    def isend(name, slot, w, target):
        send(name, piece(slot, w), piece(slot, w), r_img.at[slot, w], target)

    def iwait(slot, w):
        landed(piece(slot, w), r_img.at[slot, w])

    def to_sibling(name, slot):
        send(name, images.at[slot, c], images.at[slot, c], r_sib.at[slot], sibling)

    def image_hop(name, k):
        left, right = (z + 8 - k) % 8, (z + k) % 8
        for w in range(WAVES):
            iwait(left, w)
            if k < 3 or w < WAVES // 2:
                isend(name, left, w, zp)
            if k == 3 and w < WAVES // 2:
                send(name, piece(left, w), piece(left, w), r_far.at[w], zp_sibling)
            iwait(right, w)
            if k < 3 or w >= WAVES // 2:
                isend(name, right, w, zm)
            if k == 3 and w >= WAVES // 2:
                send(name, piece(right, w), piece(right, w), r_far.at[w], zm_sibling)
        to_sibling(name, left)
        to_sibling(name, right)

    def image_last(name):
        far = (z + 4) % 8
        for w in range(WAVES):
            iwait(far, w)
            landed(images.at[far, 1 - c, pl.ds(w * size, size)], r_far.at[w])

    def siblings(p):
        for h in range(2):
            landed(images.at[2 * p + h, 1 - c], r_sib.at[2 * p + h])

    half_z = z // 2
    p_far, p_up, p_dn, p_own = [(half_z + k) % 4 for k in (2, 1, 3, 0)]

    if STEPS > 1:
        @when("even")
        def _():
            n = "even"
            first, second = device(t, (y + 1 + 2 * xh) % 4, xh, z, c), device(t, (y + 1 + 2 * xo) % 4, xh, z, c)

            def mine(w):
                return own.at[pl.ds(w * size, size)]

            for w in range(WAVES):
                isend(n, z, w, zp)
                isend(n, z, w, zm)
                if DIRECT:
                    send(n, mine(w), piece(z, w), r_img.at[z, w], partner_zp)
                    send(n, mine(w), piece(z, w), r_img.at[z, w], partner_zm)
                else:
                    send(n, mine(w), piece(z, w), r_x.at[w], partner)
            to_sibling(n, z)
            image_hop(n, 1)
            for q in range(2):
                index = y * 2 + q
                twait(index, xh)
                tsend(n, index, xh, across[1 - q])
                tsend(n, index, xh, first)
            for q in range(2):
                index = y * 2 + q
                twait(index, xo)
                tsend(n, index, xo, second)
            for q in range(2):
                index = y * 2 + q
                twait(index, 2 + xh)
                tsend(n, index, 2 + xh, across[1 - q])
            for q in range(2):
                index = y * 2 + q
                tsend(n, index, xh, second)
                tsend(n, index, xo, first)
            ya, yb = (y + 3 + 2 * xh) % 4, (y + 1 + 2 * xh) % 4
            for q in range(2):
                index = ya * 2 + q
                twait(index, 2 + xh)
                tsend(n, index, 2 + xh, across[1 - q])
            image_hop(n, 2)
            for q in range(2):
                index = yb * 2 + q
                twait(index, 2 + xh)
                tsend(n, index, 2 + xh, across[1 - q])
            for w in range(WAVES if DIRECT else 0):
                send(n, mine(w), piece(z, w), r_x.at[w], partner)
            for q in range(2):
                twait(y_dn * 2 + q, 0)
                tsend(n, y_dn * 2 + q, 0, up)
                twait(y_up * 2 + q, 1)
                tsend(n, y_up * 2 + q, 1, dn)
            for q in range(2):
                index = y_far * 2 + q
                twait(index, 2 + xh)
                tsend(n, index, 2 + xh, across[1 - q])
            image_hop(n, 3)
            for q in range(2):
                twait(y_dn * 2 + q, 1)
                twait(y_up * 2 + q, 0)
                for k in range(2):
                    twait(y_far * 2 + q, k)
                for ya in (y, y_dn, y_up, y_far):
                    twait(ya * 2 + q, 2 + xo)

        @when("odd")
        def _():
            n = "odd"
            mine, below, above, far = me, y_dn * 2 + xh, y_up * 2 + xh, y_far * 2 + xh
            other = y * 2 + xo

            def relayed(index, k):
                tsend(n, index, 2 + k, across[k])

            def kept(index):
                for e in range(2):
                    tsend(n, index, 3 - e, across[e])

            for e in range(2):
                tsend(n, mine, e, across[e], "s")
            tsend(n, mine, 2, up, "s")
            tsend(n, mine, 3, dn, "s")
            if DRAINS > 0:
                drain(n, "s")
            for e in range(2):
                tsend(n, mine, 1 - e, across[e], "s")
            tsend(n, mine, 3, up, "s")
            tsend(n, mine, 2, dn, "s")
            if DRAINS > 1:
                drain(n, "s")
            if not DIRECT:
                for w in range(WAVES):
                    landed(piece(z, w), r_x.at[w])
                    isend(n, z, w, zp)
                    isend(n, z, w, zm)
                to_sibling(n, z)
            for e in range(2):
                relayed(mine, e)
            tsend(n, mine, 0, up)
            tsend(n, mine, 1, dn)
            twait(below, 2)
            tsend(n, below, 2, up)
            relayed(below, 0)
            twait(above, 3)
            tsend(n, above, 3, dn)
            relayed(above, 1)
            tsend(n, mine, 1, up)
            tsend(n, mine, 0, dn)
            twait(below, 3)
            relayed(below, 1)
            twait(above, 2)
            relayed(above, 0)
            image_hop(n, 1)
            twait(below, 0)
            tsend(n, below, 0, up)
            twait(above, 1)
            tsend(n, above, 1, dn)
            twait(far, 2)
            relayed(far, 0)
            twait(far, 3)
            relayed(far, 1)
            twait(other, 0)
            tsend(n, other, 0, up)
            twait(other, 1)
            tsend(n, other, 1, dn)
            kept(mine)
            tsend(n, other, 1, up)
            tsend(n, other, 0, dn)
            kept(below)
            kept(above)
            image_hop(n, 2)
            kept(far)
            twait(y_dn * 2 + xo, 0)
            tsend(n, y_dn * 2 + xo, 0, up)
            twait(y_up * 2 + xo, 1)
            tsend(n, y_up * 2 + xo, 1, dn)
            for q in (xh, xo):
                twait(y_dn * 2 + q, 1)
                twait(y_up * 2 + q, 0)
                for k in range(2):
                    twait(y_far * 2 + q, k)
            for ya in (y, y_dn, y_up, y_far):
                for k in range(2):
                    twait(ya * 2 + xo, 2 + k)
            if DIRECT:
                for w in range(WAVES):
                    landed(piece(z, w), r_x.at[w])
                to_sibling(n, z)

        siblings(p_own)

    def first_id(index):
        return ((index * 8 + z) * 2 + c) * TOK

    sub_ids = lax.broadcasted_iota(jnp.int32, (TOK, 1), 0)

    def total(x):
        return jnp.sum(jnp.sum(x, axis=0, keepdims=True), axis=1, keepdims=True)

    if STEPS > 2:
        all_texts = texts[...].reshape(WIDE, D)

        def stats(p, first):
            two = images[pl.ds(2 * p, 2)].reshape(2 * TOK, D)
            dots = lax.dot_general(all_texts, two, (((1,), (1,)), ((), ())), preferred_element_type=f32)
            scores = scale * dots
            ex = jnp.exp(scores - scale)
            exps[:, :, pl.ds(pl.multiple_of(p * 2 * TOK, 2 * TOK), 2 * TOK)] = ex.reshape(8, TOK, 2 * TOK)
            es = ex * scores
            z_sum = jnp.sum(ex, axis=0, keepdims=True)
            e_sum = jnp.sum(es, axis=0, keepdims=True)
            for h in range(2):
                part = slice(h * TOK, (h + 1) * TOK)
                stat_send[0, pl.ds(2 * p + h, 1), :] = z_sum[:, part]
                e_sums[pl.ds(2 * p + h, 1), :] = e_sum[:, part]
            zr = (ex[:, 0:TOK] + ex[:, TOK:]).reshape(8, TOK, TOK)
            er = (es[:, 0:TOK] + es[:, TOK:]).reshape(8, TOK, TOK)
            z_row[...] = zr if first else z_row[...] + zr
            e_row[...] = er if first else e_row[...] + er

        stats(p_own, True)

        @when("odd")
        def _():
            image_hop("odd", 3)

        for p in (p_up, p_dn):
            siblings(p)
            stats(p, False)

        @when("even")
        def _():
            image_last("even")

        @when("odd")
        def _():
            image_last("odd")

        for peer in line_peers if STEPS > 3 else ():
            send("all", pairs.at[line_rank], pairs.at[line_rank], r_pair.at[0], peer)
        near_far = (z + 3 + 2 * ((z + 1) % 2)) % 8
        landed(images.at[near_far, 1 - c], r_sib.at[near_far])
        stats(p_far, False)
        for k in range(8):
            stat_send[1, k:k + 1, :] = jnp.sum(z_row[k].T, axis=0, keepdims=True)
        all_images = images[...].reshape(WIDE, D)

    if STEPS > 3:
        for peer in line_peers:
            send("all", stat_send.at[0], z_img_all.at[line_rank], r_zi.at[0], peer)
        for peer in plane_peers:
            send("all", stat_send.at[1], z_txt_all.at[plane_rank], r_zt.at[0], peer)
        z_img_all[line_rank] = stat_send[0]
        z_txt_all[plane_rank] = stat_send[1]
        landed(pairs.at[0:15], r_pair.at[0])

        def own_half(k, core):
            line = pairs[2 * k + core, 0:1]
            return jnp.where(odd, line[:, HALF:TOK], line[:, 0:HALF])

        for k in range(8):
            pair_rows[k:k + 1, :] = jnp.concatenate([own_half(k, core) for core in range(2)], axis=1)
        landed(z_img_all.at[0:15], r_zi.at[0])
        landed(z_txt_all.at[0:15], r_zt.at[0])
        z_img = jnp.sum(z_img_all[...], axis=0)
        z_txt = jnp.sum(z_txt_all[...], axis=0)

    if STEPS > 4:
        stat_send[3] = 0.5 / z_img
        stat_send[2] = 0.5 / z_txt
        for k in range(8):
            columns[k] = jnp.broadcast_to(stat_send[2, k:k + 1, :], (TOK, TOK)).T

        def weigh(p):
            lanes = pl.ds(pl.multiple_of(p * 2 * TOK, 2 * TOK), 2 * TOK)
            img = jnp.concatenate([stat_send[3, pl.ds(2 * p + h, 1), :] for h in range(2)], axis=1)
            partners = jnp.concatenate([pair_rows[pl.ds(2 * p + h, 1), :] for h in range(2)], axis=1)

            def step(index, carry):
                column = columns[index]
                ids = first_id(index) + sub_ids
                match = partners == ids
                ex = exps[index, :, lanes]
                value = ex * (img + jnp.concatenate([column, column], axis=1))
                weights[index, :, lanes] = (value - jnp.where(match, 1.0, 0.0)).astype(bf16)
                return carry + jnp.sum(jnp.where(match, ex, 0.0), axis=0, keepdims=True)

            hit = lax.fori_loop(0, 8, step, jnp.zeros((1, 2 * TOK), f32))
            for h in range(2):
                hits[pl.ds(2 * p + h, 1), :] = hit[:, h * TOK:(h + 1) * TOK]

        weigh(p_far)

    def text_block(ya):
        pair_of = pl.ds(2 * ya, 2)
        two = weights[pair_of].reshape(2 * TOK, WIDE)
        part = jnp.dot(two, all_images, preferred_element_type=f32)
        text_part[pair_of] = part.reshape(2, TOK, D)

    def quart(k):
        return pl.ds(k * QUART, QUART)

    def stage(index, k):
        text_send[index, quart(k)] = text_part[index, quart(k)].astype(bf16)
        return text_send.at[index, quart(k)]

    def stage_two(ya, k):
        for q in range(2):
            stage(ya * 2 + q, k)
        return text_send.at[pl.ds(2 * ya, 2), quart(k)]

    def add(index, k, value):
        text_part[index, quart(k)] = text_part[index, quart(k)] + value.astype(f32)

    def give_b(slot, ya):
        for k in range(2):
            send("odd", stage(ya * 2 + xo, 2 + k), rb_even.at[slot, xh], r_be.at[slot, xh], across[k])

    def free_b(slot, ya):
        for q in range(2):
            send("even", stage(ya * 2 + q, 2 + xo), rb_odd.at[slot, xh, 0], r_bo.at[slot, xh, 0], across[q])

    def pass_b(slot, ya):
        for q in range(2):
            index = ya * 2 + q
            landed(rb_even.at[slot, 1 - q], r_be.at[slot, 1 - q])
            add(index, 2 + xh, rb_even[slot, 1 - q])
            send("even", stage(index, 2 + xh), rb_odd.at[slot, xh, 1], r_bo.at[slot, xh, 1], across[q])

    def take_b(slot, ya):
        index = ya * 2 + xh
        for part in range(2):
            for e in range(2):
                landed(rb_odd.at[slot, e, part], r_bo.at[slot, e, part])
                add(index, 2 + (e if part else 1 - e), rb_odd[slot, e, part])

    def image_block(p, with_sibling=True):
        lanes = pl.ds(pl.multiple_of(p * 2 * TOK, 2 * TOK), 2 * TOK)
        part = lax.dot_general(
            weights[:, :, lanes].reshape(WIDE, 2 * TOK), texts[...].reshape(WIDE, D),
            (((0,), (0,)), ((), ())), preferred_element_type=f32,
        )
        both = pl.ds(2 * p, 2)
        image_part[both] = part.reshape(2, 2, HALF, D)
        if with_sibling:
            image_send[both, 1 - c] = image_part[both, 1 - c].astype(bf16)
            send("all", image_send.at[both, 1 - c], image_sib.at[both], r_is.at[p], sibling)

    def swap_near_far():
        image_send[near_far, 1 - c] = image_part[near_far, 1 - c].astype(bf16)
        send("all", image_send.at[near_far, 1 - c], image_sib.at[near_far], r_is.at[p_far], sibling)

    def add_near_far():
        landed(image_sib.at[near_far], r_is.at[p_far])
        image_part[near_far, c] = image_part[near_far, c] + image_sib[near_far].astype(f32)

    def add_sibling(p):
        both = pl.ds(2 * p, 2)
        landed(image_sib.at[both], r_is.at[p])
        image_part[both, c] = image_part[both, c] + image_sib[both].astype(f32)

    def source_of(slot, h):
        return image_send.at[slot, c, quart(h)]

    def ring_send(m, h, right):
        hops = 4 - m
        slot = (z + hops) % 8 if right else (z + 8 - hops) % 8
        into = image_right if right else image_left
        sem = r_ir if right else r_il
        value = image_part[slot, c, quart(h)]
        if m == 1 and h == (0 if right else 1):
            for core in range(2):
                landed(image_first.at[h, core], r_i0.at[h, core])
                value = value + image_first[h, core].astype(f32)
        if m > 1:
            landed(into.at[m - 1, quart(h)], sem.at[m - 1, h])
            value = value + into[m - 1, quart(h)].astype(f32)
        image_send[slot, c, quart(h)] = value.astype(bf16)
        if m < 3:
            send("all", source_of(slot, h), into.at[m, quart(h)], sem.at[m, h], zp if right else zm)
            return
        way = 0 if right else 1

        @when("even")
        def _():
            send("even", source_of(slot, h), into.at[m, quart(h)], sem.at[m, h], zp if right else zm)

        @when("odd")
        def _():
            send(
                "odd", source_of(slot, h), fin_recv.at[way, quart(h)], r_fin.at[way, h],
                partner_zp if right else partner_zm,
            )

    if STEPS > 5:
        def spread(slot, ya):
            @when("odd")
            def _():
                give_b(slot, ya)

            @when("even")
            def _():
                free_b(slot, ya)

        def pass_on(slot, ya):
            @when("even")
            def _():
                pass_b(slot, ya)

        def hop_a(way, ya, target):
            landed(ra_one.at[way], r_a1.at[way])
            for q in range(2):
                add(ya * 2 + q, way, ra_one[way, q])
            send("all", stage_two(ya, way), ra_two.at[way, 1], r_a2.at[way, 1], target)

        def r1():
            send("all", stage_two(y_far, 0), ra_one.at[0], r_a1.at[0], up)
            send("all", stage_two(y_far, 1), ra_one.at[1], r_a1.at[1], dn)

        def m0():
            far = (z + 4) % 8
            for way, right, left in ((0, zp, zp_sibling), (1, zm, zm_sibling)):
                for core, target in ((c, right), (1 - c, left)):
                    image_send[far, core, quart(way)] = image_part[far, core, quart(way)].astype(bf16)
                    send(
                        "all", image_send.at[far, core, quart(way)], image_first.at[way, c], r_i0.at[way, c], target
                    )

        def m1_free():
            add_near_far()
            add_sibling(p_up)
            add_sibling(p_dn)
            ring_send(1, 1, True)
            ring_send(1, 0, False)

        def m1():
            ring_send(1, 0, True)
            ring_send(1, 1, False)

        def far_b():
            @when("odd")
            def _():
                take_b(0, y_far)
                send("odd", stage(y_far * 2 + xh, 2), rb_one.at[0], r_b1.at[0], up)
                send("odd", stage(y_far * 2 + xh, 3), rb_one.at[1], r_b1.at[1], dn)

        def free_a(way, ya, target):
            send("all", stage_two(ya, 1 - way), ra_two.at[way, 0], r_a2.at[way, 0], target)

        def m2():
            for h in (1, 0):
                ring_send(2, h, True)
                ring_send(2, 1 - h, False)

        T = lambda ya, slot: (text_block(ya), spread(slot, ya))
        I = image_block
        def rest():
            for p in (p_up, p_dn, p_own):
                weigh(p)

        if ORDER == 1:
            I(p_far, False); m0(); swap_near_far(); rest(); T(y_far, 0); r1(); I(p_up); I(p_dn); T(y_dn, 1); m1_free(); free_a(1, y_dn, dn)
            T(y_up, 2); free_a(0, y_up, up); m1(); pass_on(0, y_far); hop_a(0, y_up, up); hop_a(1, y_dn, dn); T(y, 3)
            pass_on(1, y_dn); pass_on(2, y_up); I(p_own); far_b(); pass_on(3, y); m2()
        if ORDER == 2:
            I(p_far, False); m0(); swap_near_far(); rest(); T(y_far, 0); r1(); I(p_up); T(y_dn, 1); I(p_dn); m1_free(); free_a(1, y_dn, dn)
            T(y_up, 2); free_a(0, y_up, up); pass_on(0, y_far); m1(); T(y, 3); hop_a(0, y_up, up); hop_a(1, y_dn, dn)
            pass_on(1, y_dn); I(p_own); pass_on(2, y_up); pass_on(3, y); m2(); far_b()
        if ORDER == 3:
            I(p_far, False); m0(); swap_near_far(); rest(); T(y_far, 0); r1(); I(p_up); I(p_dn); m1_free(); T(y_dn, 1); free_a(1, y_dn, dn)
            T(y_up, 2); free_a(0, y_up, up); T(y, 3); m1(); pass_on(0, y_far); hop_a(0, y_up, up); hop_a(1, y_dn, dn)
            pass_on(1, y_dn); pass_on(2, y_up); I(p_own); far_b(); pass_on(3, y); m2()

        lane = lax.broadcasted_iota(jnp.int32, (8, TOK), 1)

        def scalars():
            log_img = total(jnp.log(z_img))
            log_txt = total(jnp.log(z_txt))
            t_img = total(e_sums[...] / z_img)
            t_acc = e_row[0] * columns[0]
            for k in range(1, 8):
                t_acc = t_acc + e_row[k] * columns[k]
            t_txt = 2.0 * total(t_acc)
            hit = hits[...]
            found = hit > 0.0
            matched = total(jnp.where(found, jnp.log(jnp.where(found, hit, 1.0)) + scale, 0.0))
            scal_send[0] = jnp.where(
                lane == 0, log_txt,
                jnp.where(lane == 1, t_img, jnp.where(lane == 2, t_txt, jnp.where(lane == 3, matched, 0.0))),
            )
            for peer in line_peers:
                send("all", scal_send.at[0], scal_z.at[line_rank], r_sz.at[0], peer)
            scal_z[line_rank] = scal_send[0]
            return log_img

        if SCAL == 0:
            log_img = scalars()
        add_sibling(p_own)

        @when("odd")
        def _():
            fin_send[...] = image_part[z, c].astype(bf16)
            send("odd", fin_send, fin_recv.at[2], r_fin.at[2, 0], partner)

        if SCAL == 1:
            log_img = scalars()

        for part in range(2):
            for way in range(2):
                landed(ra_two.at[way, part], r_a2.at[way, part])
                for q in range(2):
                    add(y * 2 + q, way if part else 1 - way, ra_two[way, part, q])

        @when("odd")
        def _():
            for k in range(2):
                send("odd", stage(y * 2 + xo, k), ra_x.at[xh], r_ax.at[xh], across[k])
            take_b(1, y_dn)
            take_b(2, y_up)
            send("odd", stage(y_up * 2 + xh, 3), rb_two.at[0, 0], r_b2.at[0, 0], up)
            send("odd", stage(y_dn * 2 + xh, 2), rb_two.at[1, 0], r_b2.at[1, 0], dn)
            for way, ya, target in ((0, y_up, up), (1, y_dn, dn)):
                landed(rb_one.at[way], r_b1.at[way])
                add(ya * 2 + xh, 2 + way, rb_one[way])
                send("odd", stage(ya * 2 + xh, 2 + way), rb_two.at[way, 1], r_b2.at[way, 1], target)

        @when("even")
        def _():
            for q in range(2):
                send("even", stage(y * 2 + q, xo), ra_fin.at[xh, 0], r_af.at[xh, 0], across[q])

        def second_step():
            landed(scal_z.at[0:15], r_sz.at[0])
            line_sum = jnp.sum(scal_z[...], axis=0)
            scal_send[1] = jnp.where(lane == 4, log_img, line_sum)
            for peer in plane_peers:
                send("all", scal_send.at[1], scal_p.at[plane_rank], r_sp.at[0], peer)
            scal_p[plane_rank] = scal_send[1]
            return line_sum

        if SCAL2 == 1:
            line_sum = second_step()

        for h in (1, 0):
            ring_send(3, h, True)
            ring_send(3, 1 - h, False)

        @when("even")
        def _():
            for q in range(2):
                landed(ra_x.at[1 - q], r_ax.at[1 - q])
                add(y * 2 + q, xh, ra_x[1 - q])
                send("even", stage(y * 2 + q, xh), ra_fin.at[xh, 1], r_af.at[xh, 1], across[q])

        if SCAL2 == 0:
            line_sum = second_step()

        def finish(part, grads):
            unit32, lengths = normal(part)
            grads = scale * grads
            inner = jnp.sum(unit32 * grads, axis=1, keepdims=True)
            out_ref[0, part] = ((grads - unit32 * inner) / lengths).astype(bf16)

        @when("odd")
        def _():
            take_b(3, y)

        @when("odd")
        def _():
            for part in range(2):
                for way in range(2):
                    landed(rb_two.at[way, part], r_b2.at[way, part])
                    add(me, 2 + (way if part else 1 - way), rb_two[way, part])
            finish(upper, text_part[me, upper])
            for part in range(2):
                for e in range(2):
                    landed(ra_fin.at[e, part], r_af.at[e, part])
                    add(me, e if part else 1 - e, ra_fin[e, part])
            finish(lower, text_part[me, lower])

        @when("even")
        def _():
            for h in range(2):
                landed(image_right.at[3, quart(h)], r_ir.at[3, h])
                landed(image_left.at[3, quart(h)], r_il.at[3, h])
            finish(lower, image_part[z, c] + image_right[3].astype(f32) + image_left[3].astype(f32))
            landed(fin_recv.at[2], r_fin.at[2, 0])
            for h in range(2):
                landed(fin_recv.at[0, quart(h)], r_fin.at[0, h])
                landed(fin_recv.at[1, quart(h)], r_fin.at[1, h])
            finish(
                upper,
                fin_recv[0].astype(f32) + fin_recv[1].astype(f32) + fin_recv[2].astype(f32),
            )

        landed(scal_p.at[0:15], r_sp.at[0])
        all_sum = jnp.sum(scal_p[...], axis=0)

        def pick(x, k):
            return jnp.sum(jnp.where(lane[0:1] == k, x[0:1], 0.0))

        log_all = jnp.where(odd, pick(line_sum, 0), pick(all_sum, 4))
        t_all = jnp.where(odd, pick(all_sum, 2), pick(all_sum, 1))
        p_all = pick(all_sum, 3)
        loss_ref[0] = (scale * TOKENS + log_all - p_all) * (1.0 / (2 * TOKENS))
        sgrad_ref[0] = (t_all - p_all) / scale * (1.0 / (2 * TOKENS))

    for name in pending:
        if pending[name]:
            @when(name)
            def _():
                drain(name)


def body(embeddings, pair, logit_scale):
    vmem = pl.BlockSpec(memory_space=pltpu.VMEM)
    smem = pl.BlockSpec(memory_space=pltpu.SMEM)
    dma = pltpu.SemaphoreType.DMA
    scratch = [
        ((TOK, D), bf16),
        ((HALF, D), bf16),
        ((8, 2, HALF, D), bf16),
        ((8, TOK, D), bf16),
        ((16, 8, TOK), jnp.int32),
        ((8, TOK, WIDE), f32),
        ((8, TOK, WIDE), bf16),
        ((8, TOK, D), f32),
        ((8, TOK, D), bf16),
        ((2, 2, QUART, D), bf16),
        ((2, 2, 2, QUART, D), bf16),
        ((2, QUART, D), bf16),
        ((2, 2, QUART, D), bf16),
        ((4, 2, 2, QUART, D), bf16),
        ((4, 2, QUART, D), bf16),
        ((2, QUART, D), bf16),
        ((2, 2, QUART, D), bf16),
        ((8, 2, HALF, D), f32),
        ((8, 2, HALF, D), bf16),
        ((8, HALF, D), bf16),
        ((4, HALF, D), bf16),
        ((4, HALF, D), bf16),
        ((2, 2, QUART, D), bf16),
        ((8, TOK, TOK), f32),
        ((8, TOK, TOK), f32),
        ((8, TOK, TOK), f32),
        ((8, TOK), jnp.int32),
        ((8, TOK), f32),
        ((4, 8, TOK), f32),
        ((16, 8, TOK), f32),
        ((16, 8, TOK), f32),
        ((8, TOK), f32),
        ((2, 8, TOK), f32),
        ((16, 8, TOK), f32),
        ((16, 8, TOK), f32),
        ((HALF, D), bf16),
        ((3, HALF, D), bf16),
    ]
    sems = [
        (1,), (SENDS,), (8, 4), (8, 4), (8,), (1,), (4,), (1,), (1,), (1,), (1,),
        (2,), (2, 2), (2,), (2, 2), (4, 2, 2), (4, 2), (2,), (2, 2), (4,), (4, 2), (4, 2), (3, 2), (4,), (2, 2),
    ]
    return pl.pallas_call(
        kernel,
        out_shape=(
            jax.ShapeDtypeStruct((1, TOK, D), bf16),
            jax.ShapeDtypeStruct((1,), f32),
            jax.ShapeDtypeStruct((1,), f32),
        ),
        in_specs=[smem, pl.BlockSpec(memory_space=pl.ANY), vmem],
        out_specs=(vmem, smem, smem),
        scratch_shapes=[pltpu.VMEM(shape, dtype) for shape, dtype in scratch] + [dma(shape) for shape in sems],
        compiler_params=pltpu.CompilerParams(
            collective_id=0, has_side_effects=True, vmem_limit_bytes=56 * 2 ** 20
        ),
        cost_estimate=pl.CostEstimate(flops=6 * WIDE * WIDE * D, bytes_accessed=2 ** 20, transcendentals=2 ** 20),
        name="contrastive",
    )(
        logit_scale.astype(f32).reshape(1),
        embeddings,
        pair.reshape(1, TOK),
    )


def solution(mesh):
    placed = (P("tower", "blk", None), P("blk"), P())
    return jax.shard_map(
        body,
        mesh=mesh,
        in_specs=placed,
        out_specs=(P("tower", "blk", None), P("tower"), P("tower")),
        check_vma=False,
    )
```

```python
import jax
import jax.numpy as jnp
from jax import lax
from jax.experimental import pallas as pl
from jax.experimental.pallas import tpu as pltpu
from jax.sharding import PartitionSpec as P

eps = 1e-06
TOK = 128
D = 896
TOKENS = 16384
NY, NXH, NZ, NC = 4, 2, 8, 2
HALF, QUART = TOK // 2, TOK // 4
WIDE = 8 * TOK
f32 = jnp.float32
bf16 = jnp.bfloat16
MESH = pl.DeviceIdType.MESH
STEPS = 9
WAVES = 2
DIRECT = 0
DRAINS = 0
ORDER = 4
OUTF = 1
SCAL = 0
SCAL2 = 1
SENDS = 48


def device(t, y, xh, z, c):
    return (t, ((y * NXH + xh) * NZ + z) * NC + c)


def kernel(
    scale_ref, emb_hbm, pair_ref,
    out_ref, loss_ref, sgrad_ref,
    emb_ref, own, images, texts, z_msg, exps, weights,
    text_part, text_send, ra_one, ra_two, ra_x, ra_fin, rb_odd, rb_even, rb_one, rb_two,
    image_part, image_send, image_sib, image_right, image_left, image_first,
    z_row, e_row, columns, pair_rows, hits, stat_send, z_img_all, z_txt_all, e_sums, scal_send, scal_z, scal_p, fin_send, fin_recv,
    s_in, s_all, r_txt, r_img, r_sib, r_x, r_zi, r_zt, r_sz, r_sp,
    r_a1, r_a2, r_ax, r_af, r_bo, r_be, r_b1, r_b2, r_is, r_ir, r_il, r_fin, r_far, r_i0,
):
    t = lax.axis_index("tower")
    b = lax.axis_index("blk")
    c = b % 2
    z = (b // 2) % 8
    xh = (b // 16) % 2
    y = b // 32
    odd = t == 1
    even = t == 0
    line_rank = z * 2 + c
    plane_rank = (t * 4 + y) * 2 + xh
    me = y * 2 + xh
    scale = scale_ref[0]
    y_up, y_dn, y_far = (y + 1) % 4, (y + 3) % 4, (y + 2) % 4
    xo = 1 - xh

    conds = {"all": None, "odd": odd, "even": even}
    pending = {name: {} for name in conds}
    count = [0]

    def when(name):
        if name == "all":
            return lambda fn: fn()
        return pl.when(conds[name])

    def send(name, src, dst, rsem, target, batch=""):
        groups = pending[name].setdefault((src.shape, batch), [])
        if not groups or groups[-1][1] == (4 if len(src.shape) == 3 else 15 if src.shape[1] == TOK else 8):
            groups.append([count[0], 0])
            count[0] += 1
        groups[-1][1] += 1
        pltpu.make_async_remote_copy(
            src_ref=src, dst_ref=dst, send_sem=s_all.at[groups[-1][0]], recv_sem=rsem,
            device_id=target, device_id_type=MESH,
        ).start()

    def drain(name, batch=None):
        for key in [k for k in pending[name] if batch is None or k[1] == batch]:
            shape = key[0]
            for slot, copies in pending[name].pop(key):
                if len(shape) == 3:
                    like = texts.at[0:2 * copies, 0:shape[1]]
                elif shape == (16, TOK):
                    like = z_img_all.at[0:copies]
                elif shape == (8, TOK):
                    like = z_txt_all.at[0:copies]
                else:
                    like = texts.at[0:copies, 0:shape[0]]
                pltpu.make_async_copy(like, like, s_all.at[slot]).wait()

    def landed(dst, rsem):
        pltpu.make_async_copy(dst, dst, rsem).wait()

    up = device(t, y_up, xh, z, c)
    dn = device(t, y_dn, xh, z, c)
    zp = device(t, y, xh, (z + 1) % 8, c)
    zm = device(t, y, xh, (z + 7) % 8, c)
    sibling = device(t, y, xh, z, 1 - c)
    zp_sibling = device(t, y, xh, (z + 1) % 8, 1 - c)
    zm_sibling = device(t, y, xh, (z + 7) % 8, 1 - c)
    across = [device(1 - t, y, 0, z, c), device(1 - t, y, 1, z, c)]
    partner = device(1 - t, y, xh, z, c)
    partner_zp = device(1 - t, y, xh, (z + 1) % 8, c)
    partner_zm = device(1 - t, y, xh, (z + 7) % 8, c)
    line_peers = [
        device(t, y, xh, (z + dz) % 8, (c + dc) % 2)
        for dz in (4, 3, 5, 2, 6, 1, 7, 0) for dc in (0, 1) if dz or dc
    ]
    plane_peers = [
        device((t + dt) % 2, (y + dy) % 4, (xh + dx) % 2, z, c)
        for dy in (2, 1, 3, 0) for dx in (1, 0) for dt in (0, 1) if dy or dx or dt
    ]

    fetch = pltpu.make_async_copy(emb_hbm.at[0], emb_ref, s_in.at[0])
    fetch.start()
    barrier = pltpu.get_barrier_semaphore()
    for peer in (up, dn, zp, zm, sibling, across[0], across[1], partner_zp, partner_zm):
        pl.semaphore_signal(barrier, inc=1, device_id=peer, device_id_type=MESH)
    fetch.wait()

    def normal(part):
        wide = emb_ref[part].astype(f32)
        lengths = jnp.sqrt(jnp.sum(wide * wide, axis=1, keepdims=True) + eps)
        return wide / lengths, lengths

    lower, upper = slice(0, HALF), slice(HALF, TOK)
    unit_low = normal(lower)[0].astype(bf16)
    unit_high = normal(upper)[0].astype(bf16)

    @when("odd")
    def _():
        texts[me, lower] = unit_low
        texts[me, upper] = unit_high

    @when("even")
    def _():
        images[z, c] = unit_low
        own[...] = unit_high

    z_msg[8:16, :] = jnp.broadcast_to(pair_ref[...], (8, TOK)).astype(f32)
    pl.semaphore_wait(barrier, 9)

    def rows(index, quarter):
        return texts.at[index, pl.ds(quarter * QUART, QUART)]

    def tsend(name, index, quarter, target, batch=""):
        send(name, rows(index, quarter), rows(index, quarter), r_txt.at[index, quarter], target, batch)

    def twait(index, quarter):
        landed(rows(index, quarter), r_txt.at[index, quarter])

    size = HALF // WAVES

    def piece(slot, w):
        return images.at[slot, c, pl.ds(w * size, size)]

    def isend(name, slot, w, target):
        send(name, piece(slot, w), piece(slot, w), r_img.at[slot, w], target)

    def iwait(slot, w):
        landed(piece(slot, w), r_img.at[slot, w])

    def to_sibling(name, slot):
        send(name, images.at[slot, c], images.at[slot, c], r_sib.at[slot], sibling)

    def image_hop(name, k):
        left, right = (z + 8 - k) % 8, (z + k) % 8
        for w in range(WAVES):
            iwait(left, w)
            if k < 3 or w < WAVES // 2:
                isend(name, left, w, zp)
            if k == 3 and w < WAVES // 2:
                send(name, piece(left, w), piece(left, w), r_far.at[w], zp_sibling)
            iwait(right, w)
            if k < 3 or w >= WAVES // 2:
                isend(name, right, w, zm)
            if k == 3 and w >= WAVES // 2:
                send(name, piece(right, w), piece(right, w), r_far.at[w], zm_sibling)
        to_sibling(name, left)
        to_sibling(name, right)

    def image_last(name):
        far = (z + 4) % 8
        for w in range(WAVES):
            iwait(far, w)
            landed(images.at[far, 1 - c, pl.ds(w * size, size)], r_far.at[w])

    def siblings(p):
        for h in range(2):
            landed(images.at[2 * p + h, 1 - c], r_sib.at[2 * p + h])

    half_z = z // 2
    p_far, p_up, p_dn, p_own = [(half_z + k) % 4 for k in (2, 1, 3, 0)]

    if STEPS > 1:
        @when("even")
        def _():
            n = "even"
            first, second = device(t, (y + 1 + 2 * xh) % 4, xh, z, c), device(t, (y + 1 + 2 * xo) % 4, xh, z, c)

            def mine(w):
                return own.at[pl.ds(w * size, size)]

            for w in range(WAVES):
                isend(n, z, w, zp)
                isend(n, z, w, zm)
                if DIRECT:
                    send(n, mine(w), piece(z, w), r_img.at[z, w], partner_zp)
                    send(n, mine(w), piece(z, w), r_img.at[z, w], partner_zm)
                else:
                    send(n, mine(w), piece(z, w), r_x.at[w], partner)
            to_sibling(n, z)
            image_hop(n, 1)
            for q in range(2):
                index = y * 2 + q
                twait(index, xh)
                tsend(n, index, xh, across[1 - q])
                tsend(n, index, xh, first)
            for q in range(2):
                index = y * 2 + q
                twait(index, xo)
                tsend(n, index, xo, second)
            for q in range(2):
                index = y * 2 + q
                twait(index, 2 + xh)
                tsend(n, index, 2 + xh, across[1 - q])
            for q in range(2):
                index = y * 2 + q
                tsend(n, index, xh, second)
                tsend(n, index, xo, first)
            ya, yb = (y + 3 + 2 * xh) % 4, (y + 1 + 2 * xh) % 4
            for q in range(2):
                index = ya * 2 + q
                twait(index, 2 + xh)
                tsend(n, index, 2 + xh, across[1 - q])
            image_hop(n, 2)
            for q in range(2):
                index = yb * 2 + q
                twait(index, 2 + xh)
                tsend(n, index, 2 + xh, across[1 - q])
            for w in range(WAVES if DIRECT else 0):
                send(n, mine(w), piece(z, w), r_x.at[w], partner)
            for q in range(2):
                twait(y_dn * 2 + q, 0)
                tsend(n, y_dn * 2 + q, 0, up)
                twait(y_up * 2 + q, 1)
                tsend(n, y_up * 2 + q, 1, dn)
            for q in range(2):
                index = y_far * 2 + q
                twait(index, 2 + xh)
                tsend(n, index, 2 + xh, across[1 - q])
            image_hop(n, 3)
            for q in range(2):
                twait(y_dn * 2 + q, 1)
                twait(y_up * 2 + q, 0)
                for k in range(2):
                    twait(y_far * 2 + q, k)
                for ya in (y, y_dn, y_up, y_far):
                    twait(ya * 2 + q, 2 + xo)

        @when("odd")
        def _():
            n = "odd"
            mine, below, above, far = me, y_dn * 2 + xh, y_up * 2 + xh, y_far * 2 + xh
            other = y * 2 + xo

            def relayed(index, k):
                tsend(n, index, 2 + k, across[k])

            def kept(index):
                for e in range(2):
                    tsend(n, index, 3 - e, across[e])

            for e in range(2):
                tsend(n, mine, e, across[e], "s")
            tsend(n, mine, 2, up, "s")
            tsend(n, mine, 3, dn, "s")
            if DRAINS > 0:
                drain(n, "s")
            for e in range(2):
                tsend(n, mine, 1 - e, across[e], "s")
            tsend(n, mine, 3, up, "s")
            tsend(n, mine, 2, dn, "s")
            if DRAINS > 1:
                drain(n, "s")
            if not DIRECT:
                for w in range(WAVES):
                    landed(piece(z, w), r_x.at[w])
                    isend(n, z, w, zp)
                    isend(n, z, w, zm)
                to_sibling(n, z)
            for e in range(2):
                relayed(mine, e)
            tsend(n, mine, 0, up)
            tsend(n, mine, 1, dn)
            twait(below, 2)
            tsend(n, below, 2, up)
            relayed(below, 0)
            twait(above, 3)
            tsend(n, above, 3, dn)
            relayed(above, 1)
            tsend(n, mine, 1, up)
            tsend(n, mine, 0, dn)
            twait(below, 3)
            relayed(below, 1)
            twait(above, 2)
            relayed(above, 0)
            image_hop(n, 1)
            twait(below, 0)
            tsend(n, below, 0, up)
            twait(above, 1)
            tsend(n, above, 1, dn)
            twait(far, 2)
            relayed(far, 0)
            twait(far, 3)
            relayed(far, 1)
            twait(other, 0)
            tsend(n, other, 0, up)
            twait(other, 1)
            tsend(n, other, 1, dn)
            kept(mine)
            tsend(n, other, 1, up)
            tsend(n, other, 0, dn)
            kept(below)
            kept(above)
            image_hop(n, 2)
            kept(far)
            twait(y_dn * 2 + xo, 0)
            tsend(n, y_dn * 2 + xo, 0, up)
            twait(y_up * 2 + xo, 1)
            tsend(n, y_up * 2 + xo, 1, dn)
            for q in (xh, xo):
                twait(y_dn * 2 + q, 1)
                twait(y_up * 2 + q, 0)
                for k in range(2):
                    twait(y_far * 2 + q, k)
            for ya in (y, y_dn, y_up, y_far):
                for k in range(2):
                    twait(ya * 2 + xo, 2 + k)
            if DIRECT:
                for w in range(WAVES):
                    landed(piece(z, w), r_x.at[w])
                to_sibling(n, z)

        siblings(p_own)

    def first_id(index):
        return ((index * 8 + z) * 2 + c) * TOK

    sub_ids = lax.broadcasted_iota(jnp.int32, (TOK, 1), 0)

    def total(x):
        return jnp.sum(jnp.sum(x, axis=0, keepdims=True), axis=1, keepdims=True)

    if STEPS > 2:
        all_texts = texts[...].reshape(WIDE, D)

        def stats(p, first):
            two = images[pl.ds(2 * p, 2)].reshape(2 * TOK, D)
            dots = lax.dot_general(all_texts, two, (((1,), (1,)), ((), ())), preferred_element_type=f32)
            scores = scale * dots
            ex = jnp.exp(scores - scale)
            exps[:, :, pl.ds(pl.multiple_of(p * 2 * TOK, 2 * TOK), 2 * TOK)] = ex.reshape(8, TOK, 2 * TOK)
            es = ex * scores
            z_sum = jnp.sum(ex, axis=0, keepdims=True)
            e_sum = jnp.sum(es, axis=0, keepdims=True)
            for h in range(2):
                part = slice(h * TOK, (h + 1) * TOK)
                z_msg[pl.ds(2 * p + h, 1), :] = z_sum[:, part]
                e_sums[pl.ds(2 * p + h, 1), :] = e_sum[:, part]
            zr = (ex[:, 0:TOK] + ex[:, TOK:]).reshape(8, TOK, TOK)
            er = (es[:, 0:TOK] + es[:, TOK:]).reshape(8, TOK, TOK)
            z_row[...] = zr if first else z_row[...] + zr
            e_row[...] = er if first else e_row[...] + er

        stats(p_own, True)

        @when("odd")
        def _():
            image_hop("odd", 3)

        for p in (p_up, p_dn):
            siblings(p)
            stats(p, False)

        @when("even")
        def _():
            image_last("even")

        @when("odd")
        def _():
            image_last("odd")

        near_far = (z + 3 + 2 * ((z + 1) % 2)) % 8
        landed(images.at[near_far, 1 - c], r_sib.at[near_far])
        stats(p_far, False)
        for peer in line_peers if STEPS > 3 else ():
            send("all", z_msg, z_img_all.at[line_rank], r_zi.at[0], peer)
        for k in range(8):
            stat_send[1, k:k + 1, :] = jnp.sum(z_row[k].T, axis=0, keepdims=True)
        all_images = images[...].reshape(WIDE, D)

    if STEPS > 3:
        for peer in plane_peers:
            send("all", stat_send.at[1], z_txt_all.at[plane_rank], r_zt.at[0], peer)
        z_img_all[line_rank] = z_msg[...]
        z_txt_all[plane_rank] = stat_send[1]
        landed(z_img_all.at[0:15], r_zi.at[0])

        def own_half(k, core):
            line = z_img_all[2 * k + core, 8:9]
            return jnp.where(odd, line[:, HALF:TOK], line[:, 0:HALF]).astype(jnp.int32)

        for k in range(8):
            pair_rows[k:k + 1, :] = jnp.concatenate([own_half(k, core) for core in range(2)], axis=1)
        landed(z_txt_all.at[0:15], r_zt.at[0])
        z_img = jnp.sum(z_img_all[:, 0:8], axis=0)
        z_txt = jnp.sum(z_txt_all[...], axis=0)

    if STEPS > 4:
        stat_send[3] = 0.5 / z_img
        stat_send[2] = 0.5 / z_txt
        for k in range(8):
            columns[k] = jnp.broadcast_to(stat_send[2, k:k + 1, :], (TOK, TOK)).T

        def weigh(p):
            lanes = pl.ds(pl.multiple_of(p * 2 * TOK, 2 * TOK), 2 * TOK)
            img = jnp.concatenate([stat_send[3, pl.ds(2 * p + h, 1), :] for h in range(2)], axis=1)
            partners = jnp.concatenate([pair_rows[pl.ds(2 * p + h, 1), :] for h in range(2)], axis=1)

            def step(index, carry):
                column = columns[index]
                ids = first_id(index) + sub_ids
                match = partners == ids
                ex = exps[index, :, lanes]
                value = ex * (img + jnp.concatenate([column, column], axis=1))
                weights[index, :, lanes] = (value - jnp.where(match, 1.0, 0.0)).astype(bf16)
                return carry + jnp.sum(jnp.where(match, ex, 0.0), axis=0, keepdims=True)

            hit = lax.fori_loop(0, 8, step, jnp.zeros((1, 2 * TOK), f32))
            for h in range(2):
                hits[pl.ds(2 * p + h, 1), :] = hit[:, h * TOK:(h + 1) * TOK]

        weigh(p_far)

    def text_block(ya):
        pair_of = pl.ds(2 * ya, 2)
        two = weights[pair_of].reshape(2 * TOK, WIDE)
        part = jnp.dot(two, all_images, preferred_element_type=f32)
        text_part[pair_of] = part.reshape(2, TOK, D)

    def quart(k):
        return pl.ds(k * QUART, QUART)

    def stage(index, k):
        text_send[index, quart(k)] = text_part[index, quart(k)].astype(bf16)
        return text_send.at[index, quart(k)]

    def stage_two(ya, k):
        for q in range(2):
            stage(ya * 2 + q, k)
        return text_send.at[pl.ds(2 * ya, 2), quart(k)]

    def add(index, k, value):
        text_part[index, quart(k)] = text_part[index, quart(k)] + value.astype(f32)

    def give_b(slot, ya):
        for k in range(2):
            send("odd", stage(ya * 2 + xo, 2 + k), rb_even.at[slot, xh], r_be.at[slot, xh], across[k])

    def free_b(slot, ya):
        for q in range(2):
            send("even", stage(ya * 2 + q, 2 + xo), rb_odd.at[slot, xh, 0], r_bo.at[slot, xh, 0], across[q])

    def pass_b(slot, ya):
        for q in range(2):
            index = ya * 2 + q
            landed(rb_even.at[slot, 1 - q], r_be.at[slot, 1 - q])
            add(index, 2 + xh, rb_even[slot, 1 - q])
            send("even", stage(index, 2 + xh), rb_odd.at[slot, xh, 1], r_bo.at[slot, xh, 1], across[q])

    def take_b(slot, ya):
        index = ya * 2 + xh
        for part in range(2):
            for e in range(2):
                landed(rb_odd.at[slot, e, part], r_bo.at[slot, e, part])
                add(index, 2 + (e if part else 1 - e), rb_odd[slot, e, part])

    def image_block(p, with_sibling=True):
        lanes = pl.ds(pl.multiple_of(p * 2 * TOK, 2 * TOK), 2 * TOK)
        part = lax.dot_general(
            weights[:, :, lanes].reshape(WIDE, 2 * TOK), texts[...].reshape(WIDE, D),
            (((0,), (0,)), ((), ())), preferred_element_type=f32,
        )
        both = pl.ds(2 * p, 2)
        image_part[both] = part.reshape(2, 2, HALF, D)
        if with_sibling:
            image_send[both, 1 - c] = image_part[both, 1 - c].astype(bf16)
            send("all", image_send.at[both, 1 - c], image_sib.at[both], r_is.at[p], sibling)

    def swap_near_far():
        image_send[near_far, 1 - c] = image_part[near_far, 1 - c].astype(bf16)
        send("all", image_send.at[near_far, 1 - c], image_sib.at[near_far], r_is.at[p_far], sibling)

    def add_near_far():
        landed(image_sib.at[near_far], r_is.at[p_far])
        image_part[near_far, c] = image_part[near_far, c] + image_sib[near_far].astype(f32)

    def add_sibling(p):
        both = pl.ds(2 * p, 2)
        landed(image_sib.at[both], r_is.at[p])
        image_part[both, c] = image_part[both, c] + image_sib[both].astype(f32)

    def source_of(slot, h):
        return image_send.at[slot, c, quart(h)]

    def ring_send(m, h, right):
        hops = 4 - m
        slot = (z + hops) % 8 if right else (z + 8 - hops) % 8
        into = image_right if right else image_left
        sem = r_ir if right else r_il
        value = image_part[slot, c, quart(h)]
        if m == 1 and h == (0 if right else 1):
            for core in range(2):
                landed(image_first.at[h, core], r_i0.at[h, core])
                value = value + image_first[h, core].astype(f32)
        if m > 1:
            landed(into.at[m - 1, quart(h)], sem.at[m - 1, h])
            value = value + into[m - 1, quart(h)].astype(f32)
        image_send[slot, c, quart(h)] = value.astype(bf16)
        if m < 3:
            send("all", source_of(slot, h), into.at[m, quart(h)], sem.at[m, h], zp if right else zm)
            return
        way = 0 if right else 1

        @when("even")
        def _():
            send("even", source_of(slot, h), into.at[m, quart(h)], sem.at[m, h], zp if right else zm)

        @when("odd")
        def _():
            send(
                "odd", source_of(slot, h), fin_recv.at[way, quart(h)], r_fin.at[way, h],
                partner_zp if right else partner_zm,
            )

    if STEPS > 5:
        def spread(slot, ya):
            @when("odd")
            def _():
                give_b(slot, ya)

            @when("even")
            def _():
                free_b(slot, ya)

        def pass_on(slot, ya):
            @when("even")
            def _():
                pass_b(slot, ya)

        def hop_a(way, ya, target):
            landed(ra_one.at[way], r_a1.at[way])
            for q in range(2):
                add(ya * 2 + q, way, ra_one[way, q])
            send("all", stage_two(ya, way), ra_two.at[way, 1], r_a2.at[way, 1], target)

        def r1():
            send("all", stage_two(y_far, 0), ra_one.at[0], r_a1.at[0], up)
            send("all", stage_two(y_far, 1), ra_one.at[1], r_a1.at[1], dn)

        def m0():
            far = (z + 4) % 8
            for way, right, left in ((0, zp, zp_sibling), (1, zm, zm_sibling)):
                for core, target in ((c, right), (1 - c, left)):
                    image_send[far, core, quart(way)] = image_part[far, core, quart(way)].astype(bf16)
                    send(
                        "all", image_send.at[far, core, quart(way)], image_first.at[way, c], r_i0.at[way, c], target
                    )

        def m1_free():
            add_near_far()
            add_sibling(p_up)
            add_sibling(p_dn)
            ring_send(1, 1, True)
            ring_send(1, 0, False)

        def m1():
            ring_send(1, 0, True)
            ring_send(1, 1, False)

        def far_b():
            @when("odd")
            def _():
                take_b(0, y_far)
                send("odd", stage(y_far * 2 + xh, 2), rb_one.at[0], r_b1.at[0], up)
                send("odd", stage(y_far * 2 + xh, 3), rb_one.at[1], r_b1.at[1], dn)

        def free_a(way, ya, target):
            send("all", stage_two(ya, 1 - way), ra_two.at[way, 0], r_a2.at[way, 0], target)

        def m2():
            for h in (1, 0):
                ring_send(2, h, True)
                ring_send(2, 1 - h, False)

        T = lambda ya, slot: (text_block(ya), spread(slot, ya))
        I = image_block
        def rest():
            for p in (p_up, p_dn, p_own):
                weigh(p)

        lane = lax.broadcasted_iota(jnp.int32, (8, TOK), 1)

        def scalars():
            log_img = total(jnp.log(z_img))
            log_txt = total(jnp.log(z_txt))
            t_img = total(e_sums[...] / z_img)
            t_acc = e_row[0] * columns[0]
            for k in range(1, 8):
                t_acc = t_acc + e_row[k] * columns[k]
            t_txt = 2.0 * total(t_acc)
            hit = hits[...]
            found = hit > 0.0
            matched = total(jnp.where(found, jnp.log(jnp.where(found, hit, 1.0)) + scale, 0.0))
            scal_send[0] = jnp.where(
                lane == 0, log_txt,
                jnp.where(lane == 1, t_img, jnp.where(lane == 2, t_txt, jnp.where(lane == 3, matched, 0.0))),
            )
            for peer in line_peers:
                send("all", scal_send.at[0], scal_z.at[line_rank], r_sz.at[0], peer)
            scal_z[line_rank] = scal_send[0]
            return log_img

        def second_step(log_img):
            landed(scal_z.at[0:15], r_sz.at[0])
            line_sum = jnp.sum(scal_z[...], axis=0)
            scal_send[1] = jnp.where(lane == 4, log_img, line_sum)
            for peer in plane_peers:
                send("all", scal_send.at[1], scal_p.at[plane_rank], r_sp.at[0], peer)
            scal_p[plane_rank] = scal_send[1]
            return line_sum

        S1, S2 = scalars, second_step
        if ORDER == 1:
            I(p_far, False); m0(); swap_near_far(); rest(); T(y_far, 0); r1(); log_img = S1(); I(p_up); I(p_dn); T(y_dn, 1); m1_free()
            free_a(1, y_dn, dn); T(y_up, 2); free_a(0, y_up, up); m1(); pass_on(0, y_far); hop_a(0, y_up, up); hop_a(1, y_dn, dn)
            T(y, 3); pass_on(1, y_dn); pass_on(2, y_up); line_sum = S2(log_img); I(p_own); far_b(); pass_on(3, y); m2()
        if ORDER == 2:
            rest(); T(y_far, 0); r1(); I(p_far, False); m0(); swap_near_far(); log_img = S1(); I(p_up); T(y_dn, 1); I(p_dn); m1_free()
            free_a(1, y_dn, dn); T(y_up, 2); free_a(0, y_up, up); pass_on(0, y_far); m1(); hop_a(0, y_up, up); hop_a(1, y_dn, dn)
            T(y, 3); pass_on(1, y_dn); line_sum = S2(log_img); pass_on(2, y_up); I(p_own); far_b(); pass_on(3, y); m2()
        if ORDER == 3:
            I(p_far, False); m0(); swap_near_far(); rest(); T(y_far, 0); r1(); T(y_dn, 1); log_img = S1(); I(p_up); I(p_dn); m1_free()
            T(y_up, 2); pass_on(0, y_far); m1(); free_a(1, y_dn, dn); free_a(0, y_up, up); hop_a(0, y_up, up); hop_a(1, y_dn, dn)
            T(y, 3); pass_on(1, y_dn); pass_on(2, y_up); line_sum = S2(log_img); far_b(); I(p_own); pass_on(3, y); m2()
        if ORDER == 4:
            I(p_far, False); m0(); swap_near_far(); rest(); T(y_far, 0); r1(); I(p_up); I(p_dn); T(y_dn, 1); m1_free(); T(y_up, 2)
            log_img = S1(); pass_on(0, y_far); m1(); hop_a(0, y_up, up); hop_a(1, y_dn, dn); free_a(1, y_dn, dn); free_a(0, y_up, up)
            T(y, 3); pass_on(1, y_dn); pass_on(2, y_up); I(p_own); far_b(); pass_on(3, y); line_sum = S2(log_img); m2()

        add_sibling(p_own)

        @when("odd")
        def _():
            fin_send[...] = image_part[z, c].astype(bf16)
            send("odd", fin_send, fin_recv.at[2], r_fin.at[2, 0], partner)

        for part in range(2):
            for way in range(2):
                landed(ra_two.at[way, part], r_a2.at[way, part])
                for q in range(2):
                    add(y * 2 + q, way if part else 1 - way, ra_two[way, part, q])

        @when("odd")
        def _():
            for k in range(2):
                send("odd", stage(y * 2 + xo, k), ra_x.at[xh], r_ax.at[xh], across[k])
            take_b(1, y_dn)
            take_b(2, y_up)
            send("odd", stage(y_up * 2 + xh, 3), rb_two.at[0, 0], r_b2.at[0, 0], up)
            send("odd", stage(y_dn * 2 + xh, 2), rb_two.at[1, 0], r_b2.at[1, 0], dn)
            for way, ya, target in ((0, y_up, up), (1, y_dn, dn)):
                landed(rb_one.at[way], r_b1.at[way])
                add(ya * 2 + xh, 2 + way, rb_one[way])
                send("odd", stage(ya * 2 + xh, 2 + way), rb_two.at[way, 1], r_b2.at[way, 1], target)

        @when("even")
        def _():
            for q in range(2):
                send("even", stage(y * 2 + q, xo), ra_fin.at[xh, 0], r_af.at[xh, 0], across[q])

        for h in (1, 0):
            ring_send(3, h, True)
            ring_send(3, 1 - h, False)

        @when("even")
        def _():
            for q in range(2):
                landed(ra_x.at[1 - q], r_ax.at[1 - q])
                add(y * 2 + q, xh, ra_x[1 - q])
                send("even", stage(y * 2 + q, xh), ra_fin.at[xh, 1], r_af.at[xh, 1], across[q])

        def finish(part, grads):
            unit32, lengths = normal(part)
            grads = scale * grads
            inner = jnp.sum(unit32 * grads, axis=1, keepdims=True)
            result = (grads - unit32 * inner) / lengths
            if OUTF:
                out_ref[part] = result
            else:
                out_ref[0, part] = result.astype(bf16)

        @when("odd")
        def _():
            take_b(3, y)

        @when("odd")
        def _():
            for part in range(2):
                for way in range(2):
                    landed(rb_two.at[way, part], r_b2.at[way, part])
                    add(me, 2 + (way if part else 1 - way), rb_two[way, part])
            finish(upper, text_part[me, upper])
            for part in range(2):
                for e in range(2):
                    landed(ra_fin.at[e, part], r_af.at[e, part])
                    add(me, e if part else 1 - e, ra_fin[e, part])
            finish(lower, text_part[me, lower])

        @when("even")
        def _():
            for h in range(2):
                landed(image_right.at[3, quart(h)], r_ir.at[3, h])
                landed(image_left.at[3, quart(h)], r_il.at[3, h])
            finish(lower, image_part[z, c] + image_right[3].astype(f32) + image_left[3].astype(f32))
            landed(fin_recv.at[2], r_fin.at[2, 0])
            for h in range(2):
                landed(fin_recv.at[0, quart(h)], r_fin.at[0, h])
                landed(fin_recv.at[1, quart(h)], r_fin.at[1, h])
            finish(
                upper,
                fin_recv[0].astype(f32) + fin_recv[1].astype(f32) + fin_recv[2].astype(f32),
            )

        landed(scal_p.at[0:15], r_sp.at[0])
        all_sum = jnp.sum(scal_p[...], axis=0)

        def pick(x, k):
            return jnp.sum(jnp.where(lane[0:1] == k, x[0:1], 0.0))

        log_all = jnp.where(odd, pick(line_sum, 0), pick(all_sum, 4))
        t_all = jnp.where(odd, pick(all_sum, 2), pick(all_sum, 1))
        p_all = pick(all_sum, 3)
        loss_ref[0] = (scale * TOKENS + log_all - p_all) * (1.0 / (2 * TOKENS))
        sgrad_ref[0] = (t_all - p_all) / scale * (1.0 / (2 * TOKENS))

    for name in pending:
        if pending[name]:
            @when(name)
            def _():
                drain(name)


def body(embeddings, pair, logit_scale):
    vmem = pl.BlockSpec(memory_space=pltpu.VMEM)
    smem = pl.BlockSpec(memory_space=pltpu.SMEM)
    dma = pltpu.SemaphoreType.DMA
    scratch = [
        ((TOK, D), bf16),
        ((HALF, D), bf16),
        ((8, 2, HALF, D), bf16),
        ((8, TOK, D), bf16),
        ((16, TOK), f32),
        ((8, TOK, WIDE), f32),
        ((8, TOK, WIDE), bf16),
        ((8, TOK, D), f32),
        ((8, TOK, D), bf16),
        ((2, 2, QUART, D), bf16),
        ((2, 2, 2, QUART, D), bf16),
        ((2, QUART, D), bf16),
        ((2, 2, QUART, D), bf16),
        ((4, 2, 2, QUART, D), bf16),
        ((4, 2, QUART, D), bf16),
        ((2, QUART, D), bf16),
        ((2, 2, QUART, D), bf16),
        ((8, 2, HALF, D), f32),
        ((8, 2, HALF, D), bf16),
        ((8, HALF, D), bf16),
        ((4, HALF, D), bf16),
        ((4, HALF, D), bf16),
        ((2, 2, QUART, D), bf16),
        ((8, TOK, TOK), f32),
        ((8, TOK, TOK), f32),
        ((8, TOK, TOK), f32),
        ((8, TOK), jnp.int32),
        ((8, TOK), f32),
        ((4, 8, TOK), f32),
        ((16, 16, TOK), f32),
        ((16, 8, TOK), f32),
        ((8, TOK), f32),
        ((2, 8, TOK), f32),
        ((16, 8, TOK), f32),
        ((16, 8, TOK), f32),
        ((HALF, D), bf16),
        ((3, HALF, D), bf16),
    ]
    sems = [
        (1,), (SENDS,), (8, 4), (8, WAVES), (8,), (WAVES,), (1,), (1,), (1,), (1,),
        (2,), (2, 2), (2,), (2, 2), (4, 2, 2), (4, 2), (2,), (2, 2), (4,), (4, 2), (4, 2), (3, 2), (WAVES,), (2, 2),
    ]
    grads, loss, scale_grad = pl.pallas_call(
        kernel,
        out_shape=(
            jax.ShapeDtypeStruct((TOK, D), f32) if OUTF else jax.ShapeDtypeStruct((1, TOK, D), bf16),
            jax.ShapeDtypeStruct((1,), f32),
            jax.ShapeDtypeStruct((1,), f32),
        ),
        in_specs=[smem, pl.BlockSpec(memory_space=pl.ANY), vmem],
        out_specs=(vmem, smem, smem),
        scratch_shapes=[pltpu.VMEM(shape, dtype) for shape, dtype in scratch] + [dma(shape) for shape in sems],
        compiler_params=pltpu.CompilerParams(
            collective_id=0, has_side_effects=True, vmem_limit_bytes=56 * 2 ** 20
        ),
        cost_estimate=pl.CostEstimate(flops=6 * WIDE * WIDE * D, bytes_accessed=2 ** 20, transcendentals=2 ** 20),
        name="contrastive",
    )(
        logit_scale.astype(f32).reshape(1),
        embeddings,
        pair.reshape(1, TOK),
    )
    return (grads.astype(bf16)[None] if OUTF else grads), loss, scale_grad


def solution(mesh):
    placed = (P("tower", "blk", None), P("blk"), P())
    return jax.shard_map(
        body,
        mesh=mesh,
        in_specs=placed,
        out_specs=(P("tower", "blk", None), P("tower"), P("tower")),
        check_vma=False,
    )
```

```python
import jax
import jax.numpy as jnp
from jax import lax
from jax.experimental import pallas as pl
from jax.experimental.pallas import tpu as pltpu
from jax.sharding import PartitionSpec as P

eps = 1e-06
TOK = 128
D = 896
TOKENS = 16384
NY, NXH, NZ, NC = 4, 2, 8, 2
HALF, QUART = TOK // 2, TOK // 4
WIDE = 8 * TOK
f32 = jnp.float32
bf16 = jnp.bfloat16
MESH = pl.DeviceIdType.MESH
STEPS = 9
WAVES = 2
DIRECT = 0
DRAINS = 0
ORDER = 4
HOP3 = 1
XF = 1
OUTF = 0
SCAL = 0
SCAL2 = 1
SENDS = 30


def device(t, y, xh, z, c):
    return (t, ((y * NXH + xh) * NZ + z) * NC + c)


def kernel(
    scale_ref, emb_hbm, pair_ref,
    out_ref, loss_ref, sgrad_ref,
    emb_ref, unit_ref, length_ref, own, images, texts, z_msg, exps, weights,
    text_part, text_send, ra_one, ra_two, ra_x, ra_fin, rb_odd, rb_even, rb_one, rb_two,
    image_part, image_send, image_sib, image_right, image_left, image_first,
    z_row, e_row, columns, pair_rows, hits, stat_send, z_img_all, z_txt_all, e_sums, scal_send, scal_z, scal_p, fin_send, fin_recv,
    s_in, s_all, r_txt, r_img, r_sib, r_x, r_zi, r_zt, r_sz, r_sp,
    r_a1, r_a2, r_ax, r_af, r_bo, r_be, r_b1, r_b2, r_is, r_ir, r_il, r_fin, r_far, r_i0,
):
    t = lax.axis_index("tower")
    b = lax.axis_index("blk")
    c = b % 2
    z = (b // 2) % 8
    xh = (b // 16) % 2
    y = b // 32
    odd = t == 1
    even = t == 0
    line_rank = z * 2 + c
    plane_rank = (t * 4 + y) * 2 + xh
    me = y * 2 + xh
    scale = scale_ref[0]
    y_up, y_dn, y_far = (y + 1) % 4, (y + 3) % 4, (y + 2) % 4
    xo = 1 - xh

    conds = {"all": None, "odd": odd, "even": even}
    pending = {name: {} for name in conds}
    count = [0]

    def when(name):
        if name == "all":
            return lambda fn: fn()
        return pl.when(conds[name])

    def send(name, src, dst, rsem, target, batch=""):
        groups = pending[name].setdefault((src.shape, batch), [])
        if not groups or groups[-1][1] == (4 if len(src.shape) == 3 else 15 if src.shape[1] == TOK else 8):
            groups.append([count[0], 0])
            count[0] += 1
        groups[-1][1] += 1
        pltpu.make_async_remote_copy(
            src_ref=src, dst_ref=dst, send_sem=s_all.at[groups[-1][0]], recv_sem=rsem,
            device_id=target, device_id_type=MESH,
        ).start()

    def drain(name, batch=None):
        for key in [k for k in pending[name] if batch is None or k[1] == batch]:
            shape = key[0]
            for slot, copies in pending[name].pop(key):
                if len(shape) == 3:
                    like = texts.at[0:2 * copies, 0:shape[1]]
                elif shape == (16, TOK):
                    like = z_img_all.at[0:copies]
                elif shape == (8, TOK):
                    like = z_txt_all.at[0:copies]
                else:
                    like = texts.at[0:copies, 0:shape[0]]
                pltpu.make_async_copy(like, like, s_all.at[slot]).wait()

    def landed(dst, rsem):
        pltpu.make_async_copy(dst, dst, rsem).wait()

    up = device(t, y_up, xh, z, c)
    dn = device(t, y_dn, xh, z, c)
    zp = device(t, y, xh, (z + 1) % 8, c)
    zm = device(t, y, xh, (z + 7) % 8, c)
    sibling = device(t, y, xh, z, 1 - c)
    zp_sibling = device(t, y, xh, (z + 1) % 8, 1 - c)
    zm_sibling = device(t, y, xh, (z + 7) % 8, 1 - c)
    across = [device(1 - t, y, 0, z, c), device(1 - t, y, 1, z, c)]
    partner = device(1 - t, y, xh, z, c)
    partner_zp = device(1 - t, y, xh, (z + 1) % 8, c)
    partner_zm = device(1 - t, y, xh, (z + 7) % 8, c)
    line_peers = [
        device(t, y, xh, (z + dz) % 8, (c + dc) % 2)
        for dz in (4, 3, 5, 2, 6, 1, 7, 0) for dc in (0, 1) if dz or dc
    ]
    plane_peers = [
        device((t + dt) % 2, (y + dy) % 4, (xh + dx) % 2, z, c)
        for dy in (2, 1, 3, 0) for dx in (1, 0) for dt in (0, 1) if dy or dx or dt
    ]

    fetch = pltpu.make_async_copy(emb_hbm.at[0], emb_ref, s_in.at[0])
    fetch.start()
    barrier = pltpu.get_barrier_semaphore()
    for peer in (up, dn, zp, zm, sibling, across[0], across[1], partner_zp, partner_zm):
        pl.semaphore_signal(barrier, inc=1, device_id=peer, device_id_type=MESH)
    fetch.wait()

    def normal(part):
        wide = emb_ref[part].astype(f32)
        lengths = jnp.sqrt(jnp.sum(wide * wide, axis=1, keepdims=True) + eps)
        unit32 = wide / lengths
        unit_ref[part] = unit32
        length_ref[part] = lengths
        return unit32.astype(bf16)

    lower, upper = slice(0, HALF), slice(HALF, TOK)
    unit_low = normal(lower)
    unit_high = normal(upper)

    @when("odd")
    def _():
        texts[me, lower] = unit_low
        texts[me, upper] = unit_high

    @when("even")
    def _():
        images[z, c] = unit_low
        own[...] = unit_high

    z_msg[8:16, :] = jnp.broadcast_to(pair_ref[...], (8, TOK)).astype(f32)
    pl.semaphore_wait(barrier, 9)

    def rows(index, quarter):
        return texts.at[index, pl.ds(quarter * QUART, QUART)]

    def tsend(name, index, quarter, target, batch=""):
        send(name, rows(index, quarter), rows(index, quarter), r_txt.at[index, quarter], target, batch)

    def twait(index, quarter):
        landed(rows(index, quarter), r_txt.at[index, quarter])

    size = HALF // WAVES

    def piece(slot, w):
        return images.at[slot, c, pl.ds(w * size, size)]

    def isend(name, slot, w, target):
        send(name, piece(slot, w), piece(slot, w), r_img.at[slot, w], target)

    def iwait(slot, w):
        landed(piece(slot, w), r_img.at[slot, w])

    def to_sibling(name, slot):
        send(name, images.at[slot, c], images.at[slot, c], r_sib.at[slot], sibling)

    def image_hop(name, k):
        left, right = (z + 8 - k) % 8, (z + k) % 8
        for w in range(WAVES):
            iwait(left, w)
            if k < 3 or w < WAVES // 2:
                isend(name, left, w, zp)
            if k == 3 and w < WAVES // 2:
                send(name, piece(left, w), piece(left, w), r_far.at[w], zp_sibling)
            iwait(right, w)
            if k < 3 or w >= WAVES // 2:
                isend(name, right, w, zm)
            if k == 3 and w >= WAVES // 2:
                send(name, piece(right, w), piece(right, w), r_far.at[w], zm_sibling)
        to_sibling(name, left)
        to_sibling(name, right)

    def image_last(name):
        far = (z + 4) % 8
        for w in range(WAVES):
            iwait(far, w)
            landed(images.at[far, 1 - c, pl.ds(w * size, size)], r_far.at[w])

    def siblings(p):
        for h in range(2):
            landed(images.at[2 * p + h, 1 - c], r_sib.at[2 * p + h])

    half_z = z // 2
    p_far, p_up, p_dn, p_own = [(half_z + k) % 4 for k in (2, 1, 3, 0)]

    if STEPS > 1:
        @when("even")
        def _():
            n = "even"
            first, second = device(t, (y + 1 + 2 * xh) % 4, xh, z, c), device(t, (y + 1 + 2 * xo) % 4, xh, z, c)

            def mine(w):
                return own.at[pl.ds(w * size, size)]

            for w in range(WAVES if XF else 0):
                send(n, mine(w), piece(z, w), r_x.at[w], partner)
            for w in range(WAVES):
                isend(n, z, w, zp)
                isend(n, z, w, zm)
                if XF:
                    continue
                if DIRECT:
                    send(n, mine(w), piece(z, w), r_img.at[z, w], partner_zp)
                    send(n, mine(w), piece(z, w), r_img.at[z, w], partner_zm)
                else:
                    send(n, mine(w), piece(z, w), r_x.at[w], partner)
            to_sibling(n, z)
            image_hop(n, 1)
            for q in range(2):
                index = y * 2 + q
                twait(index, xh)
                tsend(n, index, xh, across[1 - q])
                tsend(n, index, xh, first)
            for q in range(2):
                index = y * 2 + q
                twait(index, xo)
                tsend(n, index, xo, second)
            for q in range(2):
                index = y * 2 + q
                twait(index, 2 + xh)
                tsend(n, index, 2 + xh, across[1 - q])
            for q in range(2):
                index = y * 2 + q
                tsend(n, index, xh, second)
                tsend(n, index, xo, first)
            ya, yb = (y + 3 + 2 * xh) % 4, (y + 1 + 2 * xh) % 4
            for q in range(2):
                index = ya * 2 + q
                twait(index, 2 + xh)
                tsend(n, index, 2 + xh, across[1 - q])
            image_hop(n, 2)
            for q in range(2):
                index = yb * 2 + q
                twait(index, 2 + xh)
                tsend(n, index, 2 + xh, across[1 - q])
            for w in range(WAVES if DIRECT else 0):
                send(n, mine(w), piece(z, w), r_x.at[w], partner)
            for q in range(2):
                twait(y_dn * 2 + q, 0)
                tsend(n, y_dn * 2 + q, 0, up)
                twait(y_up * 2 + q, 1)
                tsend(n, y_up * 2 + q, 1, dn)
            for q in range(2):
                index = y_far * 2 + q
                twait(index, 2 + xh)
                tsend(n, index, 2 + xh, across[1 - q])
            image_hop(n, 3)
            for q in range(2):
                twait(y_dn * 2 + q, 1)
                twait(y_up * 2 + q, 0)
                for k in range(2):
                    twait(y_far * 2 + q, k)
                for ya in (y, y_dn, y_up, y_far):
                    twait(ya * 2 + q, 2 + xo)

        @when("odd")
        def _():
            n = "odd"
            mine, below, above, far = me, y_dn * 2 + xh, y_up * 2 + xh, y_far * 2 + xh
            other = y * 2 + xo

            def relayed(index, k):
                tsend(n, index, 2 + k, across[k])

            def kept(index):
                for e in range(2):
                    tsend(n, index, 3 - e, across[e])

            for e in range(2):
                tsend(n, mine, e, across[e], "s")
            tsend(n, mine, 2, up, "s")
            tsend(n, mine, 3, dn, "s")
            if DRAINS > 0:
                drain(n, "s")
            for e in range(2):
                tsend(n, mine, 1 - e, across[e], "s")
            tsend(n, mine, 3, up, "s")
            tsend(n, mine, 2, dn, "s")
            if DRAINS > 1:
                drain(n, "s")
            if not DIRECT:
                for w in range(WAVES):
                    landed(piece(z, w), r_x.at[w])
                    isend(n, z, w, zp)
                    isend(n, z, w, zm)
                to_sibling(n, z)
            for e in range(2):
                relayed(mine, e)
            tsend(n, mine, 0, up)
            tsend(n, mine, 1, dn)
            twait(below, 2)
            tsend(n, below, 2, up)
            relayed(below, 0)
            twait(above, 3)
            tsend(n, above, 3, dn)
            relayed(above, 1)
            tsend(n, mine, 1, up)
            tsend(n, mine, 0, dn)
            twait(below, 3)
            relayed(below, 1)
            twait(above, 2)
            relayed(above, 0)
            image_hop(n, 1)
            twait(below, 0)
            tsend(n, below, 0, up)
            twait(above, 1)
            tsend(n, above, 1, dn)
            twait(far, 2)
            relayed(far, 0)
            twait(far, 3)
            relayed(far, 1)
            twait(other, 0)
            tsend(n, other, 0, up)
            twait(other, 1)
            tsend(n, other, 1, dn)
            kept(mine)
            tsend(n, other, 1, up)
            tsend(n, other, 0, dn)
            kept(below)
            kept(above)
            image_hop(n, 2)
            kept(far)
            twait(y_dn * 2 + xo, 0)
            tsend(n, y_dn * 2 + xo, 0, up)
            twait(y_up * 2 + xo, 1)
            tsend(n, y_up * 2 + xo, 1, dn)
            if HOP3:
                image_hop(n, 3)
            for q in (xh, xo):
                twait(y_dn * 2 + q, 1)
                twait(y_up * 2 + q, 0)
                for k in range(2):
                    twait(y_far * 2 + q, k)
            for ya in (y, y_dn, y_up, y_far):
                for k in range(2):
                    twait(ya * 2 + xo, 2 + k)
            if DIRECT:
                for w in range(WAVES):
                    landed(piece(z, w), r_x.at[w])
                to_sibling(n, z)

        siblings(p_own)

    def first_id(index):
        return ((index * 8 + z) * 2 + c) * TOK

    sub_ids = lax.broadcasted_iota(jnp.int32, (TOK, 1), 0)

    def total(x):
        return jnp.sum(jnp.sum(x, axis=0, keepdims=True), axis=1, keepdims=True)

    if STEPS > 2:
        all_texts = texts[...].reshape(WIDE, D)

        def stats(p, first):
            two = images[pl.ds(2 * p, 2)].reshape(2 * TOK, D)
            dots = lax.dot_general(all_texts, two, (((1,), (1,)), ((), ())), preferred_element_type=f32)
            scores = scale * dots
            ex = jnp.exp(scores - scale)
            exps[:, :, pl.ds(pl.multiple_of(p * 2 * TOK, 2 * TOK), 2 * TOK)] = ex.reshape(8, TOK, 2 * TOK)
            es = ex * scores
            z_sum = jnp.sum(ex, axis=0, keepdims=True)
            e_sum = jnp.sum(es, axis=0, keepdims=True)
            for h in range(2):
                part = slice(h * TOK, (h + 1) * TOK)
                z_msg[pl.ds(2 * p + h, 1), :] = z_sum[:, part]
                e_sums[pl.ds(2 * p + h, 1), :] = e_sum[:, part]
            zr = (ex[:, 0:TOK] + ex[:, TOK:]).reshape(8, TOK, TOK)
            er = (es[:, 0:TOK] + es[:, TOK:]).reshape(8, TOK, TOK)
            z_row[...] = zr if first else z_row[...] + zr
            e_row[...] = er if first else e_row[...] + er

        stats(p_own, True)

        if not HOP3:
            @when("odd")
            def _():
                image_hop("odd", 3)

        for p in (p_up, p_dn):
            siblings(p)
            stats(p, False)

        @when("even")
        def _():
            image_last("even")

        @when("odd")
        def _():
            image_last("odd")

        near_far = (z + 3 + 2 * ((z + 1) % 2)) % 8
        landed(images.at[near_far, 1 - c], r_sib.at[near_far])
        stats(p_far, False)
        for peer in line_peers if STEPS > 3 else ():
            send("all", z_msg, z_img_all.at[line_rank], r_zi.at[0], peer)
        for k in range(8):
            stat_send[1, k:k + 1, :] = jnp.sum(z_row[k].T, axis=0, keepdims=True)
        all_images = images[...].reshape(WIDE, D)

    if STEPS > 3:
        for peer in plane_peers:
            send("all", stat_send.at[1], z_txt_all.at[plane_rank], r_zt.at[0], peer)
        z_img_all[line_rank] = z_msg[...]
        z_txt_all[plane_rank] = stat_send[1]
        landed(z_img_all.at[0:15], r_zi.at[0])

        def own_half(k, core):
            line = z_img_all[2 * k + core, 8:9]
            return jnp.where(odd, line[:, HALF:TOK], line[:, 0:HALF]).astype(jnp.int32)

        for k in range(8):
            pair_rows[k:k + 1, :] = jnp.concatenate([own_half(k, core) for core in range(2)], axis=1)
        landed(z_txt_all.at[0:15], r_zt.at[0])
        z_img = jnp.sum(z_img_all[:, 0:8], axis=0)
        z_txt = jnp.sum(z_txt_all[...], axis=0)

    if STEPS > 4:
        stat_send[3] = 0.5 / z_img
        stat_send[2] = 0.5 / z_txt
        for k in range(8):
            columns[k] = jnp.broadcast_to(stat_send[2, k:k + 1, :], (TOK, TOK)).T

        def weigh(p):
            lanes = pl.ds(pl.multiple_of(p * 2 * TOK, 2 * TOK), 2 * TOK)
            img = jnp.concatenate([stat_send[3, pl.ds(2 * p + h, 1), :] for h in range(2)], axis=1)
            partners = jnp.concatenate([pair_rows[pl.ds(2 * p + h, 1), :] for h in range(2)], axis=1)

            def step(index, carry):
                column = columns[index]
                ids = first_id(index) + sub_ids
                match = partners == ids
                ex = exps[index, :, lanes]
                value = ex * (img + jnp.concatenate([column, column], axis=1))
                weights[index, :, lanes] = (value - jnp.where(match, 1.0, 0.0)).astype(bf16)
                return carry + jnp.sum(jnp.where(match, ex, 0.0), axis=0, keepdims=True)

            hit = lax.fori_loop(0, 8, step, jnp.zeros((1, 2 * TOK), f32))
            for h in range(2):
                hits[pl.ds(2 * p + h, 1), :] = hit[:, h * TOK:(h + 1) * TOK]

        weigh(p_far)

    def text_block(ya):
        pair_of = pl.ds(2 * ya, 2)
        two = weights[pair_of].reshape(2 * TOK, WIDE)
        part = jnp.dot(two, all_images, preferred_element_type=f32)
        text_part[pair_of] = part.reshape(2, TOK, D)

    def quart(k):
        return pl.ds(k * QUART, QUART)

    def stage(index, k):
        text_send[index, quart(k)] = text_part[index, quart(k)].astype(bf16)
        return text_send.at[index, quart(k)]

    def stage_two(ya, k):
        for q in range(2):
            stage(ya * 2 + q, k)
        return text_send.at[pl.ds(2 * ya, 2), quart(k)]

    def add(index, k, value):
        text_part[index, quart(k)] = text_part[index, quart(k)] + value.astype(f32)

    def give_b(slot, ya):
        for k in range(2):
            send("odd", stage(ya * 2 + xo, 2 + k), rb_even.at[slot, xh], r_be.at[slot, xh], across[k])

    def free_b(slot, ya):
        for q in range(2):
            send("even", stage(ya * 2 + q, 2 + xo), rb_odd.at[slot, xh, 0], r_bo.at[slot, xh, 0], across[q])

    def pass_b(slot, ya):
        for q in range(2):
            index = ya * 2 + q
            landed(rb_even.at[slot, 1 - q], r_be.at[slot, 1 - q])
            add(index, 2 + xh, rb_even[slot, 1 - q])
            send("even", stage(index, 2 + xh), rb_odd.at[slot, xh, 1], r_bo.at[slot, xh, 1], across[q])

    def take_b(slot, ya):
        index = ya * 2 + xh
        for part in range(2):
            for e in range(2):
                landed(rb_odd.at[slot, e, part], r_bo.at[slot, e, part])
                add(index, 2 + (e if part else 1 - e), rb_odd[slot, e, part])

    def image_block(p, with_sibling=True):
        lanes = pl.ds(pl.multiple_of(p * 2 * TOK, 2 * TOK), 2 * TOK)
        part = lax.dot_general(
            weights[:, :, lanes].reshape(WIDE, 2 * TOK), texts[...].reshape(WIDE, D),
            (((0,), (0,)), ((), ())), preferred_element_type=f32,
        )
        both = pl.ds(2 * p, 2)
        image_part[both] = part.reshape(2, 2, HALF, D)
        if with_sibling:
            image_send[both, 1 - c] = image_part[both, 1 - c].astype(bf16)
            send("all", image_send.at[both, 1 - c], image_sib.at[both], r_is.at[p], sibling)

    def swap_near_far():
        image_send[near_far, 1 - c] = image_part[near_far, 1 - c].astype(bf16)
        send("all", image_send.at[near_far, 1 - c], image_sib.at[near_far], r_is.at[p_far], sibling)

    def add_near_far():
        landed(image_sib.at[near_far], r_is.at[p_far])
        image_part[near_far, c] = image_part[near_far, c] + image_sib[near_far].astype(f32)

    def add_sibling(p):
        both = pl.ds(2 * p, 2)
        landed(image_sib.at[both], r_is.at[p])
        image_part[both, c] = image_part[both, c] + image_sib[both].astype(f32)

    def source_of(slot, h):
        return image_send.at[slot, c, quart(h)]

    def ring_send(m, h, right):
        hops = 4 - m
        slot = (z + hops) % 8 if right else (z + 8 - hops) % 8
        into = image_right if right else image_left
        sem = r_ir if right else r_il
        value = image_part[slot, c, quart(h)]
        if m == 1 and h == (0 if right else 1):
            for core in range(2):
                landed(image_first.at[h, core], r_i0.at[h, core])
                value = value + image_first[h, core].astype(f32)
        if m > 1:
            landed(into.at[m - 1, quart(h)], sem.at[m - 1, h])
            value = value + into[m - 1, quart(h)].astype(f32)
        image_send[slot, c, quart(h)] = value.astype(bf16)
        if m < 3:
            send("all", source_of(slot, h), into.at[m, quart(h)], sem.at[m, h], zp if right else zm)
            return
        way = 0 if right else 1

        @when("even")
        def _():
            send("even", source_of(slot, h), into.at[m, quart(h)], sem.at[m, h], zp if right else zm)

        @when("odd")
        def _():
            send(
                "odd", source_of(slot, h), fin_recv.at[way, quart(h)], r_fin.at[way, h],
                partner_zp if right else partner_zm,
            )

    if STEPS > 5:
        def spread(slot, ya):
            @when("odd")
            def _():
                give_b(slot, ya)

            @when("even")
            def _():
                free_b(slot, ya)

        def pass_on(slot, ya):
            @when("even")
            def _():
                pass_b(slot, ya)

        def hop_a(way, ya, target):
            landed(ra_one.at[way], r_a1.at[way])
            for q in range(2):
                add(ya * 2 + q, way, ra_one[way, q])
            send("all", stage_two(ya, way), ra_two.at[way, 1], r_a2.at[way, 1], target)

        def r1():
            send("all", stage_two(y_far, 0), ra_one.at[0], r_a1.at[0], up)
            send("all", stage_two(y_far, 1), ra_one.at[1], r_a1.at[1], dn)

        def m0():
            far = (z + 4) % 8
            for way, right, left in ((0, zp, zp_sibling), (1, zm, zm_sibling)):
                for core, target in ((c, right), (1 - c, left)):
                    image_send[far, core, quart(way)] = image_part[far, core, quart(way)].astype(bf16)
                    send(
                        "all", image_send.at[far, core, quart(way)], image_first.at[way, c], r_i0.at[way, c], target
                    )

        def m1_free():
            add_near_far()
            add_sibling(p_up)
            add_sibling(p_dn)
            ring_send(1, 1, True)
            ring_send(1, 0, False)

        def m1():
            ring_send(1, 0, True)
            ring_send(1, 1, False)

        def far_b():
            @when("odd")
            def _():
                take_b(0, y_far)
                send("odd", stage(y_far * 2 + xh, 2), rb_one.at[0], r_b1.at[0], up)
                send("odd", stage(y_far * 2 + xh, 3), rb_one.at[1], r_b1.at[1], dn)

        def free_a(way, ya, target):
            send("all", stage_two(ya, 1 - way), ra_two.at[way, 0], r_a2.at[way, 0], target)

        def m2():
            for h in (1, 0):
                ring_send(2, h, True)
                ring_send(2, 1 - h, False)

        T = lambda ya, slot: (text_block(ya), spread(slot, ya))
        I = image_block
        def rest():
            for p in (p_up, p_dn, p_own):
                weigh(p)

        lane = lax.broadcasted_iota(jnp.int32, (8, TOK), 1)

        def scalars():
            log_img = total(jnp.log(z_img))
            log_txt = total(jnp.log(z_txt))
            t_img = total(e_sums[...] / z_img)
            t_acc = e_row[0] * columns[0]
            for k in range(1, 8):
                t_acc = t_acc + e_row[k] * columns[k]
            t_txt = 2.0 * total(t_acc)
            hit = hits[...]
            found = hit > 0.0
            matched = total(jnp.where(found, jnp.log(jnp.where(found, hit, 1.0)) + scale, 0.0))
            scal_send[0] = jnp.where(
                lane == 0, log_txt,
                jnp.where(lane == 1, t_img, jnp.where(lane == 2, t_txt, jnp.where(lane == 3, matched, 0.0))),
            )
            for peer in line_peers:
                send("all", scal_send.at[0], scal_z.at[line_rank], r_sz.at[0], peer)
            scal_z[line_rank] = scal_send[0]
            return log_img

        def second_step(log_img):
            landed(scal_z.at[0:15], r_sz.at[0])
            line_sum = jnp.sum(scal_z[...], axis=0)
            scal_send[1] = jnp.where(lane == 4, log_img, line_sum)
            for peer in plane_peers:
                send("all", scal_send.at[1], scal_p.at[plane_rank], r_sp.at[0], peer)
            scal_p[plane_rank] = scal_send[1]
            return line_sum

        S1, S2 = scalars, second_step
        if ORDER == 1:
            I(p_far, False); m0(); swap_near_far(); rest(); T(y_far, 0); r1(); log_img = S1(); I(p_up); I(p_dn); T(y_dn, 1); m1_free()
            free_a(1, y_dn, dn); T(y_up, 2); free_a(0, y_up, up); m1(); pass_on(0, y_far); hop_a(0, y_up, up); hop_a(1, y_dn, dn)
            T(y, 3); pass_on(1, y_dn); pass_on(2, y_up); line_sum = S2(log_img); I(p_own); far_b(); pass_on(3, y); m2()
        if ORDER == 2:
            rest(); T(y_far, 0); r1(); I(p_far, False); m0(); swap_near_far(); log_img = S1(); I(p_up); T(y_dn, 1); I(p_dn); m1_free()
            free_a(1, y_dn, dn); T(y_up, 2); free_a(0, y_up, up); pass_on(0, y_far); m1(); hop_a(0, y_up, up); hop_a(1, y_dn, dn)
            T(y, 3); pass_on(1, y_dn); line_sum = S2(log_img); pass_on(2, y_up); I(p_own); far_b(); pass_on(3, y); m2()
        if ORDER == 3:
            I(p_far, False); m0(); swap_near_far(); rest(); T(y_far, 0); r1(); T(y_dn, 1); log_img = S1(); I(p_up); I(p_dn); m1_free()
            T(y_up, 2); pass_on(0, y_far); m1(); free_a(1, y_dn, dn); free_a(0, y_up, up); hop_a(0, y_up, up); hop_a(1, y_dn, dn)
            T(y, 3); pass_on(1, y_dn); pass_on(2, y_up); line_sum = S2(log_img); far_b(); I(p_own); pass_on(3, y); m2()
        if ORDER == 4:
            I(p_far, False); m0(); swap_near_far(); rest(); T(y_far, 0); r1(); I(p_up); I(p_dn); T(y_dn, 1); m1_free(); T(y_up, 2)
            log_img = S1(); pass_on(0, y_far); m1(); hop_a(0, y_up, up); hop_a(1, y_dn, dn); free_a(1, y_dn, dn); free_a(0, y_up, up)
            T(y, 3); pass_on(1, y_dn); pass_on(2, y_up); I(p_own); far_b(); pass_on(3, y); line_sum = S2(log_img); m2()

        add_sibling(p_own)

        @when("odd")
        def _():
            fin_send[...] = image_part[z, c].astype(bf16)
            send("odd", fin_send, fin_recv.at[2], r_fin.at[2, 0], partner)

        for part in range(2):
            for way in range(2):
                landed(ra_two.at[way, part], r_a2.at[way, part])
                for q in range(2):
                    add(y * 2 + q, way if part else 1 - way, ra_two[way, part, q])

        @when("odd")
        def _():
            for k in range(2):
                send("odd", stage(y * 2 + xo, k), ra_x.at[xh], r_ax.at[xh], across[k])
            take_b(1, y_dn)
            take_b(2, y_up)
            send("odd", stage(y_up * 2 + xh, 3), rb_two.at[0, 0], r_b2.at[0, 0], up)
            send("odd", stage(y_dn * 2 + xh, 2), rb_two.at[1, 0], r_b2.at[1, 0], dn)
            for way, ya, target in ((0, y_up, up), (1, y_dn, dn)):
                landed(rb_one.at[way], r_b1.at[way])
                add(ya * 2 + xh, 2 + way, rb_one[way])
                send("odd", stage(ya * 2 + xh, 2 + way), rb_two.at[way, 1], r_b2.at[way, 1], target)

        @when("even")
        def _():
            for q in range(2):
                send("even", stage(y * 2 + q, xo), ra_fin.at[xh, 0], r_af.at[xh, 0], across[q])

        for h in (1, 0):
            ring_send(3, h, True)
            ring_send(3, 1 - h, False)

        @when("even")
        def _():
            for q in range(2):
                landed(ra_x.at[1 - q], r_ax.at[1 - q])
                add(y * 2 + q, xh, ra_x[1 - q])
                send("even", stage(y * 2 + q, xh), ra_fin.at[xh, 1], r_af.at[xh, 1], across[q])

        landed(scal_p.at[0:15], r_sp.at[0])
        all_sum = jnp.sum(scal_p[...], axis=0)

        def pick(x, k):
            return jnp.sum(jnp.where(lane[0:1] == k, x[0:1], 0.0))

        log_all = jnp.where(odd, pick(line_sum, 0), pick(all_sum, 4))
        t_all = jnp.where(odd, pick(all_sum, 2), pick(all_sum, 1))
        p_all = pick(all_sum, 3)
        loss_ref[0] = (scale * TOKENS + log_all - p_all) * (1.0 / (2 * TOKENS))
        sgrad_ref[0] = (t_all - p_all) / scale * (1.0 / (2 * TOKENS))

        def finish(part, grads):
            unit32, lengths = unit_ref[part], length_ref[part]
            grads = scale * grads
            inner = jnp.sum(unit32 * grads, axis=1, keepdims=True)
            result = (grads - unit32 * inner) / lengths
            if OUTF:
                out_ref[part] = result
            else:
                out_ref[0, part] = result.astype(bf16)

        @when("odd")
        def _():
            take_b(3, y)

        @when("odd")
        def _():
            for part in range(2):
                for way in range(2):
                    landed(rb_two.at[way, part], r_b2.at[way, part])
                    add(me, 2 + (way if part else 1 - way), rb_two[way, part])
            finish(upper, text_part[me, upper])
            for part in range(2):
                for e in range(2):
                    landed(ra_fin.at[e, part], r_af.at[e, part])
                    add(me, e if part else 1 - e, ra_fin[e, part])
            finish(lower, text_part[me, lower])

        @when("even")
        def _():
            for h in range(2):
                landed(image_right.at[3, quart(h)], r_ir.at[3, h])
                landed(image_left.at[3, quart(h)], r_il.at[3, h])
            finish(lower, image_part[z, c] + image_right[3].astype(f32) + image_left[3].astype(f32))
            landed(fin_recv.at[2], r_fin.at[2, 0])
            for h in range(2):
                landed(fin_recv.at[0, quart(h)], r_fin.at[0, h])
                landed(fin_recv.at[1, quart(h)], r_fin.at[1, h])
            finish(
                upper,
                fin_recv[0].astype(f32) + fin_recv[1].astype(f32) + fin_recv[2].astype(f32),
            )


    assert count[0] <= SENDS, count[0]
    for name in pending:
        if pending[name]:
            @when(name)
            def _():
                drain(name)


def body(embeddings, pair, logit_scale):
    vmem = pl.BlockSpec(memory_space=pltpu.VMEM)
    smem = pl.BlockSpec(memory_space=pltpu.SMEM)
    dma = pltpu.SemaphoreType.DMA
    scratch = [
        ((TOK, D), bf16),
        ((TOK, D), f32),
        ((TOK, 1), f32),
        ((HALF, D), bf16),
        ((8, 2, HALF, D), bf16),
        ((8, TOK, D), bf16),
        ((16, TOK), f32),
        ((8, TOK, WIDE), f32),
        ((8, TOK, WIDE), bf16),
        ((8, TOK, D), f32),
        ((8, TOK, D), bf16),
        ((2, 2, QUART, D), bf16),
        ((2, 2, 2, QUART, D), bf16),
        ((2, QUART, D), bf16),
        ((2, 2, QUART, D), bf16),
        ((4, 2, 2, QUART, D), bf16),
        ((4, 2, QUART, D), bf16),
        ((2, QUART, D), bf16),
        ((2, 2, QUART, D), bf16),
        ((8, 2, HALF, D), f32),
        ((8, 2, HALF, D), bf16),
        ((8, HALF, D), bf16),
        ((4, HALF, D), bf16),
        ((4, HALF, D), bf16),
        ((2, 2, QUART, D), bf16),
        ((8, TOK, TOK), f32),
        ((8, TOK, TOK), f32),
        ((8, TOK, TOK), f32),
        ((8, TOK), jnp.int32),
        ((8, TOK), f32),
        ((4, 8, TOK), f32),
        ((16, 16, TOK), f32),
        ((16, 8, TOK), f32),
        ((8, TOK), f32),
        ((2, 8, TOK), f32),
        ((16, 8, TOK), f32),
        ((16, 8, TOK), f32),
        ((HALF, D), bf16),
        ((3, HALF, D), bf16),
    ]
    sems = [
        (1,), (SENDS,), (8, 4), (8, WAVES), (8,), (WAVES,), (1,), (1,), (1,), (1,),
        (2,), (2, 2), (2,), (2, 2), (4, 2, 2), (4, 2), (2,), (2, 2), (4,), (4, 2), (4, 2), (3, 2), (WAVES,), (2, 2),
    ]
    grads, loss, scale_grad = pl.pallas_call(
        kernel,
        out_shape=(
            jax.ShapeDtypeStruct((TOK, D), f32) if OUTF else jax.ShapeDtypeStruct((1, TOK, D), bf16),
            jax.ShapeDtypeStruct((1,), f32),
            jax.ShapeDtypeStruct((1,), f32),
        ),
        in_specs=[smem, pl.BlockSpec(memory_space=pl.ANY), vmem],
        out_specs=(vmem, smem, smem),
        scratch_shapes=[pltpu.VMEM(shape, dtype) for shape, dtype in scratch] + [dma(shape) for shape in sems],
        compiler_params=pltpu.CompilerParams(
            collective_id=0, has_side_effects=True, vmem_limit_bytes=56 * 2 ** 20
        ),
        cost_estimate=pl.CostEstimate(flops=6 * WIDE * WIDE * D, bytes_accessed=2 ** 20, transcendentals=2 ** 20),
        name="contrastive",
    )(
        logit_scale.astype(f32).reshape(1),
        embeddings,
        pair.reshape(1, TOK),
    )
    return (grads.astype(bf16)[None] if OUTF else grads), loss, scale_grad


def solution(mesh):
    placed = (P("tower", "blk", None), P("blk"), P())
    return jax.shard_map(
        body,
        mesh=mesh,
        in_specs=placed,
        out_specs=(P("tower", "blk", None), P("tower"), P("tower")),
        check_vma=False,
    )
```

```python
import jax
import jax.numpy as jnp
from jax import lax
from jax.experimental import pallas as pl
from jax.experimental.pallas import tpu as pltpu
from jax.sharding import PartitionSpec as P

eps = 1e-06
TOK = 128
D = 896
TOKENS = 16384
NY, NXH, NZ, NC = 4, 2, 8, 2
HALF, QUART = TOK // 2, TOK // 4
WIDE = 8 * TOK
f32 = jnp.float32
bf16 = jnp.bfloat16
MESH = pl.DeviceIdType.MESH
STEPS = 9
WAVES = 2
SENDS = 30


def device(t, y, xh, z, c):
    return (t, ((y * NXH + xh) * NZ + z) * NC + c)


def kernel(
    scale_ref, emb_hbm, pair_ref,
    out_ref, loss_ref, sgrad_ref,
    emb_ref, unit_ref, length_ref, own, images, texts, z_msg, exps, weights,
    text_part, text_send, ra_one, ra_two, ra_x, ra_fin, rb_odd, rb_even, rb_one, rb_two,
    image_part, image_send, image_sib, image_right, image_left, image_first,
    z_row, e_row, columns, pair_rows, hits, stat_send, z_img_all, z_txt_all, e_sums, scal_send, scal_z, scal_p, fin_send, fin_recv,
    s_in, s_all, r_txt, r_img, r_sib, r_x, r_zi, r_zt, r_sz, r_sp,
    r_a1, r_a2, r_ax, r_af, r_bo, r_be, r_b1, r_b2, r_is, r_ir, r_il, r_fin, r_far, r_i0,
):
    t = lax.axis_index("tower")
    b = lax.axis_index("blk")
    c = b % 2
    z = (b // 2) % 8
    xh = (b // 16) % 2
    y = b // 32
    odd = t == 1
    even = t == 0
    line_rank = z * 2 + c
    plane_rank = (t * 4 + y) * 2 + xh
    me = y * 2 + xh
    scale = scale_ref[0]
    y_up, y_dn, y_far = (y + 1) % 4, (y + 3) % 4, (y + 2) % 4
    xo = 1 - xh

    conds = {"all": None, "odd": odd, "even": even}
    pending = {name: {} for name in conds}
    count = [0]

    def when(name):
        if name == "all":
            return lambda fn: fn()
        return pl.when(conds[name])

    def send(name, src, dst, rsem, target, batch=""):
        groups = pending[name].setdefault((src.shape, batch), [])
        if not groups or groups[-1][1] == (4 if len(src.shape) == 3 else 15 if src.shape[1] == TOK else 8):
            groups.append([count[0], 0])
            count[0] += 1
        groups[-1][1] += 1
        pltpu.make_async_remote_copy(
            src_ref=src, dst_ref=dst, send_sem=s_all.at[groups[-1][0]], recv_sem=rsem,
            device_id=target, device_id_type=MESH,
        ).start()

    def drain(name, batch=None):
        for key in [k for k in pending[name] if batch is None or k[1] == batch]:
            shape = key[0]
            for slot, copies in pending[name].pop(key):
                if len(shape) == 3:
                    like = texts.at[0:2 * copies, 0:shape[1]]
                elif shape == (16, TOK):
                    like = z_img_all.at[0:copies]
                elif shape == (8, TOK):
                    like = z_txt_all.at[0:copies]
                else:
                    like = texts.at[0:copies, 0:shape[0]]
                pltpu.make_async_copy(like, like, s_all.at[slot]).wait()

    def landed(dst, rsem):
        pltpu.make_async_copy(dst, dst, rsem).wait()

    up = device(t, y_up, xh, z, c)
    dn = device(t, y_dn, xh, z, c)
    zp = device(t, y, xh, (z + 1) % 8, c)
    zm = device(t, y, xh, (z + 7) % 8, c)
    sibling = device(t, y, xh, z, 1 - c)
    zp_sibling = device(t, y, xh, (z + 1) % 8, 1 - c)
    zm_sibling = device(t, y, xh, (z + 7) % 8, 1 - c)
    across = [device(1 - t, y, 0, z, c), device(1 - t, y, 1, z, c)]
    partner = device(1 - t, y, xh, z, c)
    partner_zp = device(1 - t, y, xh, (z + 1) % 8, c)
    partner_zm = device(1 - t, y, xh, (z + 7) % 8, c)
    line_peers = [
        device(t, y, xh, (z + dz) % 8, (c + dc) % 2)
        for dz in (4, 3, 5, 2, 6, 1, 7, 0) for dc in (0, 1) if dz or dc
    ]
    plane_peers = [
        device((t + dt) % 2, (y + dy) % 4, (xh + dx) % 2, z, c)
        for dy in (2, 1, 3, 0) for dx in (1, 0) for dt in (0, 1) if dy or dx or dt
    ]

    fetch = pltpu.make_async_copy(emb_hbm.at[0], emb_ref, s_in.at[0])
    fetch.start()
    barrier = pltpu.get_barrier_semaphore()
    for peer in (up, dn, zp, zm, sibling, across[0], across[1], partner_zp, partner_zm):
        pl.semaphore_signal(barrier, inc=1, device_id=peer, device_id_type=MESH)
    fetch.wait()

    def normal(part):
        wide = emb_ref[part].astype(f32)
        lengths = jnp.sqrt(jnp.sum(wide * wide, axis=1, keepdims=True) + eps)
        unit32 = wide / lengths
        unit_ref[part] = unit32
        length_ref[part] = lengths
        return unit32.astype(bf16)

    lower, upper = slice(0, HALF), slice(HALF, TOK)
    unit_low = normal(lower)
    unit_high = normal(upper)

    @when("odd")
    def _():
        texts[me, lower] = unit_low
        texts[me, upper] = unit_high

    @when("even")
    def _():
        images[z, c] = unit_low
        own[...] = unit_high

    z_msg[8:16, :] = jnp.broadcast_to(pair_ref[...], (8, TOK)).astype(f32)
    pl.semaphore_wait(barrier, 9)

    def rows(index, quarter):
        return texts.at[index, pl.ds(quarter * QUART, QUART)]

    def tsend(name, index, quarter, target, batch=""):
        send(name, rows(index, quarter), rows(index, quarter), r_txt.at[index, quarter], target, batch)

    def twait(index, quarter):
        landed(rows(index, quarter), r_txt.at[index, quarter])

    size = HALF // WAVES

    def piece(slot, w):
        return images.at[slot, c, pl.ds(w * size, size)]

    def isend(name, slot, w, target):
        send(name, piece(slot, w), piece(slot, w), r_img.at[slot, w], target)

    def iwait(slot, w):
        landed(piece(slot, w), r_img.at[slot, w])

    def to_sibling(name, slot):
        send(name, images.at[slot, c], images.at[slot, c], r_sib.at[slot], sibling)

    def image_hop(name, k):
        left, right = (z + 8 - k) % 8, (z + k) % 8
        for w in range(WAVES):
            iwait(left, w)
            if k < 3 or w < WAVES // 2:
                isend(name, left, w, zp)
            if k == 3 and w < WAVES // 2:
                send(name, piece(left, w), piece(left, w), r_far.at[w], zp_sibling)
            iwait(right, w)
            if k < 3 or w >= WAVES // 2:
                isend(name, right, w, zm)
            if k == 3 and w >= WAVES // 2:
                send(name, piece(right, w), piece(right, w), r_far.at[w], zm_sibling)
        to_sibling(name, left)
        to_sibling(name, right)

    def image_last(name):
        far = (z + 4) % 8
        for w in range(WAVES):
            iwait(far, w)
            landed(images.at[far, 1 - c, pl.ds(w * size, size)], r_far.at[w])

    def siblings(p):
        for h in range(2):
            landed(images.at[2 * p + h, 1 - c], r_sib.at[2 * p + h])

    half_z = z // 2
    p_far, p_up, p_dn, p_own = [(half_z + k) % 4 for k in (2, 1, 3, 0)]

    if STEPS > 1:
        @when("even")
        def _():
            n = "even"
            first, second = device(t, (y + 1 + 2 * xh) % 4, xh, z, c), device(t, (y + 1 + 2 * xo) % 4, xh, z, c)

            def mine(w):
                return own.at[pl.ds(w * size, size)]

            for w in range(WAVES):
                send(n, mine(w), piece(z, w), r_x.at[w], partner)
            for w in range(WAVES):
                isend(n, z, w, zp)
                isend(n, z, w, zm)
            to_sibling(n, z)
            image_hop(n, 1)
            for q in range(2):
                index = y * 2 + q
                twait(index, xh)
                tsend(n, index, xh, across[1 - q])
                tsend(n, index, xh, first)
            for q in range(2):
                index = y * 2 + q
                twait(index, xo)
                tsend(n, index, xo, second)
            for q in range(2):
                index = y * 2 + q
                twait(index, 2 + xh)
                tsend(n, index, 2 + xh, across[1 - q])
            for q in range(2):
                index = y * 2 + q
                tsend(n, index, xh, second)
                tsend(n, index, xo, first)
            ya, yb = (y + 3 + 2 * xh) % 4, (y + 1 + 2 * xh) % 4
            for q in range(2):
                index = ya * 2 + q
                twait(index, 2 + xh)
                tsend(n, index, 2 + xh, across[1 - q])
            image_hop(n, 2)
            for q in range(2):
                index = yb * 2 + q
                twait(index, 2 + xh)
                tsend(n, index, 2 + xh, across[1 - q])
            for q in range(2):
                twait(y_dn * 2 + q, 0)
                tsend(n, y_dn * 2 + q, 0, up)
                twait(y_up * 2 + q, 1)
                tsend(n, y_up * 2 + q, 1, dn)
            for q in range(2):
                index = y_far * 2 + q
                twait(index, 2 + xh)
                tsend(n, index, 2 + xh, across[1 - q])
            image_hop(n, 3)
            for q in range(2):
                twait(y_dn * 2 + q, 1)
                twait(y_up * 2 + q, 0)
                for k in range(2):
                    twait(y_far * 2 + q, k)
                for ya in (y, y_dn, y_up, y_far):
                    twait(ya * 2 + q, 2 + xo)

        @when("odd")
        def _():
            n = "odd"
            mine, below, above, far = me, y_dn * 2 + xh, y_up * 2 + xh, y_far * 2 + xh
            other = y * 2 + xo

            def relayed(index, k):
                tsend(n, index, 2 + k, across[k])

            def kept(index):
                for e in range(2):
                    tsend(n, index, 3 - e, across[e])

            for e in range(2):
                tsend(n, mine, e, across[e], "s")
            tsend(n, mine, 2, up, "s")
            tsend(n, mine, 3, dn, "s")
            for e in range(2):
                tsend(n, mine, 1 - e, across[e], "s")
            tsend(n, mine, 3, up, "s")
            tsend(n, mine, 2, dn, "s")
            for w in range(WAVES):
                landed(piece(z, w), r_x.at[w])
                isend(n, z, w, zp)
                isend(n, z, w, zm)
            to_sibling(n, z)
            for e in range(2):
                relayed(mine, e)
            tsend(n, mine, 0, up)
            tsend(n, mine, 1, dn)
            twait(below, 2)
            tsend(n, below, 2, up)
            relayed(below, 0)
            twait(above, 3)
            tsend(n, above, 3, dn)
            relayed(above, 1)
            tsend(n, mine, 1, up)
            tsend(n, mine, 0, dn)
            twait(below, 3)
            relayed(below, 1)
            twait(above, 2)
            relayed(above, 0)
            image_hop(n, 1)
            twait(below, 0)
            tsend(n, below, 0, up)
            twait(above, 1)
            tsend(n, above, 1, dn)
            twait(far, 2)
            relayed(far, 0)
            twait(far, 3)
            relayed(far, 1)
            twait(other, 0)
            tsend(n, other, 0, up)
            twait(other, 1)
            tsend(n, other, 1, dn)
            kept(mine)
            tsend(n, other, 1, up)
            tsend(n, other, 0, dn)
            kept(below)
            kept(above)
            image_hop(n, 2)
            kept(far)
            twait(y_dn * 2 + xo, 0)
            tsend(n, y_dn * 2 + xo, 0, up)
            twait(y_up * 2 + xo, 1)
            tsend(n, y_up * 2 + xo, 1, dn)
            image_hop(n, 3)
            for q in (xh, xo):
                twait(y_dn * 2 + q, 1)
                twait(y_up * 2 + q, 0)
                for k in range(2):
                    twait(y_far * 2 + q, k)
            for ya in (y, y_dn, y_up, y_far):
                for k in range(2):
                    twait(ya * 2 + xo, 2 + k)

        siblings(p_own)

    def first_id(index):
        return ((index * 8 + z) * 2 + c) * TOK

    sub_ids = lax.broadcasted_iota(jnp.int32, (TOK, 1), 0)

    def total(x):
        return jnp.sum(jnp.sum(x, axis=0, keepdims=True), axis=1, keepdims=True)

    if STEPS > 2:
        all_texts = texts[...].reshape(WIDE, D)

        def stats(p, first):
            two = images[pl.ds(2 * p, 2)].reshape(2 * TOK, D)
            dots = lax.dot_general(all_texts, two, (((1,), (1,)), ((), ())), preferred_element_type=f32)
            scores = scale * dots
            ex = jnp.exp(scores - scale)
            exps[:, :, pl.ds(pl.multiple_of(p * 2 * TOK, 2 * TOK), 2 * TOK)] = ex.reshape(8, TOK, 2 * TOK)
            es = ex * scores
            z_sum = jnp.sum(ex, axis=0, keepdims=True)
            e_sum = jnp.sum(es, axis=0, keepdims=True)
            for h in range(2):
                part = slice(h * TOK, (h + 1) * TOK)
                z_msg[pl.ds(2 * p + h, 1), :] = z_sum[:, part]
                e_sums[pl.ds(2 * p + h, 1), :] = e_sum[:, part]
            zr = (ex[:, 0:TOK] + ex[:, TOK:]).reshape(8, TOK, TOK)
            er = (es[:, 0:TOK] + es[:, TOK:]).reshape(8, TOK, TOK)
            z_row[...] = zr if first else z_row[...] + zr
            e_row[...] = er if first else e_row[...] + er

        stats(p_own, True)

        for p in (p_up, p_dn):
            siblings(p)
            stats(p, False)

        @when("even")
        def _():
            image_last("even")

        @when("odd")
        def _():
            image_last("odd")

        near_far = (z + 3 + 2 * ((z + 1) % 2)) % 8
        landed(images.at[near_far, 1 - c], r_sib.at[near_far])
        stats(p_far, False)
        for peer in line_peers if STEPS > 3 else ():
            send("all", z_msg, z_img_all.at[line_rank], r_zi.at[0], peer)
        for k in range(8):
            stat_send[1, k:k + 1, :] = jnp.sum(z_row[k].T, axis=0, keepdims=True)
        all_images = images[...].reshape(WIDE, D)

    if STEPS > 3:
        for peer in plane_peers:
            send("all", stat_send.at[1], z_txt_all.at[plane_rank], r_zt.at[0], peer)
        z_img_all[line_rank] = z_msg[...]
        z_txt_all[plane_rank] = stat_send[1]
        landed(z_img_all.at[0:15], r_zi.at[0])

        def own_half(k, core):
            line = z_img_all[2 * k + core, 8:9]
            return jnp.where(odd, line[:, HALF:TOK], line[:, 0:HALF]).astype(jnp.int32)

        for k in range(8):
            pair_rows[k:k + 1, :] = jnp.concatenate([own_half(k, core) for core in range(2)], axis=1)
        landed(z_txt_all.at[0:15], r_zt.at[0])
        z_img = jnp.sum(z_img_all[:, 0:8], axis=0)
        z_txt = jnp.sum(z_txt_all[...], axis=0)

    if STEPS > 4:
        stat_send[3] = 0.5 / z_img
        stat_send[2] = 0.5 / z_txt
        for k in range(8):
            columns[k] = jnp.broadcast_to(stat_send[2, k:k + 1, :], (TOK, TOK)).T

        def weigh(p):
            lanes = pl.ds(pl.multiple_of(p * 2 * TOK, 2 * TOK), 2 * TOK)
            img = jnp.concatenate([stat_send[3, pl.ds(2 * p + h, 1), :] for h in range(2)], axis=1)
            partners = jnp.concatenate([pair_rows[pl.ds(2 * p + h, 1), :] for h in range(2)], axis=1)

            def step(index, carry):
                column = columns[index]
                ids = first_id(index) + sub_ids
                match = partners == ids
                ex = exps[index, :, lanes]
                value = ex * (img + jnp.concatenate([column, column], axis=1))
                weights[index, :, lanes] = (value - jnp.where(match, 1.0, 0.0)).astype(bf16)
                return carry + jnp.sum(jnp.where(match, ex, 0.0), axis=0, keepdims=True)

            hit = lax.fori_loop(0, 8, step, jnp.zeros((1, 2 * TOK), f32))
            for h in range(2):
                hits[pl.ds(2 * p + h, 1), :] = hit[:, h * TOK:(h + 1) * TOK]

        weigh(p_far)

    def text_block(ya):
        pair_of = pl.ds(2 * ya, 2)
        two = weights[pair_of].reshape(2 * TOK, WIDE)
        part = jnp.dot(two, all_images, preferred_element_type=f32)
        text_part[pair_of] = part.reshape(2, TOK, D)

    def quart(k):
        return pl.ds(k * QUART, QUART)

    def stage(index, k):
        text_send[index, quart(k)] = text_part[index, quart(k)].astype(bf16)
        return text_send.at[index, quart(k)]

    def stage_two(ya, k):
        for q in range(2):
            stage(ya * 2 + q, k)
        return text_send.at[pl.ds(2 * ya, 2), quart(k)]

    def add(index, k, value):
        text_part[index, quart(k)] = text_part[index, quart(k)] + value.astype(f32)

    def give_b(slot, ya):
        for k in range(2):
            send("odd", stage(ya * 2 + xo, 2 + k), rb_even.at[slot, xh], r_be.at[slot, xh], across[k])

    def free_b(slot, ya):
        for q in range(2):
            send("even", stage(ya * 2 + q, 2 + xo), rb_odd.at[slot, xh, 0], r_bo.at[slot, xh, 0], across[q])

    def pass_b(slot, ya):
        for q in range(2):
            index = ya * 2 + q
            landed(rb_even.at[slot, 1 - q], r_be.at[slot, 1 - q])
            add(index, 2 + xh, rb_even[slot, 1 - q])
            send("even", stage(index, 2 + xh), rb_odd.at[slot, xh, 1], r_bo.at[slot, xh, 1], across[q])

    def take_b(slot, ya):
        index = ya * 2 + xh
        for part in range(2):
            for e in range(2):
                landed(rb_odd.at[slot, e, part], r_bo.at[slot, e, part])
                add(index, 2 + (e if part else 1 - e), rb_odd[slot, e, part])

    def image_block(p, with_sibling=True):
        lanes = pl.ds(pl.multiple_of(p * 2 * TOK, 2 * TOK), 2 * TOK)
        part = lax.dot_general(
            weights[:, :, lanes].reshape(WIDE, 2 * TOK), texts[...].reshape(WIDE, D),
            (((0,), (0,)), ((), ())), preferred_element_type=f32,
        )
        both = pl.ds(2 * p, 2)
        image_part[both] = part.reshape(2, 2, HALF, D)
        if with_sibling:
            image_send[both, 1 - c] = image_part[both, 1 - c].astype(bf16)
            send("all", image_send.at[both, 1 - c], image_sib.at[both], r_is.at[p], sibling)

    def swap_near_far():
        image_send[near_far, 1 - c] = image_part[near_far, 1 - c].astype(bf16)
        send("all", image_send.at[near_far, 1 - c], image_sib.at[near_far], r_is.at[p_far], sibling)

    def add_near_far():
        landed(image_sib.at[near_far], r_is.at[p_far])
        image_part[near_far, c] = image_part[near_far, c] + image_sib[near_far].astype(f32)

    def add_sibling(p):
        both = pl.ds(2 * p, 2)
        landed(image_sib.at[both], r_is.at[p])
        image_part[both, c] = image_part[both, c] + image_sib[both].astype(f32)

    def source_of(slot, h):
        return image_send.at[slot, c, quart(h)]

    def ring_send(m, h, right):
        hops = 4 - m
        slot = (z + hops) % 8 if right else (z + 8 - hops) % 8
        into = image_right if right else image_left
        sem = r_ir if right else r_il
        value = image_part[slot, c, quart(h)]
        if m == 1 and h == (0 if right else 1):
            for core in range(2):
                landed(image_first.at[h, core], r_i0.at[h, core])
                value = value + image_first[h, core].astype(f32)
        if m > 1:
            landed(into.at[m - 1, quart(h)], sem.at[m - 1, h])
            value = value + into[m - 1, quart(h)].astype(f32)
        image_send[slot, c, quart(h)] = value.astype(bf16)
        if m < 3:
            send("all", source_of(slot, h), into.at[m, quart(h)], sem.at[m, h], zp if right else zm)
            return
        way = 0 if right else 1

        @when("even")
        def _():
            send("even", source_of(slot, h), into.at[m, quart(h)], sem.at[m, h], zp if right else zm)

        @when("odd")
        def _():
            send(
                "odd", source_of(slot, h), fin_recv.at[way, quart(h)], r_fin.at[way, h],
                partner_zp if right else partner_zm,
            )

    if STEPS > 5:
        def spread(slot, ya):
            @when("odd")
            def _():
                give_b(slot, ya)

            @when("even")
            def _():
                free_b(slot, ya)

        def pass_on(slot, ya):
            @when("even")
            def _():
                pass_b(slot, ya)

        def hop_a(way, ya, target):
            landed(ra_one.at[way], r_a1.at[way])
            for q in range(2):
                add(ya * 2 + q, way, ra_one[way, q])
            send("all", stage_two(ya, way), ra_two.at[way, 1], r_a2.at[way, 1], target)

        def r1():
            send("all", stage_two(y_far, 0), ra_one.at[0], r_a1.at[0], up)
            send("all", stage_two(y_far, 1), ra_one.at[1], r_a1.at[1], dn)

        def m0():
            far = (z + 4) % 8
            for way, right, left in ((0, zp, zp_sibling), (1, zm, zm_sibling)):
                for core, target in ((c, right), (1 - c, left)):
                    image_send[far, core, quart(way)] = image_part[far, core, quart(way)].astype(bf16)
                    send(
                        "all", image_send.at[far, core, quart(way)], image_first.at[way, c], r_i0.at[way, c], target
                    )

        def m1_free():
            add_near_far()
            add_sibling(p_up)
            add_sibling(p_dn)
            ring_send(1, 1, True)
            ring_send(1, 0, False)

        def m1():
            ring_send(1, 0, True)
            ring_send(1, 1, False)

        def far_b():
            @when("odd")
            def _():
                take_b(0, y_far)
                send("odd", stage(y_far * 2 + xh, 2), rb_one.at[0], r_b1.at[0], up)
                send("odd", stage(y_far * 2 + xh, 3), rb_one.at[1], r_b1.at[1], dn)

        def free_a(way, ya, target):
            send("all", stage_two(ya, 1 - way), ra_two.at[way, 0], r_a2.at[way, 0], target)

        def m2():
            for h in (1, 0):
                ring_send(2, h, True)
                ring_send(2, 1 - h, False)

        T = lambda ya, slot: (text_block(ya), spread(slot, ya))
        I = image_block
        def rest():
            for p in (p_up, p_dn, p_own):
                weigh(p)

        lane = lax.broadcasted_iota(jnp.int32, (8, TOK), 1)

        def scalars():
            log_img = total(jnp.log(z_img))
            log_txt = total(jnp.log(z_txt))
            t_img = total(e_sums[...] / z_img)
            t_acc = e_row[0] * columns[0]
            for k in range(1, 8):
                t_acc = t_acc + e_row[k] * columns[k]
            t_txt = 2.0 * total(t_acc)
            hit = hits[...]
            found = hit > 0.0
            matched = total(jnp.where(found, jnp.log(jnp.where(found, hit, 1.0)) + scale, 0.0))
            scal_send[0] = jnp.where(
                lane == 0, log_txt,
                jnp.where(lane == 1, t_img, jnp.where(lane == 2, t_txt, jnp.where(lane == 3, matched, 0.0))),
            )
            for peer in line_peers:
                send("all", scal_send.at[0], scal_z.at[line_rank], r_sz.at[0], peer)
            scal_z[line_rank] = scal_send[0]
            return log_img

        def second_step(log_img):
            landed(scal_z.at[0:15], r_sz.at[0])
            line_sum = jnp.sum(scal_z[...], axis=0)
            scal_send[1] = jnp.where(lane == 4, log_img, line_sum)
            for peer in plane_peers:
                send("all", scal_send.at[1], scal_p.at[plane_rank], r_sp.at[0], peer)
            scal_p[plane_rank] = scal_send[1]
            return line_sum

        S1, S2 = scalars, second_step
        I(p_far, False)
        m0()
        swap_near_far()
        rest()
        T(y_far, 0)
        r1()
        I(p_up)
        I(p_dn)
        T(y_dn, 1)
        m1_free()
        T(y_up, 2)
        log_img = S1()
        pass_on(0, y_far)
        m1()
        hop_a(0, y_up, up)
        hop_a(1, y_dn, dn)
        free_a(1, y_dn, dn)
        free_a(0, y_up, up)
        T(y, 3)
        pass_on(1, y_dn)
        pass_on(2, y_up)
        I(p_own)
        far_b()
        pass_on(3, y)
        line_sum = S2(log_img)
        m2()

        add_sibling(p_own)

        @when("odd")
        def _():
            fin_send[...] = image_part[z, c].astype(bf16)
            send("odd", fin_send, fin_recv.at[2], r_fin.at[2, 0], partner)

        for part in range(2):
            for way in range(2):
                landed(ra_two.at[way, part], r_a2.at[way, part])
                for q in range(2):
                    add(y * 2 + q, way if part else 1 - way, ra_two[way, part, q])

        @when("odd")
        def _():
            for k in range(2):
                send("odd", stage(y * 2 + xo, k), ra_x.at[xh], r_ax.at[xh], across[k])

        @when("even")
        def _():
            for q in range(2):
                send("even", stage(y * 2 + q, xo), ra_fin.at[xh, 0], r_af.at[xh, 0], across[q])

        def m3():
            for h in (1, 0):
                ring_send(3, h, True)
                ring_send(3, 1 - h, False)

        m3()

        @when("odd")
        def _():
            take_b(1, y_dn)
            take_b(2, y_up)
            send("odd", stage(y_up * 2 + xh, 3), rb_two.at[0, 0], r_b2.at[0, 0], up)
            send("odd", stage(y_dn * 2 + xh, 2), rb_two.at[1, 0], r_b2.at[1, 0], dn)
            for way, ya, target in ((0, y_up, up), (1, y_dn, dn)):
                landed(rb_one.at[way], r_b1.at[way])
                add(ya * 2 + xh, 2 + way, rb_one[way])
                send("odd", stage(ya * 2 + xh, 2 + way), rb_two.at[way, 1], r_b2.at[way, 1], target)

        @when("even")
        def _():
            for q in range(2):
                landed(ra_x.at[1 - q], r_ax.at[1 - q])
                add(y * 2 + q, xh, ra_x[1 - q])
                send("even", stage(y * 2 + q, xh), ra_fin.at[xh, 1], r_af.at[xh, 1], across[q])

        landed(scal_p.at[0:15], r_sp.at[0])
        all_sum = jnp.sum(scal_p[...], axis=0)

        def pick(x, k):
            return jnp.sum(jnp.where(lane[0:1] == k, x[0:1], 0.0))

        log_all = jnp.where(odd, pick(line_sum, 0), pick(all_sum, 4))
        t_all = jnp.where(odd, pick(all_sum, 2), pick(all_sum, 1))
        p_all = pick(all_sum, 3)
        loss_ref[0] = (scale * TOKENS + log_all - p_all) * (1.0 / (2 * TOKENS))
        sgrad_ref[0] = (t_all - p_all) / scale * (1.0 / (2 * TOKENS))

        def finish(part, grads):
            unit32, lengths = unit_ref[part], length_ref[part]
            grads = scale * grads
            inner = jnp.sum(unit32 * grads, axis=1, keepdims=True)
            result = (grads - unit32 * inner) / lengths
            out_ref[0, part] = result.astype(bf16)

        @when("odd")
        def _():
            take_b(3, y)

        @when("odd")
        def _():
            for part in range(2):
                for way in range(2):
                    landed(rb_two.at[way, part], r_b2.at[way, part])
                    add(me, 2 + (way if part else 1 - way), rb_two[way, part])
            finish(upper, text_part[me, upper])
            for part in range(2):
                for e in range(2):
                    landed(ra_fin.at[e, part], r_af.at[e, part])
                    add(me, e if part else 1 - e, ra_fin[e, part])
            finish(lower, text_part[me, lower])

        @when("even")
        def _():
            for h in range(2):
                landed(image_right.at[3, quart(h)], r_ir.at[3, h])
                landed(image_left.at[3, quart(h)], r_il.at[3, h])
            finish(lower, image_part[z, c] + image_right[3].astype(f32) + image_left[3].astype(f32))
            landed(fin_recv.at[2], r_fin.at[2, 0])
            for h in range(2):
                landed(fin_recv.at[0, quart(h)], r_fin.at[0, h])
                landed(fin_recv.at[1, quart(h)], r_fin.at[1, h])
            finish(
                upper,
                fin_recv[0].astype(f32) + fin_recv[1].astype(f32) + fin_recv[2].astype(f32),
            )


    assert count[0] <= SENDS, count[0]
    for name in pending:
        if pending[name]:
            @when(name)
            def _():
                drain(name)


def body(embeddings, pair, logit_scale):
    vmem = pl.BlockSpec(memory_space=pltpu.VMEM)
    smem = pl.BlockSpec(memory_space=pltpu.SMEM)
    dma = pltpu.SemaphoreType.DMA
    scratch = [
        ((TOK, D), bf16),
        ((TOK, D), f32),
        ((TOK, 1), f32),
        ((HALF, D), bf16),
        ((8, 2, HALF, D), bf16),
        ((8, TOK, D), bf16),
        ((16, TOK), f32),
        ((8, TOK, WIDE), f32),
        ((8, TOK, WIDE), bf16),
        ((8, TOK, D), f32),
        ((8, TOK, D), bf16),
        ((2, 2, QUART, D), bf16),
        ((2, 2, 2, QUART, D), bf16),
        ((2, QUART, D), bf16),
        ((2, 2, QUART, D), bf16),
        ((4, 2, 2, QUART, D), bf16),
        ((4, 2, QUART, D), bf16),
        ((2, QUART, D), bf16),
        ((2, 2, QUART, D), bf16),
        ((8, 2, HALF, D), f32),
        ((8, 2, HALF, D), bf16),
        ((8, HALF, D), bf16),
        ((4, HALF, D), bf16),
        ((4, HALF, D), bf16),
        ((2, 2, QUART, D), bf16),
        ((8, TOK, TOK), f32),
        ((8, TOK, TOK), f32),
        ((8, TOK, TOK), f32),
        ((8, TOK), jnp.int32),
        ((8, TOK), f32),
        ((4, 8, TOK), f32),
        ((16, 16, TOK), f32),
        ((16, 8, TOK), f32),
        ((8, TOK), f32),
        ((2, 8, TOK), f32),
        ((16, 8, TOK), f32),
        ((16, 8, TOK), f32),
        ((HALF, D), bf16),
        ((3, HALF, D), bf16),
    ]
    sems = [
        (1,), (SENDS,), (8, 4), (8, WAVES), (8,), (WAVES,), (1,), (1,), (1,), (1,),
        (2,), (2, 2), (2,), (2, 2), (4, 2, 2), (4, 2), (2,), (2, 2), (4,), (4, 2), (4, 2), (3, 2), (WAVES,), (2, 2),
    ]
    grads, loss, scale_grad = pl.pallas_call(
        kernel,
        out_shape=(
            jax.ShapeDtypeStruct((1, TOK, D), bf16),
            jax.ShapeDtypeStruct((1,), f32),
            jax.ShapeDtypeStruct((1,), f32),
        ),
        in_specs=[smem, pl.BlockSpec(memory_space=pl.ANY), vmem],
        out_specs=(vmem, smem, smem),
        scratch_shapes=[pltpu.VMEM(shape, dtype) for shape, dtype in scratch] + [dma(shape) for shape in sems],
        compiler_params=pltpu.CompilerParams(
            collective_id=0, has_side_effects=True, vmem_limit_bytes=56 * 2 ** 20
        ),
        cost_estimate=pl.CostEstimate(flops=6 * WIDE * WIDE * D, bytes_accessed=2 ** 20, transcendentals=2 ** 20),
        name="contrastive",
    )(
        logit_scale.astype(f32).reshape(1),
        embeddings,
        pair.reshape(1, TOK),
    )
    return grads, loss, scale_grad


def solution(mesh):
    placed = (P("tower", "blk", None), P("blk"), P())
    return jax.shard_map(
        body,
        mesh=mesh,
        in_specs=placed,
        out_specs=(P("tower", "blk", None), P("tower"), P("tower")),
        check_vma=False,
    )
```

```python
import jax
import jax.numpy as jnp
from jax import lax
from jax.experimental import pallas as pl
from jax.experimental.pallas import tpu as pltpu
from jax.sharding import PartitionSpec as P

eps = 1e-06
TOK = 128
D = 896
TOKENS = 16384
NY, NXH, NZ, NC = 4, 2, 8, 2
HALF, QUART = TOK // 2, TOK // 4
WIDE = 8 * TOK
f32 = jnp.float32
bf16 = jnp.bfloat16
MESH = pl.DeviceIdType.MESH
STEPS = 9
WAVES = 2
SENDS = 30


def device(t, y, xh, z, c):
    return (t, ((y * NXH + xh) * NZ + z) * NC + c)


def kernel(
    scale_ref, emb_hbm, pair_ref,
    out_ref, loss_ref, sgrad_ref,
    emb_ref, unit_ref, length_ref, own, images, texts, z_msg, exps, weights,
    text_part, text_send, ra_one, ra_two, ra_x, ra_fin, rb_odd, rb_even, rb_one, rb_two,
    image_part, image_send, image_sib, image_right, image_left, image_first,
    z_row, e_row, columns, pair_rows, hits, stat_send, z_img_all, z_txt_all, e_sums, scal_send, scal_z, scal_p, fin_send, fin_recv,
    s_in, s_all, r_txt, r_img, r_sib, r_x, r_zi, r_zt, r_sz, r_sp,
    r_a1, r_a2, r_ax, r_af, r_bo, r_be, r_b1, r_b2, r_is, r_ir, r_il, r_fin, r_far, r_i0,
):
    t = lax.axis_index("tower")
    b = lax.axis_index("blk")
    c = b % 2
    z = (b // 2) % 8
    xh = (b // 16) % 2
    y = b // 32
    odd = t == 1
    even = t == 0
    line_rank = z * 2 + c
    plane_rank = (t * 4 + y) * 2 + xh
    me = y * 2 + xh
    scale = scale_ref[0]
    y_up, y_dn, y_far = (y + 1) % 4, (y + 3) % 4, (y + 2) % 4
    xo = 1 - xh

    conds = {"all": None, "odd": odd, "even": even}
    pending = {name: {} for name in conds}
    count = [0]

    def when(name):
        if name == "all":
            return lambda fn: fn()
        return pl.when(conds[name])

    def send(name, src, dst, rsem, target, batch=""):
        groups = pending[name].setdefault((src.shape, batch), [])
        if not groups or groups[-1][1] == (4 if len(src.shape) == 3 else 15 if src.shape[1] == TOK else 8):
            groups.append([count[0], 0])
            count[0] += 1
        groups[-1][1] += 1
        pltpu.make_async_remote_copy(
            src_ref=src, dst_ref=dst, send_sem=s_all.at[groups[-1][0]], recv_sem=rsem,
            device_id=target, device_id_type=MESH,
        ).start()

    def drain(name, batch=None):
        for key in [k for k in pending[name] if batch is None or k[1] == batch]:
            shape = key[0]
            for slot, copies in pending[name].pop(key):
                if len(shape) == 3:
                    like = texts.at[0:2 * copies, 0:shape[1]]
                elif shape == (16, TOK):
                    like = z_img_all.at[0:copies]
                elif shape == (8, TOK):
                    like = z_txt_all.at[0:copies]
                else:
                    like = texts.at[0:copies, 0:shape[0]]
                pltpu.make_async_copy(like, like, s_all.at[slot]).wait()

    def landed(dst, rsem):
        pltpu.make_async_copy(dst, dst, rsem).wait()

    up = device(t, y_up, xh, z, c)
    dn = device(t, y_dn, xh, z, c)
    zp = device(t, y, xh, (z + 1) % 8, c)
    zm = device(t, y, xh, (z + 7) % 8, c)
    sibling = device(t, y, xh, z, 1 - c)
    zp_sibling = device(t, y, xh, (z + 1) % 8, 1 - c)
    zm_sibling = device(t, y, xh, (z + 7) % 8, 1 - c)
    across = [device(1 - t, y, 0, z, c), device(1 - t, y, 1, z, c)]
    partner = device(1 - t, y, xh, z, c)
    partner_zp = device(1 - t, y, xh, (z + 1) % 8, c)
    partner_zm = device(1 - t, y, xh, (z + 7) % 8, c)
    line_peers = [
        device(t, y, xh, (z + dz) % 8, (c + dc) % 2)
        for dz in (4, 3, 5, 2, 6, 1, 7, 0) for dc in (0, 1) if dz or dc
    ]
    plane_peers = [
        device((t + dt) % 2, (y + dy) % 4, (xh + dx) % 2, z, c)
        for dy in (2, 1, 3, 0) for dx in (1, 0) for dt in (0, 1) if dy or dx or dt
    ]

    fetch = pltpu.make_async_copy(emb_hbm.at[0], emb_ref, s_in.at[0])
    fetch.start()
    barrier = pltpu.get_barrier_semaphore()
    for peer in (up, dn, zp, zm, sibling, across[0], across[1]):
        pl.semaphore_signal(barrier, inc=1, device_id=peer, device_id_type=MESH)
    fetch.wait()

    def normal(part):
        wide = emb_ref[part].astype(f32)
        lengths = jnp.sqrt(jnp.sum(wide * wide, axis=1, keepdims=True) + eps)
        unit32 = wide / lengths
        unit_ref[part] = unit32
        length_ref[part] = lengths
        return unit32.astype(bf16)

    lower, upper = slice(0, HALF), slice(HALF, TOK)
    unit_low = normal(lower)
    unit_high = normal(upper)

    @when("odd")
    def _():
        texts[me, lower] = unit_low
        texts[me, upper] = unit_high

    @when("even")
    def _():
        images[z, c] = unit_low
        own[...] = unit_high

    z_msg[8:16, :] = jnp.broadcast_to(pair_ref[...], (8, TOK)).astype(f32)
    pl.semaphore_wait(barrier, 7)

    def rows(index, quarter):
        return texts.at[index, pl.ds(quarter * QUART, QUART)]

    def tsend(name, index, quarter, target, batch=""):
        send(name, rows(index, quarter), rows(index, quarter), r_txt.at[index, quarter], target, batch)

    def twait(index, quarter):
        landed(rows(index, quarter), r_txt.at[index, quarter])

    size = HALF // WAVES

    def piece(slot, w):
        return images.at[slot, c, pl.ds(w * size, size)]

    def isend(name, slot, w, target):
        send(name, piece(slot, w), piece(slot, w), r_img.at[slot, w], target)

    def iwait(slot, w):
        landed(piece(slot, w), r_img.at[slot, w])

    def to_sibling(name, slot):
        send(name, images.at[slot, c], images.at[slot, c], r_sib.at[slot], sibling)

    def image_hop(name, k):
        left, right = (z + 8 - k) % 8, (z + k) % 8
        for w in range(WAVES):
            iwait(left, w)
            if k < 3 or w < WAVES // 2:
                isend(name, left, w, zp)
            if k == 3 and w < WAVES // 2:
                send(name, piece(left, w), piece(left, w), r_far.at[w], zp_sibling)
            iwait(right, w)
            if k < 3 or w >= WAVES // 2:
                isend(name, right, w, zm)
            if k == 3 and w >= WAVES // 2:
                send(name, piece(right, w), piece(right, w), r_far.at[w], zm_sibling)
        to_sibling(name, left)
        to_sibling(name, right)

    def image_last(name):
        far = (z + 4) % 8
        for w in range(WAVES):
            iwait(far, w)
            landed(images.at[far, 1 - c, pl.ds(w * size, size)], r_far.at[w])

    def siblings(p):
        for h in range(2):
            landed(images.at[2 * p + h, 1 - c], r_sib.at[2 * p + h])

    half_z = z // 2
    p_far, p_up, p_dn, p_own = [(half_z + k) % 4 for k in (2, 1, 3, 0)]

    if STEPS > 1:
        @when("even")
        def _():
            n = "even"
            first, second = device(t, (y + 1 + 2 * xh) % 4, xh, z, c), device(t, (y + 1 + 2 * xo) % 4, xh, z, c)

            def mine(w):
                return own.at[pl.ds(w * size, size)]

            for w in range(WAVES):
                send(n, mine(w), piece(z, w), r_x.at[w], partner)
            for w in range(WAVES):
                isend(n, z, w, zp)
                isend(n, z, w, zm)
            to_sibling(n, z)
            image_hop(n, 1)
            for q in range(2):
                index = y * 2 + q
                twait(index, xh)
                tsend(n, index, xh, across[1 - q])
                tsend(n, index, xh, first)
            for q in range(2):
                index = y * 2 + q
                twait(index, xo)
                tsend(n, index, xo, second)
            for q in range(2):
                index = y * 2 + q
                twait(index, 2 + xh)
                tsend(n, index, 2 + xh, across[1 - q])
            for q in range(2):
                index = y * 2 + q
                tsend(n, index, xh, second)
                tsend(n, index, xo, first)
            ya, yb = (y + 3 + 2 * xh) % 4, (y + 1 + 2 * xh) % 4
            for q in range(2):
                index = ya * 2 + q
                twait(index, 2 + xh)
                tsend(n, index, 2 + xh, across[1 - q])
            image_hop(n, 2)
            for q in range(2):
                index = yb * 2 + q
                twait(index, 2 + xh)
                tsend(n, index, 2 + xh, across[1 - q])
            for q in range(2):
                twait(y_dn * 2 + q, 0)
                tsend(n, y_dn * 2 + q, 0, up)
                twait(y_up * 2 + q, 1)
                tsend(n, y_up * 2 + q, 1, dn)
            for q in range(2):
                index = y_far * 2 + q
                twait(index, 2 + xh)
                tsend(n, index, 2 + xh, across[1 - q])
            image_hop(n, 3)
            for q in range(2):
                twait(y_dn * 2 + q, 1)
                twait(y_up * 2 + q, 0)
                for k in range(2):
                    twait(y_far * 2 + q, k)
                for ya in (y, y_dn, y_up, y_far):
                    twait(ya * 2 + q, 2 + xo)

        @when("odd")
        def _():
            n = "odd"
            mine, below, above, far = me, y_dn * 2 + xh, y_up * 2 + xh, y_far * 2 + xh
            other = y * 2 + xo

            def relayed(index, k):
                tsend(n, index, 2 + k, across[k])

            def kept(index):
                for e in range(2):
                    tsend(n, index, 3 - e, across[e])

            for e in range(2):
                tsend(n, mine, e, across[e], "s")
            tsend(n, mine, 2, up, "s")
            tsend(n, mine, 3, dn, "s")
            for e in range(2):
                tsend(n, mine, 1 - e, across[e], "s")
            tsend(n, mine, 3, up, "s")
            tsend(n, mine, 2, dn, "s")
            for w in range(WAVES):
                landed(piece(z, w), r_x.at[w])
                isend(n, z, w, zp)
                isend(n, z, w, zm)
            to_sibling(n, z)
            for e in range(2):
                relayed(mine, e)
            tsend(n, mine, 0, up)
            tsend(n, mine, 1, dn)
            twait(below, 2)
            tsend(n, below, 2, up)
            relayed(below, 0)
            twait(above, 3)
            tsend(n, above, 3, dn)
            relayed(above, 1)
            tsend(n, mine, 1, up)
            tsend(n, mine, 0, dn)
            twait(below, 3)
            relayed(below, 1)
            twait(above, 2)
            relayed(above, 0)
            image_hop(n, 1)
            twait(below, 0)
            tsend(n, below, 0, up)
            twait(above, 1)
            tsend(n, above, 1, dn)
            twait(far, 2)
            relayed(far, 0)
            twait(far, 3)
            relayed(far, 1)
            twait(other, 0)
            tsend(n, other, 0, up)
            twait(other, 1)
            tsend(n, other, 1, dn)
            kept(mine)
            tsend(n, other, 1, up)
            tsend(n, other, 0, dn)
            kept(below)
            kept(above)
            image_hop(n, 2)
            kept(far)
            twait(y_dn * 2 + xo, 0)
            tsend(n, y_dn * 2 + xo, 0, up)
            twait(y_up * 2 + xo, 1)
            tsend(n, y_up * 2 + xo, 1, dn)
            image_hop(n, 3)
            for q in (xh, xo):
                twait(y_dn * 2 + q, 1)
                twait(y_up * 2 + q, 0)
                for k in range(2):
                    twait(y_far * 2 + q, k)
            for ya in (y, y_dn, y_up, y_far):
                for k in range(2):
                    twait(ya * 2 + xo, 2 + k)

        siblings(p_own)

    def first_id(index):
        return ((index * 8 + z) * 2 + c) * TOK

    sub_ids = lax.broadcasted_iota(jnp.int32, (TOK, 1), 0)

    def total(x):
        return jnp.sum(jnp.sum(x, axis=0, keepdims=True), axis=1, keepdims=True)

    if STEPS > 2:
        all_texts = texts[...].reshape(WIDE, D)

        def stats(p, first):
            two = images[pl.ds(2 * p, 2)].reshape(2 * TOK, D)
            dots = lax.dot_general(all_texts, two, (((1,), (1,)), ((), ())), preferred_element_type=f32)
            scores = scale * dots
            ex = jnp.exp(scores - scale)
            exps[:, :, pl.ds(pl.multiple_of(p * 2 * TOK, 2 * TOK), 2 * TOK)] = ex.reshape(8, TOK, 2 * TOK)
            es = ex * scores
            z_sum = jnp.sum(ex, axis=0, keepdims=True)
            e_sum = jnp.sum(es, axis=0, keepdims=True)
            for h in range(2):
                part = slice(h * TOK, (h + 1) * TOK)
                z_msg[pl.ds(2 * p + h, 1), :] = z_sum[:, part]
                e_sums[pl.ds(2 * p + h, 1), :] = e_sum[:, part]
            zr = (ex[:, 0:TOK] + ex[:, TOK:]).reshape(8, TOK, TOK)
            er = (es[:, 0:TOK] + es[:, TOK:]).reshape(8, TOK, TOK)
            z_row[...] = zr if first else z_row[...] + zr
            e_row[...] = er if first else e_row[...] + er

        stats(p_own, True)

        for p in (p_up, p_dn):
            siblings(p)
            stats(p, False)

        @when("even")
        def _():
            image_last("even")

        @when("odd")
        def _():
            image_last("odd")

        near_far = (z + 3 + 2 * ((z + 1) % 2)) % 8
        landed(images.at[near_far, 1 - c], r_sib.at[near_far])
        stats(p_far, False)
        for peer in line_peers if STEPS > 3 else ():
            send("all", z_msg, z_img_all.at[line_rank], r_zi.at[0], peer)
        for k in range(8):
            stat_send[1, k:k + 1, :] = jnp.sum(z_row[k].T, axis=0, keepdims=True)
        all_images = images[...].reshape(WIDE, D)

    if STEPS > 3:
        for peer in plane_peers:
            send("all", stat_send.at[1], z_txt_all.at[plane_rank], r_zt.at[0], peer)
        z_img_all[line_rank] = z_msg[...]
        z_txt_all[plane_rank] = stat_send[1]
        landed(z_img_all.at[0:15], r_zi.at[0])

        def own_half(k, core):
            line = z_img_all[2 * k + core, 8:9]
            return jnp.where(odd, line[:, HALF:TOK], line[:, 0:HALF]).astype(jnp.int32)

        for k in range(8):
            pair_rows[k:k + 1, :] = jnp.concatenate([own_half(k, core) for core in range(2)], axis=1)
        landed(z_txt_all.at[0:15], r_zt.at[0])
        z_img = jnp.sum(z_img_all[:, 0:8], axis=0)
        z_txt = jnp.sum(z_txt_all[...], axis=0)

    if STEPS > 4:
        stat_send[3] = 0.5 / z_img
        stat_send[2] = 0.5 / z_txt
        for k in range(8):
            columns[k] = jnp.broadcast_to(stat_send[2, k:k + 1, :], (TOK, TOK)).T

        def weigh(p):
            lanes = pl.ds(pl.multiple_of(p * 2 * TOK, 2 * TOK), 2 * TOK)
            img = jnp.concatenate([stat_send[3, pl.ds(2 * p + h, 1), :] for h in range(2)], axis=1)
            partners = jnp.concatenate([pair_rows[pl.ds(2 * p + h, 1), :] for h in range(2)], axis=1)

            def step(index, carry):
                column = columns[index]
                ids = first_id(index) + sub_ids
                match = partners == ids
                ex = exps[index, :, lanes]
                value = ex * (img + jnp.concatenate([column, column], axis=1))
                weights[index, :, lanes] = (value - jnp.where(match, 1.0, 0.0)).astype(bf16)
                return carry + jnp.sum(jnp.where(match, ex, 0.0), axis=0, keepdims=True)

            hit = lax.fori_loop(0, 8, step, jnp.zeros((1, 2 * TOK), f32))
            for h in range(2):
                hits[pl.ds(2 * p + h, 1), :] = hit[:, h * TOK:(h + 1) * TOK]

        weigh(p_far)

    def text_block(ya):
        pair_of = pl.ds(2 * ya, 2)
        two = weights[pair_of].reshape(2 * TOK, WIDE)
        part = jnp.dot(two, all_images, preferred_element_type=f32)
        text_part[pair_of] = part.reshape(2, TOK, D)

    def quart(k):
        return pl.ds(k * QUART, QUART)

    def stage(index, k):
        text_send[index, quart(k)] = text_part[index, quart(k)].astype(bf16)
        return text_send.at[index, quart(k)]

    def stage_two(ya, k):
        for q in range(2):
            stage(ya * 2 + q, k)
        return text_send.at[pl.ds(2 * ya, 2), quart(k)]

    def add(index, k, value):
        text_part[index, quart(k)] = text_part[index, quart(k)] + value.astype(f32)

    def give_b(slot, ya):
        for k in range(2):
            send("odd", stage(ya * 2 + xo, 2 + k), rb_even.at[slot, xh], r_be.at[slot, xh], across[k])

    def free_b(slot, ya):
        for q in range(2):
            send("even", stage(ya * 2 + q, 2 + xo), rb_odd.at[slot, xh, 0], r_bo.at[slot, xh, 0], across[q])

    def pass_b(slot, ya):
        for q in range(2):
            index = ya * 2 + q
            landed(rb_even.at[slot, 1 - q], r_be.at[slot, 1 - q])
            add(index, 2 + xh, rb_even[slot, 1 - q])
            send("even", stage(index, 2 + xh), rb_odd.at[slot, xh, 1], r_bo.at[slot, xh, 1], across[q])

    def take_b(slot, ya):
        index = ya * 2 + xh
        for part in range(2):
            for e in range(2):
                landed(rb_odd.at[slot, e, part], r_bo.at[slot, e, part])
                add(index, 2 + (e if part else 1 - e), rb_odd[slot, e, part])

    def image_block(p, with_sibling=True):
        lanes = pl.ds(pl.multiple_of(p * 2 * TOK, 2 * TOK), 2 * TOK)
        part = lax.dot_general(
            weights[:, :, lanes].reshape(WIDE, 2 * TOK), texts[...].reshape(WIDE, D),
            (((0,), (0,)), ((), ())), preferred_element_type=f32,
        )
        both = pl.ds(2 * p, 2)
        image_part[both] = part.reshape(2, 2, HALF, D)
        if with_sibling:
            image_send[both, 1 - c] = image_part[both, 1 - c].astype(bf16)
            send("all", image_send.at[both, 1 - c], image_sib.at[both], r_is.at[p], sibling)

    def swap_near_far():
        image_send[near_far, 1 - c] = image_part[near_far, 1 - c].astype(bf16)
        send("all", image_send.at[near_far, 1 - c], image_sib.at[near_far], r_is.at[p_far], sibling)

    def add_near_far():
        landed(image_sib.at[near_far], r_is.at[p_far])
        image_part[near_far, c] = image_part[near_far, c] + image_sib[near_far].astype(f32)

    def add_sibling(p):
        both = pl.ds(2 * p, 2)
        landed(image_sib.at[both], r_is.at[p])
        image_part[both, c] = image_part[both, c] + image_sib[both].astype(f32)

    def source_of(slot, h):
        return image_send.at[slot, c, quart(h)]

    def ring_send(m, h, right):
        hops = 4 - m
        slot = (z + hops) % 8 if right else (z + 8 - hops) % 8
        into = image_right if right else image_left
        sem = r_ir if right else r_il
        value = image_part[slot, c, quart(h)]
        if m == 1 and h == (0 if right else 1):
            for core in range(2):
                landed(image_first.at[h, core], r_i0.at[h, core])
                value = value + image_first[h, core].astype(f32)
        if m > 1:
            landed(into.at[m - 1, quart(h)], sem.at[m - 1, h])
            value = value + into[m - 1, quart(h)].astype(f32)
        image_send[slot, c, quart(h)] = value.astype(bf16)
        if m < 3:
            send("all", source_of(slot, h), into.at[m, quart(h)], sem.at[m, h], zp if right else zm)
            return
        way = 0 if right else 1

        @when("even")
        def _():
            send("even", source_of(slot, h), into.at[m, quart(h)], sem.at[m, h], zp if right else zm)

        @when("odd")
        def _():
            send(
                "odd", source_of(slot, h), fin_recv.at[way, quart(h)], r_fin.at[way, h],
                partner_zp if right else partner_zm,
            )

    if STEPS > 5:
        def spread(slot, ya):
            @when("odd")
            def _():
                give_b(slot, ya)

            @when("even")
            def _():
                free_b(slot, ya)

        def pass_on(slot, ya):
            @when("even")
            def _():
                pass_b(slot, ya)

        def hop_a(way, ya, target):
            landed(ra_one.at[way], r_a1.at[way])
            for q in range(2):
                add(ya * 2 + q, way, ra_one[way, q])
            send("all", stage_two(ya, way), ra_two.at[way, 1], r_a2.at[way, 1], target)

        def r1():
            send("all", stage_two(y_far, 0), ra_one.at[0], r_a1.at[0], up)
            send("all", stage_two(y_far, 1), ra_one.at[1], r_a1.at[1], dn)

        def m0():
            far = (z + 4) % 8
            for way, right, left in ((0, zp, zp_sibling), (1, zm, zm_sibling)):
                for core, target in ((c, right), (1 - c, left)):
                    image_send[far, core, quart(way)] = image_part[far, core, quart(way)].astype(bf16)
                    send(
                        "all", image_send.at[far, core, quart(way)], image_first.at[way, c], r_i0.at[way, c], target
                    )

        def m1_free():
            add_near_far()
            add_sibling(p_up)
            add_sibling(p_dn)
            ring_send(1, 1, True)
            ring_send(1, 0, False)

        def m1():
            ring_send(1, 0, True)
            ring_send(1, 1, False)

        def far_b():
            @when("odd")
            def _():
                take_b(0, y_far)
                send("odd", stage(y_far * 2 + xh, 2), rb_one.at[0], r_b1.at[0], up)
                send("odd", stage(y_far * 2 + xh, 3), rb_one.at[1], r_b1.at[1], dn)

        def free_a(way, ya, target):
            send("all", stage_two(ya, 1 - way), ra_two.at[way, 0], r_a2.at[way, 0], target)

        def m2():
            for h in (1, 0):
                ring_send(2, h, True)
                ring_send(2, 1 - h, False)

        T = lambda ya, slot: (text_block(ya), spread(slot, ya))
        I = image_block
        def rest():
            for p in (p_up, p_dn, p_own):
                weigh(p)

        lane = lax.broadcasted_iota(jnp.int32, (8, TOK), 1)

        def scalars():
            log_img = total(jnp.log(z_img))
            log_txt = total(jnp.log(z_txt))
            t_img = total(e_sums[...] / z_img)
            t_acc = e_row[0] * columns[0]
            for k in range(1, 8):
                t_acc = t_acc + e_row[k] * columns[k]
            t_txt = 2.0 * total(t_acc)
            hit = hits[...]
            found = hit > 0.0
            matched = total(jnp.where(found, jnp.log(jnp.where(found, hit, 1.0)) + scale, 0.0))
            scal_send[0] = jnp.where(
                lane == 0, log_txt,
                jnp.where(lane == 1, t_img, jnp.where(lane == 2, t_txt, jnp.where(lane == 3, matched, 0.0))),
            )
            for peer in line_peers:
                send("all", scal_send.at[0], scal_z.at[line_rank], r_sz.at[0], peer)
            scal_z[line_rank] = scal_send[0]
            return log_img

        def second_step(log_img):
            landed(scal_z.at[0:15], r_sz.at[0])
            line_sum = jnp.sum(scal_z[...], axis=0)
            scal_send[1] = jnp.where(lane == 4, log_img, line_sum)
            for peer in plane_peers:
                send("all", scal_send.at[1], scal_p.at[plane_rank], r_sp.at[0], peer)
            scal_p[plane_rank] = scal_send[1]
            return line_sum

        S1, S2 = scalars, second_step
        I(p_far, False)
        m0()
        swap_near_far()
        rest()
        T(y_far, 0)
        r1()
        I(p_up)
        I(p_dn)
        T(y_dn, 1)
        m1_free()
        T(y_up, 2)
        log_img = S1()
        pass_on(0, y_far)
        m1()
        hop_a(0, y_up, up)
        hop_a(1, y_dn, dn)
        free_a(1, y_dn, dn)
        free_a(0, y_up, up)
        T(y, 3)
        pass_on(1, y_dn)
        pass_on(2, y_up)
        I(p_own)
        far_b()
        pass_on(3, y)
        line_sum = S2(log_img)
        m2()

        add_sibling(p_own)

        @when("odd")
        def _():
            fin_send[...] = image_part[z, c].astype(bf16)
            send("odd", fin_send, fin_recv.at[2], r_fin.at[2, 0], partner)

        for part in range(2):
            for way in range(2):
                landed(ra_two.at[way, part], r_a2.at[way, part])
                for q in range(2):
                    add(y * 2 + q, way if part else 1 - way, ra_two[way, part, q])

        @when("odd")
        def _():
            for k in range(2):
                send("odd", stage(y * 2 + xo, k), ra_x.at[xh], r_ax.at[xh], across[k])

        @when("even")
        def _():
            for q in range(2):
                send("even", stage(y * 2 + q, xo), ra_fin.at[xh, 0], r_af.at[xh, 0], across[q])

        def m3():
            for h in (1, 0):
                ring_send(3, h, True)
                ring_send(3, 1 - h, False)

        m3()

        @when("odd")
        def _():
            take_b(1, y_dn)
            take_b(2, y_up)
            send("odd", stage(y_up * 2 + xh, 3), rb_two.at[0, 0], r_b2.at[0, 0], up)
            send("odd", stage(y_dn * 2 + xh, 2), rb_two.at[1, 0], r_b2.at[1, 0], dn)
            for way, ya, target in ((0, y_up, up), (1, y_dn, dn)):
                landed(rb_one.at[way], r_b1.at[way])
                add(ya * 2 + xh, 2 + way, rb_one[way])
                send("odd", stage(ya * 2 + xh, 2 + way), rb_two.at[way, 1], r_b2.at[way, 1], target)

        @when("even")
        def _():
            for q in range(2):
                landed(ra_x.at[1 - q], r_ax.at[1 - q])
                add(y * 2 + q, xh, ra_x[1 - q])
                send("even", stage(y * 2 + q, xh), ra_fin.at[xh, 1], r_af.at[xh, 1], across[q])

        landed(scal_p.at[0:15], r_sp.at[0])
        all_sum = jnp.sum(scal_p[...], axis=0)

        def pick(x, k):
            return jnp.sum(jnp.where(lane[0:1] == k, x[0:1], 0.0))

        log_all = jnp.where(odd, pick(line_sum, 0), pick(all_sum, 4))
        t_all = jnp.where(odd, pick(all_sum, 2), pick(all_sum, 1))
        p_all = pick(all_sum, 3)
        loss_ref[0] = (scale * TOKENS + log_all - p_all) * (1.0 / (2 * TOKENS))
        sgrad_ref[0] = (t_all - p_all) / scale * (1.0 / (2 * TOKENS))

        def finish(part, grads):
            unit32, lengths = unit_ref[part], length_ref[part]
            grads = scale * grads
            inner = jnp.sum(unit32 * grads, axis=1, keepdims=True)
            result = (grads - unit32 * inner) / lengths
            out_ref[0, part] = result.astype(bf16)

        @when("odd")
        def _():
            take_b(3, y)

        @when("odd")
        def _():
            for part in range(2):
                for way in range(2):
                    landed(rb_two.at[way, part], r_b2.at[way, part])
                    add(me, 2 + (way if part else 1 - way), rb_two[way, part])
            finish(upper, text_part[me, upper])
            for part in range(2):
                for e in range(2):
                    landed(ra_fin.at[e, part], r_af.at[e, part])
                    add(me, e if part else 1 - e, ra_fin[e, part])
            finish(lower, text_part[me, lower])

        @when("even")
        def _():
            for h in range(2):
                landed(image_right.at[3, quart(h)], r_ir.at[3, h])
                landed(image_left.at[3, quart(h)], r_il.at[3, h])
            finish(lower, image_part[z, c] + image_right[3].astype(f32) + image_left[3].astype(f32))
            landed(fin_recv.at[2], r_fin.at[2, 0])
            for h in range(2):
                landed(fin_recv.at[0, quart(h)], r_fin.at[0, h])
                landed(fin_recv.at[1, quart(h)], r_fin.at[1, h])
            finish(
                upper,
                fin_recv[0].astype(f32) + fin_recv[1].astype(f32) + fin_recv[2].astype(f32),
            )


    assert count[0] <= SENDS, count[0]
    for name in pending:
        if pending[name]:
            @when(name)
            def _():
                drain(name)


def body(embeddings, pair, logit_scale):
    vmem = pl.BlockSpec(memory_space=pltpu.VMEM)
    smem = pl.BlockSpec(memory_space=pltpu.SMEM)
    dma = pltpu.SemaphoreType.DMA
    scratch = [
        ((TOK, D), bf16),
        ((TOK, D), f32),
        ((TOK, 1), f32),
        ((HALF, D), bf16),
        ((8, 2, HALF, D), bf16),
        ((8, TOK, D), bf16),
        ((16, TOK), f32),
        ((8, TOK, WIDE), f32),
        ((8, TOK, WIDE), bf16),
        ((8, TOK, D), f32),
        ((8, TOK, D), bf16),
        ((2, 2, QUART, D), bf16),
        ((2, 2, 2, QUART, D), bf16),
        ((2, QUART, D), bf16),
        ((2, 2, QUART, D), bf16),
        ((4, 2, 2, QUART, D), bf16),
        ((4, 2, QUART, D), bf16),
        ((2, QUART, D), bf16),
        ((2, 2, QUART, D), bf16),
        ((8, 2, HALF, D), f32),
        ((8, 2, HALF, D), bf16),
        ((8, HALF, D), bf16),
        ((4, HALF, D), bf16),
        ((4, HALF, D), bf16),
        ((2, 2, QUART, D), bf16),
        ((8, TOK, TOK), f32),
        ((8, TOK, TOK), f32),
        ((8, TOK, TOK), f32),
        ((8, TOK), jnp.int32),
        ((8, TOK), f32),
        ((4, 8, TOK), f32),
        ((16, 16, TOK), f32),
        ((16, 8, TOK), f32),
        ((8, TOK), f32),
        ((2, 8, TOK), f32),
        ((16, 8, TOK), f32),
        ((16, 8, TOK), f32),
        ((HALF, D), bf16),
        ((3, HALF, D), bf16),
    ]
    sems = [
        (1,), (SENDS,), (8, 4), (8, WAVES), (8,), (WAVES,), (1,), (1,), (1,), (1,),
        (2,), (2, 2), (2,), (2, 2), (4, 2, 2), (4, 2), (2,), (2, 2), (4,), (4, 2), (4, 2), (3, 2), (WAVES,), (2, 2),
    ]
    grads, loss, scale_grad = pl.pallas_call(
        kernel,
        out_shape=(
            jax.ShapeDtypeStruct((1, TOK, D), bf16),
            jax.ShapeDtypeStruct((1,), f32),
            jax.ShapeDtypeStruct((1,), f32),
        ),
        in_specs=[smem, pl.BlockSpec(memory_space=pl.ANY), vmem],
        out_specs=(vmem, smem, smem),
        scratch_shapes=[pltpu.VMEM(shape, dtype) for shape, dtype in scratch] + [dma(shape) for shape in sems],
        compiler_params=pltpu.CompilerParams(
            collective_id=0, has_side_effects=True, vmem_limit_bytes=56 * 2 ** 20
        ),
        cost_estimate=pl.CostEstimate(flops=6 * WIDE * WIDE * D, bytes_accessed=2 ** 20, transcendentals=2 ** 20),
        name="contrastive",
    )(
        logit_scale.astype(f32).reshape(1),
        embeddings,
        pair.reshape(1, TOK),
    )
    return grads, loss, scale_grad


def solution(mesh):
    placed = (P("tower", "blk", None), P("blk"), P())
    return jax.shard_map(
        body,
        mesh=mesh,
        in_specs=placed,
        out_specs=(P("tower", "blk", None), P("tower"), P("tower")),
        check_vma=False,
    )
```
